256 devices in a mesh: sec: 2 (over y_lo), lat: 4 (over y_hi, core), lon: 32 (over x, z).
Axes of the slice: x: 4, y: 4 (y_hi: 2, y_lo: 2; y = y_hi * 2 + y_lo), z: 8, core: 2. Of those that a mesh axis runs over, the one named last changes fastest.
Arguments:
- tokens: bfloat16 [2, 48, 384, 512], P('sec', 'lat', 'lon'), may hold values from -6 to 6
- cotangent: bfloat16 [2, 24, 192, 512], P('sec', 'lat', 'lon'), may hold values from -6 to 6
- fine_gain: float32 [512], replicated, may hold values from 0.25 to 1.75
- fine_attend: bfloat16 [512, 1536], replicated, may hold values from -4 to 4
- fine_output: bfloat16 [512, 512], replicated, may hold values from -0.25 to 0.25
- merge_weight: bfloat16 [2048, 512], replicated, may hold values from -0.125 to 0.125
- coarse_gain: float32 [512], replicated, may hold values from 0.25 to 1.75
- coarse_attend: bfloat16 [512, 1536], replicated, may hold values from -4 to 4
- coarse_output: bfloat16 [512, 512], replicated, may hold values from -0.25 to 0.25
Outputs:
- coarse_field: bfloat16 [2, 24, 192, 512], P('sec', 'lat', 'lon')
- token_gradient: bfloat16 [2, 48, 384, 512], P('sec', 'lat', 'lon')
- fine_gain_gradient: float32 [512], P('lon')
- fine_attend_gradient: float32 [512, 1536], P('lon')
- fine_output_gradient: float32 [512, 512], P('lon')
- merge_gradient: float32 [2048, 512], P('lon')
- coarse_gain_gradient: float32 [512], P('lon')
- coarse_attend_gradient: float32 [512, 1536], P('lon')
- coarse_output_gradient: float32 [512, 512], P('lon')
The draws below stay inside these ranges and needn't reach their ends.
All inputs are finite; a program needn't handle non-finite values.
Results may differ from the reference program's by a relative error of at most 0.04.
Values may be sent and summed in bfloat16 or wider, within the bound.
A program may use at most 128 MiB of HBM per device.

```python
import math
import jax
import jax.numpy as jnp
from jax import lax

D = 512
HEADS = 8
RADIUS = 6
MEMBERS = 2
NLAT = 48
NLON = 384
CLAT = 24
CLON = 192


def aligned(key, strength):
    first, second, third = jax.random.split(key, 3)
    base = jnp.clip(jax.random.normal(first, (D, 3 * D), jnp.float32), -3.5, 3.5) / jnp.sqrt(jnp.float32(D))
    picked = jax.random.bernoulli(second, 0.3, (HEADS,))
    forced = jax.random.randint(third, (), 0, HEADS)
    picked = picked | (jnp.arange(HEADS) == forced)
    columns = jnp.repeat(picked, D // HEADS)[None, :]
    query = base[:, :D]
    lifted = query * jnp.where(columns, strength, 1.0)
    keys = jnp.where(columns, base[:, D:2 * D], base[:, D:2 * D])
    return jnp.concatenate([lifted, keys, base[:, 2 * D:]], axis=1)


def draw_fine_attend(key, part):
    key = jax.random.fold_in(key, 11)
    return aligned(key, 1.0).astype(jnp.bfloat16)


def draw_coarse_attend(key, part):
    key = jax.random.fold_in(key, 23)
    return aligned(key, 1.0).astype(jnp.bfloat16)


def block_scale(stream_key, dims, cuts, least, high):
    level = 1.0
    for position, shards_of in cuts:
        steps = jax.random.uniform(jax.random.fold_in(jax.random.fold_in(stream_key, 6), position), (shards_of,), jnp.float32, least / len(cuts), high / len(cuts))
        level = level * jnp.repeat(jnp.exp(steps), dims[position] // shards_of).reshape((-1,) + (1,) * (len(dims) - 1 - position))
    return level


def scatter_about(rng, dims, scale, bound, shards=(), kind=jnp.bfloat16):
    drawn = jax.random.normal(rng, dims, jnp.float32) * scale
    if len(shards) > 0:
        drawn = block_scale(rng, dims, shards, -0.22, 0.18) * drawn
    return jnp.clip(drawn, min=-bound, max=bound).astype(kind)


def setup_inputs(seed: int = 0) -> dict:
    streams_of = jax.random.split(jax.random.key(seed), 10)
    return {
        "tokens": scatter_about(streams_of[0], (MEMBERS, NLAT, NLON, D), 1.0, 6.0, ((0, 2), (1, 4), (2, 32))),
        "cotangent": scatter_about(streams_of[1], (MEMBERS, CLAT, CLON, D), 1.0, 6.0, ((0, 2), (1, 4), (2, 32))),
        "fine_gain": jnp.clip(1.0 + 0.15 * jax.random.normal(streams_of[2], (D,), jnp.float32), 0.25, 1.75),
        "fine_attend": draw_fine_attend(jax.random.fold_in(streams_of[9], 71), 0),
        "fine_output": scatter_about(streams_of[4], (D, D), D ** -0.5, 0.25),
        "merge_weight": scatter_about(streams_of[5], (4 * D, D), (4 * D) ** -0.5, 0.125),
        "coarse_gain": jnp.clip(1.0 + 0.15 * jax.random.normal(streams_of[6], (D,), jnp.float32), 0.25, 1.75),
        "coarse_attend": draw_coarse_attend(jax.random.fold_in(streams_of[9], 71), 0),
        "coarse_output": scatter_about(streams_of[8], (D, D), D ** -0.5, 0.25),
    }


EPSILON = 1e-06
NEGATIVE = -1e+30
PRECISE = lax.Precision.HIGHEST

def product(form, left, right):
    return jnp.einsum(form, left.astype(jnp.float32), right.astype(jnp.float32))

def to_blocks(field):
    rows, columns, depth = field.shape
    shaped = field.reshape(rows // RADIUS, RADIUS, columns // RADIUS, RADIUS, depth)
    return shaped.transpose(0, 2, 1, 3, 4).reshape(-1, RADIUS * RADIUS, depth)

def from_blocks(blocks, rows, columns):
    depth = blocks.shape[-1]
    shaped = blocks.reshape(rows // RADIUS, columns // RADIUS, RADIUS, RADIUS, depth)
    return shaped.transpose(0, 2, 1, 3, 4).reshape(rows, columns, depth)

def regions(padded):
    rows = padded.shape[0] // RADIUS
    columns = padded.shape[1] // RADIUS
    depth = padded.shape[2]
    shaped = padded.reshape(rows, RADIUS, columns, RADIUS, depth)
    pieces = [shaped[first:first + rows - 2, :, second:second + columns - 2] for first in range(3) for second in range(3)]
    stacked = jnp.stack(pieces, 0).reshape(3, 3, rows - 2, RADIUS, columns - 2, RADIUS, depth)
    return stacked.transpose(2, 4, 0, 3, 1, 5, 6).reshape((rows - 2) * (columns - 2), 9 * RADIUS * RADIUS, depth)

def unregions(grads, rows, columns):
    block_rows = rows // RADIUS - 2
    block_cols = columns // RADIUS - 2
    depth = grads.shape[-1]
    shaped = grads.reshape(block_rows, block_cols, 3, RADIUS, 3, RADIUS, depth).transpose(2, 4, 0, 3, 1, 5, 6)
    summed = jnp.zeros((block_rows + 2, RADIUS, block_cols + 2, RADIUS, depth), grads.dtype)
    for first in range(3):
        for second in range(3):
            summed = summed.at[first:first + block_rows, :, second:second + block_cols].add(shaped[first, second])
    return summed.reshape(rows, columns, depth)

def window_mask(valid, block_cols):
    block_rows = valid.shape[0] // RADIUS - 2
    cells = jnp.arange(RADIUS * RADIUS, dtype=jnp.int32)
    places = jnp.arange(9 * RADIUS * RADIUS, dtype=jnp.int32)
    query_row = cells // RADIUS
    query_col = cells % RADIUS
    key_row = places // (3 * RADIUS)
    key_col = places % (3 * RADIUS)
    near_rows = (key_row[None, :] >= query_row[:, None]) & (key_row[None, :] <= query_row[:, None] + 2 * RADIUS)
    near_cols = (key_col[None, :] >= query_col[:, None]) & (key_col[None, :] <= query_col[:, None] + 2 * RADIUS)
    shaped = valid.reshape(block_rows + 2, RADIUS)
    bands = jnp.stack([shaped[first:first + block_rows] for first in range(3)], 1).reshape(block_rows, 3 * RADIUS)
    open_keys = jnp.broadcast_to(bands[:, :, None], (block_rows, 3 * RADIUS, 3 * RADIUS)).reshape(block_rows, 9 * RADIUS * RADIUS)
    open_keys = jnp.repeat(open_keys, block_cols, axis=0)
    return (near_rows & near_cols)[None, None] & open_keys[:, None, None, :]

def attend(query, keys, values, valid):
    rows, columns, width = query.shape
    head_dim = width // HEADS
    factor = 1.0 / math.sqrt(head_dim)
    count = rows // RADIUS * (columns // RADIUS)
    query_blocks = to_blocks(query).reshape(count, RADIUS * RADIUS, HEADS, head_dim)
    key_blocks = regions(keys).reshape(count, 9 * RADIUS * RADIUS, HEADS, head_dim)
    value_blocks = regions(values).reshape(count, 9 * RADIUS * RADIUS, HEADS, head_dim)
    scores = product('bqnc,bknc->bnqk', query_blocks, key_blocks) * factor
    scores = jnp.where(window_mask(valid, columns // RADIUS), scores, NEGATIVE)
    peak = lax.optimization_barrier(jnp.max(scores, axis=-1, keepdims=True))
    expo = jnp.exp(scores - peak)
    attention = expo / lax.optimization_barrier(jnp.sum(expo, axis=-1, keepdims=True))
    mixed = product('bnqk,bknc->bqnc', attention.astype(jnp.bfloat16), value_blocks)
    return (from_blocks(mixed.reshape(count, RADIUS * RADIUS, width), rows, columns), attention)

def attend_back(query, keys, values, valid, slope):
    rows, columns, width = query.shape
    head_dim = width // HEADS
    factor = 1.0 / math.sqrt(head_dim)
    count = rows // RADIUS * (columns // RADIUS)
    unused, attention = attend(query, keys, values, valid)
    query_blocks = to_blocks(query).reshape(count, RADIUS * RADIUS, HEADS, head_dim)
    key_blocks = regions(keys).reshape(count, 9 * RADIUS * RADIUS, HEADS, head_dim)
    value_blocks = regions(values).reshape(count, 9 * RADIUS * RADIUS, HEADS, head_dim)
    slope_blocks = to_blocks(slope).reshape(count, RADIUS * RADIUS, HEADS, head_dim)
    prob_slope = product('bqnc,bknc->bnqk', slope_blocks, value_blocks)
    score_slope = (attention * (prob_slope - lax.optimization_barrier(jnp.sum(attention * prob_slope, axis=-1, keepdims=True))) * factor).astype(jnp.bfloat16)
    query_slope = product('bnqk,bknc->bqnc', score_slope, key_blocks)
    key_slope = product('bnqk,bqnc->bknc', score_slope, query_blocks)
    value_slope = product('bnqk,bqnc->bknc', attention.astype(jnp.bfloat16), slope_blocks)
    pair = jnp.concatenate([key_slope.reshape(count, -1, width), value_slope.reshape(count, -1, width)], axis=-1)
    wide = unregions(pair, rows + 2 * RADIUS, columns + 2 * RADIUS)
    return (from_blocks(query_slope.reshape(count, RADIUS * RADIUS, width), rows, columns), wide)

def pad_field(field):
    wrapped = jnp.concatenate([field[:, -RADIUS:], field, field[:, :RADIUS]], axis=1)
    zeros = jnp.zeros((RADIUS,) + wrapped.shape[1:], field.dtype)
    return jnp.concatenate([zeros, wrapped, zeros], axis=0)

def unpad_field(grad):
    inner = grad[RADIUS:-RADIUS]
    core = inner[:, RADIUS:-RADIUS]
    core = core.at[:, :RADIUS].add(inner[:, -RADIUS:])
    return core.at[:, -RADIUS:].add(inner[:, :RADIUS])

def pole_rows(rows):
    places = jnp.arange(rows + 2 * RADIUS, dtype=jnp.int32) - RADIUS
    return (places >= 0) & (places < rows)

def normalize(field, gain):
    upcast = field.astype(jnp.float32)
    factor = lax.rsqrt(lax.optimization_barrier(jnp.mean(upcast * upcast, axis=-1, keepdims=True)) + EPSILON)
    normed = upcast * factor
    return (upcast, factor, normed, (normed * gain).astype(jnp.bfloat16))

def layer_forward(field, gain, attend_weight, output_weight):
    rows, columns, width = field.shape
    upcast, factor, normed, hidden = normalize(field, gain)
    projected = jnp.dot(hidden.reshape(-1, width), attend_weight, preferred_element_type=jnp.float32)
    projected = projected.astype(jnp.bfloat16).reshape(rows, columns, 3 * width)
    query = projected[..., :width]
    wide = pad_field(projected[..., width:])
    valid = pole_rows(rows)

    def band(index):
        start = index * RADIUS
        part_wide = lax.dynamic_slice_in_dim(wide, start, 3 * RADIUS, 0)
        part_query = lax.dynamic_slice_in_dim(query, start, RADIUS, 0)
        part_valid = lax.dynamic_slice_in_dim(valid, start, 3 * RADIUS, 0)
        result, unused = attend(part_query, part_wide[..., :width], part_wide[..., width:], part_valid)
        return result.astype(jnp.bfloat16)
    attended = lax.map(band, jnp.arange(rows // RADIUS, dtype=jnp.int32)).reshape(rows, columns, width)
    moved = jnp.dot(attended.reshape(-1, width), output_weight, preferred_element_type=jnp.float32)
    output = (upcast + moved.reshape(rows, columns, width)).astype(jnp.bfloat16)
    return (output, (factor, normed, hidden, query, wide, valid, attended))

def layer_backward(slope, gain, attend_weight, output_weight, saved):
    factor, normed, hidden, query, wide, valid, attended = saved
    rows, columns, width = slope.shape
    flat_slope = slope.reshape(-1, width)
    output_slope = jnp.dot(attended.reshape(-1, width).T, flat_slope, preferred_element_type=jnp.float32)
    mixed_slope = jnp.dot(flat_slope, output_weight.T, preferred_element_type=jnp.float32)
    mixed_slope = mixed_slope.astype(jnp.bfloat16).reshape(rows, columns, width)

    def band_back(summed, index):
        start = index * RADIUS
        part_wide = lax.dynamic_slice_in_dim(wide, start, 3 * RADIUS, 0)
        part_query = lax.dynamic_slice_in_dim(query, start, RADIUS, 0)
        part_valid = lax.dynamic_slice_in_dim(valid, start, 3 * RADIUS, 0)
        part_slope = lax.dynamic_slice_in_dim(mixed_slope, start, RADIUS, 0)
        query_slope, wide_slope = attend_back(part_query, part_wide[..., :width], part_wide[..., width:], part_valid, part_slope)
        current = lax.dynamic_slice_in_dim(summed, start, 3 * RADIUS, 0)
        summed = lax.dynamic_update_slice_in_dim(summed, current + wide_slope, start, 0)
        return (summed, query_slope)
    start_sum = jnp.zeros((rows + 2 * RADIUS, columns + 2 * RADIUS, 2 * width), jnp.float32)
    summed, query_slopes = lax.scan(band_back, start_sum, jnp.arange(rows // RADIUS, dtype=jnp.int32))
    pair_slope = unpad_field(summed)
    joined = jnp.concatenate([query_slopes.reshape(-1, width), pair_slope.reshape(-1, 2 * width)], axis=1)
    attend_slope = jnp.dot(hidden.reshape(-1, width).astype(jnp.float32).T, joined, precision=PRECISE)
    hidden_slope = jnp.dot(joined, attend_weight.astype(jnp.float32).T, precision=PRECISE).reshape(rows, columns, width)
    gain_slope = lax.optimization_barrier(jnp.sum(hidden_slope * normed, axis=(0, 1)))
    scaled = hidden_slope * gain
    input_slope = slope.astype(jnp.float32) + factor * (scaled - normed * lax.optimization_barrier(jnp.mean(scaled * normed, axis=-1, keepdims=True)))
    return (input_slope, gain_slope, attend_slope, output_slope)

def merge_cells(field):
    rows, columns, width = field.shape
    return field.reshape(rows // 2, 2, columns // 2, 2, width).transpose(0, 2, 1, 3, 4).reshape(rows // 2, columns // 2, 4 * width)

def split_cells(field):
    rows, columns, depth = field.shape
    width = depth // 4
    return field.reshape(rows, columns, 2, 2, width).transpose(0, 2, 1, 3, 4).reshape(2 * rows, 2 * columns, width)

def reference(tokens, cotangent, fine_gain, fine_attend, fine_output, merge_weight, coarse_gain, coarse_attend, coarse_output):
    members = tokens.shape[0]
    width = tokens.shape[-1]
    fields = []
    slopes = []
    totals = None
    for member in range(members):
        fine_field, fine_saved = layer_forward(tokens[member], fine_gain, fine_attend, fine_output)
        merged = merge_cells(fine_field)
        half_rows, half_cols = (merged.shape[0], merged.shape[1])
        coarse_in = jnp.dot(merged.reshape(-1, 4 * width), merge_weight, preferred_element_type=jnp.float32)
        coarse_in = coarse_in.astype(jnp.bfloat16).reshape(half_rows, half_cols, width)
        coarse_field, coarse_saved = layer_forward(coarse_in, coarse_gain, coarse_attend, coarse_output)
        coarse_slope, coarse_gain_slope, coarse_attend_slope, coarse_output_slope = layer_backward(cotangent[member], coarse_gain, coarse_attend, coarse_output, coarse_saved)
        coarse_flat = coarse_slope.astype(jnp.bfloat16).reshape(-1, width)
        merge_slope = jnp.dot(merged.reshape(-1, 4 * width).T, coarse_flat, preferred_element_type=jnp.float32)
        merged_slope = jnp.dot(coarse_flat, merge_weight.T, preferred_element_type=jnp.float32).astype(jnp.bfloat16)
        fine_slope = split_cells(merged_slope.reshape(half_rows, half_cols, 4 * width))
        token_slope, fine_gain_slope, fine_attend_slope, fine_output_slope = layer_backward(fine_slope, fine_gain, fine_attend, fine_output, fine_saved)
        fields.append(coarse_field)
        slopes.append(token_slope.astype(jnp.bfloat16))
        grads = (fine_gain_slope, fine_attend_slope, fine_output_slope, merge_slope, coarse_gain_slope, coarse_attend_slope, coarse_output_slope)
        totals = grads if totals is None else jax.tree.map(lambda left, right: left + right, totals, grads)
    return (jnp.stack(fields, 0), jnp.stack(slopes, 0), totals[0], totals[1], totals[2], totals[3], totals[4], totals[5], totals[6])
```

```python
import functools

import jax
import jax.numpy as jnp
import numpy as np
from jax import lax
from jax.experimental import pallas as pl
from jax.experimental.pallas import tpu as pltpu
from jax.sharding import PartitionSpec as P

HEADS = 8
RADIUS = 6
EPSILON = 1e-06
NEGATIVE = -1e30
UNIT = 48
D = 512
PAIRS = 4
MESH = pl.DeviceIdType.MESH
F32 = jnp.float32
BF16 = jnp.bfloat16
AROUND = ((0, 1), (0, -1), (1, 0), (-1, 0), (1, 1), (1, -1), (-1, 1), (-1, -1))


def dot(left, right):
    return jnp.dot(left, right, preferred_element_type=F32)


def dot_t(left, right):
    return lax.dot_general(left, right, (((1,), (1,)), ((), ())), preferred_element_type=F32)


def t_dot(left, right):
    return lax.dot_general(left, right, (((0,), (0,)), ((), ())), preferred_element_type=F32)


def window_bias():
    query = np.arange(UNIT)
    row, col = query // 8, query % 8
    key = np.arange(9 * UNIT)
    unit, cell = key // UNIT, key % UNIT
    key_row = unit // 3 * RADIUS + cell // 8
    key_col = unit % 3 * RADIUS + cell % 8
    near = (
        (key_row[None] >= row[:, None])
        & (key_row[None] <= row[:, None] + 2 * RADIUS)
        & (key_col[None] >= col[:, None])
        & (key_col[None] <= col[:, None] + 2 * RADIUS)
        & (cell % 8 < RADIUS)[None]
    )
    bias = np.where(near, 0.0, NEGATIVE).astype(np.float32)
    return np.concatenate([bias, bias], 0)


def merge_matrix():
    matrix = np.zeros((4 * UNIT, 4 * UNIT), np.float32)
    for a in range(2):
        for b in range(2):
            for i in range(RADIUS):
                for j in range(RADIUS):
                    r, c = 2 * i + a, 2 * j + b
                    place = (r // 6 * 2 + c // 6) * UNIT + r % 6 * 8 + c % 6
                    matrix[(a * 2 + b) * UNIT + i * 8 + j, place] = 1.0
    return matrix


class Layout:
    def __init__(self, mesh):
        self.sec, self.lat, self.lon = (mesh.shape[k] for k in ("sec", "lat", "lon"))
        self.x = 4 if self.lon == 32 else 2
        self.z = self.lon // self.x
        self.y_hi = self.lat // 2
        self.y = self.y_hi * self.sec
        self.blocks = self.lon
        self.depth = D // self.blocks
        self.z_low = self.z // 2
        self.fine_width = 2048 // (2 * self.y)
        self.coarse_width = 4096 // (2 * self.y)


def unit_window(width, starts, ref, column):
    return jnp.concatenate([ref[pl.ds(s, width), pl.ds(column, 128)] for s in starts], 0)


def low_lanes(rows):
    return lax.broadcasted_iota(jnp.int32, (rows, 128), 1) < 64


def stack_heads(part):
    part = part.astype(F32)
    low = low_lanes(UNIT)
    return jnp.concatenate([jnp.where(low, part, 0.0), jnp.where(low, 0.0, part)], 0).astype(BF16)


def merge_heads(both):
    return jnp.where(low_lanes(UNIT), both[:UNIT], both[UNIT:])


def attend(query, keys, values, bias):
    scores = dot_t(query, keys) * 0.125 + bias
    expo = jnp.exp(scores - jnp.max(scores, axis=-1, keepdims=True))
    attention = expo / jnp.sum(expo, axis=-1, keepdims=True)
    return attention, merge_heads(dot(attention.astype(BF16), values))


def attend_back(query, keys, values, attention, slope):
    prob = dot_t(slope, values)
    mean = jnp.sum(attention * prob, axis=-1, keepdims=True)
    score = (attention * (prob - mean) * 0.125).astype(BF16)
    query_slope = merge_heads(dot(score, keys))
    key_slope = t_dot(score, query)
    value_slope = t_dot(attention.astype(BF16), slope)
    return query_slope, key_slope, value_slope


def norm(field, gain):
    factor = lax.rsqrt(jnp.mean(field * field, axis=-1, keepdims=True) + EPSILON)
    normed = field * factor
    return factor, normed, (normed * gain).astype(BF16)


def input_back(slope, hidden_slope, field, gain):
    factor = lax.rsqrt(jnp.mean(field * field, axis=-1, keepdims=True) + EPSILON)
    normed = field * factor
    scaled = hidden_slope * gain
    return slope + factor * (scaled - normed * jnp.mean(scaled * normed, axis=-1, keepdims=True))


class Reducer:
    def __init__(self, lay, place, wires, refs):
        self.lay, self.place, self.wires = lay, place, wires
        (
            self.given, self.pair_in, self.pair_sum,
            self.in_1a, self.in_1b, self.sum_2a, self.sum_2b,
            self.in_2a, self.in_2b, self.sum_3, self.in_3, self.full,
        ) = refs
        self.copies = []

    def device(self, core=None, y=None, x=None, z=None):
        here = self.place
        core = here["core"] if core is None else core
        y = here["y"] if y is None else y
        x = here["x"] if x is None else x
        z = here["z"] if z is None else z
        return (y % self.lay.sec, y // self.lay.sec * 2 + core, x * self.lay.z + z)

    def send(self, source, target, device):
        copy = self.wires(source, target, device)
        copy.start()
        self.copies.append(copy)

    def arrive(self):
        for copy in self.copies:
            copy.wait()
        self.copies = []

    def pair_start(self):
        other = 1 - self.place["core"]
        self.send(self.given.at[other], self.pair_in, self.device(core=other))

    def pair_finish(self):
        self.arrive()
        core = self.place["core"]
        span = self.lay.x

        @pl.loop(0, self.lay.y * span)
        def _(step):
            y, x = step // span, step % span
            total = self.given[core, y, x].astype(F32) + self.pair_in[y, x].astype(F32)
            self.pair_sum[y, x] = total.astype(BF16)

    def first_start(self):
        lay, here = self.lay, self.place
        low = pl.ds(0, lay.z_low)
        high = pl.ds(lay.z_low, lay.z - lay.z_low)
        for step in range(1, lay.x):
            x = (here["x"] + step) % lay.x
            self.send(self.pair_sum.at[:, x, low], self.in_1a.at[step - 1], self.device(x=x))
        for step in range(1, lay.y):
            y = (here["y"] + step) % lay.y
            self.send(self.pair_sum.at[y, :, high], self.in_1b.at[step - 1], self.device(y=y))

    def first_finish(self):
        self.arrive()
        lay, here = self.lay, self.place
        low = pl.ds(0, lay.z_low)
        high = pl.ds(lay.z_low, lay.z - lay.z_low)

        @pl.loop(0, lay.y)
        def _(y):
            total = self.pair_sum[y, here["x"], low].astype(F32)
            for k in range(lay.x - 1):
                total += self.in_1a[k, y].astype(F32)
            self.sum_2a[y] = total.astype(BF16)

        @pl.loop(0, lay.x)
        def _(x):
            total = self.pair_sum[here["y"], x, high].astype(F32)
            for k in range(lay.y - 1):
                total += self.in_1b[k, x].astype(F32)
            self.sum_2b[x] = total.astype(BF16)

    def second_start(self):
        lay, here = self.lay, self.place
        for step in range(1, lay.y):
            y = (here["y"] + step) % lay.y
            self.send(self.sum_2a.at[y], self.in_2a.at[step - 1], self.device(y=y))
        for step in range(1, lay.x):
            x = (here["x"] + step) % lay.x
            self.send(self.sum_2b.at[x], self.in_2b.at[step - 1], self.device(x=x))

    def second_finish(self):
        self.arrive()
        lay, here = self.lay, self.place
        total = self.sum_2a[here["y"]].astype(F32)
        for k in range(lay.y - 1):
            total += self.in_2a[k].astype(F32)
        self.sum_3[pl.ds(0, lay.z_low)] = total.astype(BF16)
        total = self.sum_2b[here["x"]].astype(F32)
        for k in range(lay.x - 1):
            total += self.in_2b[k].astype(F32)
        self.sum_3[pl.ds(lay.z_low, lay.z - lay.z_low)] = total.astype(BF16)

    def third_start(self):
        lay, here = self.lay, self.place
        for step in range(1, lay.z):
            z = (here["z"] + step) % lay.z
            self.send(self.sum_3.at[z], self.in_3.at[step - 1], self.device(z=z))

    def third_finish(self):
        self.arrive()
        lay, here = self.lay, self.place
        total = self.sum_3[here["z"]].astype(F32)
        for k in range(lay.z - 1):
            total += self.in_3[k].astype(F32)
        self.full[here["core"], here["y"]] = total.astype(BF16)

    def last_start(self):
        lay, here = self.lay, self.place
        own = self.full.at[here["core"], here["y"]]
        for across in range(2):
            for step in range(lay.y):
                if across or step:
                    core = (here["core"] + across) % 2
                    y = (here["y"] + step) % lay.y
                    self.send(own, own, self.device(core=core, y=y))

    def last_finish(self):
        self.arrive()

    def column(self, start, width):
        size = self.full.shape[-1]
        parts = []
        while width > 0:
            group, offset = divmod(start, size)
            take = min(width, size - offset)
            parts.append(self.full[group // self.lay.y, group % self.lay.y, :, offset : offset + take])
            start, width = start + take, width - take
        return (parts[0] if len(parts) == 1 else jnp.concatenate(parts, 1)).astype(F32)

    def put(self, start, product):
        lay = self.lay
        size = self.given.shape[-1]
        done, width = 0, product.shape[1]
        while done < width:
            group, offset = divmod(start + done, size)
            take = min(width - done, size - offset)
            piece = product[:, done : done + take].astype(BF16)
            self.given[group // lay.y, group % lay.y, :, :, :, offset : offset + take] = piece.reshape(
                lay.x, lay.z, lay.depth, take
            )
            done += take

    def put_merged(self, part, start, product):
        lay = self.lay
        size = self.given.shape[-1]
        count = lay.blocks // 4
        shaped = product.astype(BF16).reshape(count, 4, lay.depth, D)
        for run in range(4):
            group, offset = divmod(start + run * D, size)
            for block in range(count):
                x, z = divmod(part * count + block, lay.z)
                self.given[group // lay.y, group % lay.y, x, z, :, offset : offset + D] = shaped[block, run]


def kernel(
    lay,
    tokens, cotangent, fine_gain, coarse_gain, bias_ref, merge_ref, split_ref,
    fine_attend_hbm, fine_output_hbm, merge_hbm, coarse_attend_hbm, coarse_output_hbm,
    coarse_field, token_gradient,
    fine_gain_out, fine_attend_out, fine_output_out, merge_out,
    coarse_gain_out, coarse_attend_out, coarse_output_out,
    fine_attend, fine_output, merge_weight, coarse_attend, coarse_output,
    strip, field_f, wide_f, pairs_f, query_f, hidden_f, attention_f, mixed_f, merged,
    slope_f, mixed_slope_f, wide_slope_f, rims_f, query_slope_f,
    from_lon, from_lat, from_corner,
    field_c, wide_c, pairs_c, query_c, hidden_c, attention_c, mixed_c,
    slope_c, rims_c, query_slope_c, pair_slope_c, from_around,
    *rest,
):
    coarse_refs, fine_refs = rest[:12], rest[12:24]
    load_sem, send_sem, recv_sem = rest[24:]
    sec, lat, lon = (lax.axis_index(k) for k in ("sec", "lat", "lon"))
    place = {
        "core": lat % 2,
        "y": lat // 2 * lay.sec + sec,
        "x": lon // lay.z,
        "z": lon % lay.z,
    }
    used = [0]

    def wires(source, target, device):
        index = used[0]
        used[0] += 1
        return pltpu.make_async_remote_copy(
            src_ref=source,
            dst_ref=target,
            send_sem=send_sem.at[index],
            recv_sem=recv_sem.at[index],
            device_id=device,
            device_id_type=MESH,
        )

    def neighbour(step):
        return (sec, (lat + step[0] + lay.lat) % lay.lat, (lon + step[1] + lay.lon) % lay.lon)

    coarse_sum = Reducer(lay, place, wires, coarse_refs)
    fine_sum = Reducer(lay, place, wires, fine_refs)

    loads = [
        pltpu.make_async_copy(source, target, load_sem.at[i])
        for i, (source, target) in enumerate(
            (
                (fine_attend_hbm, fine_attend),
                (fine_output_hbm, fine_output),
                (merge_hbm, merge_weight),
                (coarse_attend_hbm, coarse_attend),
                (coarse_output_hbm, coarse_output),
            )
        )
    ]
    for load in loads:
        load.start()

    barrier = pltpu.get_barrier_semaphore()
    peers = [neighbour(step) for step in AROUND]
    peers += [coarse_sum.device(x=(place["x"] + s) % lay.x) for s in range(1, lay.x)]
    peers += [coarse_sum.device(z=(place["z"] + s) % lay.z) for s in range(1, lay.z)]
    peers += [
        coarse_sum.device(core=(place["core"] + c) % 2, y=(place["y"] + s) % lay.y)
        for c in range(2)
        for s in range(lay.y)
        if c or s
    ]
    for peer in peers:
        pl.semaphore_signal(barrier, inc=1, device_id=peer, device_id_type=MESH)

    field_f[...] = jnp.zeros_like(field_f)
    field_c[...] = jnp.zeros_like(field_c)
    for row in range(12):
        strip[row, :12] = tokens[0, row].astype(F32)
    for row in range(12):
        for half in range(2):
            place_of = (row // 6 * 2 + half) * UNIT + row % 6 * 8
            field_f[place_of : place_of + 6] = strip[row, 6 * half : 6 * half + 6]
    for unit in range(4):
        wide_f[1 + unit // 2, 1 + unit % 2] = field_f[unit * UNIT : (unit + 1) * UNIT].astype(BF16)
    for row in range(6):
        field_c[row * 8 : row * 8 + 6] = cotangent[0, row].astype(F32)
    slope_c[...] = field_c[...]

    pl.semaphore_wait(barrier, len(peers))

    def wide_part(step, mine):
        index = []
        for way in step:
            if way == 0:
                index.append(pl.ds(1, 2))
            elif way > 0:
                index.append(2 if mine else 3)
            else:
                index.append(1 if mine else 0)
        return tuple(index)

    def opposite(step):
        return (-step[0], -step[1])

    halo = []
    for step in AROUND:
        copy = wires(
            wide_f.at[wide_part(step, True)],
            wide_f.at[wide_part(opposite(step), False)],
            neighbour(step),
        )
        copy.start()
        halo.append(copy)

    top = jnp.where(lat == 0, NEGATIVE, 0.0)
    bottom = jnp.where(lat == lay.lat - 1, NEGATIVE, 0.0)
    lanes = lax.broadcasted_iota(jnp.int32, (1, 9 * UNIT), 1)

    def bias_at(is_first, is_last):
        above = jnp.where(is_first, top, 0.0)
        below = jnp.where(is_last, bottom, 0.0)
        rim = jnp.where(lanes < 3 * UNIT, above, 0.0) + jnp.where(lanes >= 6 * UNIT, below, 0.0)
        return bias_ref[...] + rim

    gain_f = fine_gain[...]
    gain_c = coarse_gain[...]
    loads[0].wait()
    hidden_f[...] = norm(field_f[...], gain_f)[2]
    query_f[...] = dot(hidden_f[...], fine_attend[:, :D]).astype(BF16)
    for copy in halo:
        copy.wait()

    @pl.loop(0, 4)
    def _(row):
        field = wide_f[row].reshape(4 * UNIT, D).astype(F32)
        hidden = norm(field, gain_f)[2]
        pairs_f[pl.ds(pl.multiple_of(row * 4 * UNIT, 4 * UNIT), 4 * UNIT), :] = dot(
            hidden, fine_attend[:, D:]
        ).astype(BF16)

    def starts_of(quad):
        first, second = quad // 2, quad % 2
        return [pl.multiple_of(((first + i) * 4 + second) * UNIT, UNIT) for i in range(3)]

    @pl.loop(0, 4)
    def _(quad):
        first = quad // 2
        own = pl.ds(pl.multiple_of(quad * UNIT, UNIT), UNIT)
        bias = bias_at(first == 0, first == 1)
        starts = starts_of(quad)
        for pair in range(PAIRS):
            query = stack_heads(query_f[own, pair * 128 : pair * 128 + 128])
            keys = unit_window(3 * UNIT, starts, pairs_f, pair * 128)
            values = unit_window(3 * UNIT, starts, pairs_f, D + pair * 128)
            attention, mixed = attend(query, keys, values, bias)
            attention_f[quad, pair] = attention
            mixed_f[own, pair * 128 : pair * 128 + 128] = mixed.astype(BF16)

    loads[1].wait()
    fine_field = (field_f[...] + dot(mixed_f[...], fine_output[...])).astype(BF16)
    merged[...] = dot(merge_ref[...], fine_field).astype(BF16)
    loads[2].wait()
    coarse_in = jnp.zeros((UNIT, D), F32)
    for part in range(4):
        coarse_in += dot(merged[part * UNIT : (part + 1) * UNIT], merge_weight[part * D : (part + 1) * D])
    wide_c[1, 1] = coarse_in.astype(BF16)

    halo = []
    for step in AROUND:
        copy = wires(wide_c.at[1, 1], wide_c.at[1 - step[0], 1 - step[1]], neighbour(step))
        copy.start()
        halo.append(copy)

    loads[3].wait()
    loads[4].wait()
    field_c[...] = wide_c[1, 1].astype(F32)
    hidden_c[...] = norm(field_c[...], gain_c)[2]
    query_c[...] = dot(hidden_c[...], coarse_attend[:, :D]).astype(BF16)
    mixed_slope_c = dot_t(slope_c[...].astype(BF16), coarse_output[...]).astype(BF16)
    for copy in halo:
        copy.wait()
    hidden = norm(wide_c[...].reshape(9 * UNIT, D).astype(F32), gain_c)[2]
    pairs_c[...] = dot(hidden, coarse_attend[:, D:]).astype(BF16)
    bias = bias_at(True, True)
    for pair in range(PAIRS):
        low, high = pair * 128, pair * 128 + 128
        query = stack_heads(query_c[:, low:high])
        keys, values = pairs_c[:, low:high], pairs_c[:, D + low : D + high]
        attention, mixed = attend(query, keys, values, bias)
        mixed_c[:, low:high] = mixed.astype(BF16)
        query_slope, key_slope, value_slope = attend_back(
            query, keys, values, attention, stack_heads(mixed_slope_c[:, low:high])
        )
        query_slope_c[:, low:high] = query_slope.astype(BF16)
        pair_slope_c[:, low:high] = key_slope[4 * UNIT : 5 * UNIT]
        pair_slope_c[:, D + low : D + high] = value_slope[4 * UNIT : 5 * UNIT]
        rims_c[:, :, low:high] = key_slope.astype(BF16).reshape(9, UNIT, 128)
        rims_c[:, :, D + low : D + high] = value_slope.astype(BF16).reshape(9, UNIT, 128)

    halo = []
    for index, step in enumerate(AROUND):
        source = rims_c.at[(1 + step[0]) * 3 + 1 + step[1]]
        copy = wires(source, from_around.at[index], neighbour(step))
        copy.start()
        halo.append(copy)

    moved = field_c[...] + dot(mixed_c[...], coarse_output[...])
    for row in range(6):
        coarse_field[0, row] = moved[row * 8 : row * 8 + 6].astype(BF16)
    slope_flat = slope_c[...].astype(BF16)
    coarse_sum.put(1536, t_dot(mixed_c[...], slope_flat))
    coarse_sum.put(0, t_dot(hidden_c[...], query_slope_c[...]))
    for copy in halo:
        copy.wait()
    pair_slope = pair_slope_c[...]
    for index in range(8):
        pair_slope += from_around[index].astype(F32)
    pair_slope = pair_slope.astype(BF16)
    coarse_sum.put(512, t_dot(hidden_c[...], pair_slope[:, :D]))
    coarse_sum.put(1024, t_dot(hidden_c[...], pair_slope[:, D:]))
    hidden_slope = dot_t(query_slope_c[...], coarse_attend[:, :D]) + dot_t(pair_slope, coarse_attend[:, D:])
    coarse_slope = input_back(slope_c[...], hidden_slope, field_c[...], gain_c).astype(BF16)
    for part in range(4):
        piece = merged[part * UNIT : (part + 1) * UNIT]
        coarse_sum.put_merged(part, 2048, t_dot(piece, coarse_slope))
    merged_slope = jnp.concatenate(
        [dot_t(coarse_slope, merge_weight[part * D : (part + 1) * D]).astype(BF16) for part in range(4)], 0
    )
    coarse_sum.pair_start()

    slope_f[...] = dot(split_ref[...], merged_slope).astype(BF16)
    mixed_slope_f[...] = dot_t(slope_f[...], fine_output[...]).astype(BF16)
    fine_sum.put(1536, t_dot(mixed_f[...], slope_f[...]))
    wide_slope_f[...] = jnp.zeros_like(wide_slope_f)
    coarse_sum.pair_finish()
    coarse_sum.first_start()

    @pl.loop(0, 4)
    def _(quad):
        own = pl.ds(pl.multiple_of(quad * UNIT, UNIT), UNIT)
        starts = starts_of(quad)
        for pair in range(PAIRS):
            low, high = pair * 128, pair * 128 + 128
            query = stack_heads(query_f[own, low:high])
            slope = stack_heads(mixed_slope_f[own, low:high])
            keys = unit_window(3 * UNIT, starts, pairs_f, low)
            values = unit_window(3 * UNIT, starts, pairs_f, D + low)
            query_slope, key_slope, value_slope = attend_back(
                query, keys, values, attention_f[quad, pair], slope
            )
            query_slope_f[own, low:high] = query_slope.astype(BF16)
            for i, start in enumerate(starts):
                rows = pl.ds(start, 3 * UNIT)
                part = slice(i * 3 * UNIT, (i + 1) * 3 * UNIT)
                wide_slope_f[rows, low:high] += key_slope[part]
                wide_slope_f[rows, D + low : D + high] += value_slope[part]

    @pl.loop(0, 16)
    def _(unit):
        rows = pl.ds(pl.multiple_of(unit * UNIT, UNIT), UNIT)
        rims_f[unit // 4, unit % 4] = wide_slope_f[rows, :].astype(BF16)

    targets = {}
    for index, step in enumerate(AROUND):
        if step[0] == 0:
            targets[step] = from_lon.at[index]
        elif step[1] == 0:
            targets[step] = from_lat.at[index - 2]
        else:
            targets[step] = from_corner.at[index - 4]
    halo = []
    for step in AROUND:
        copy = wires(rims_f.at[wide_part(step, False)], targets[step], neighbour(step))
        copy.start()
        halo.append(copy)
    coarse_sum.first_finish()
    coarse_sum.second_start()
    fine_sum.put(0, t_dot(hidden_f[...], query_slope_f[...]))
    for copy in halo:
        copy.wait()
    coarse_sum.second_finish()
    coarse_sum.third_start()

    for index, step in enumerate(AROUND):
        for k in range(4):
            first, second = divmod(k, 2)
            if step[0] and first != (0 if step[0] > 0 else 1):
                continue
            if step[1] and second != (0 if step[1] > 0 else 1):
                continue
            row = ((1 + first) * 4 + 1 + second) * UNIT
            if step[0] == 0:
                piece = from_lon[index, first]
            elif step[1] == 0:
                piece = from_lat[index - 2, second]
            else:
                piece = from_corner[index - 4]
            wide_slope_f[row : row + UNIT, :] += piece.astype(F32)
    centre = [wide_slope_f[r * UNIT : (r + 2) * UNIT, :].astype(BF16) for r in (5, 9)]
    pair_slope = jnp.concatenate(centre, 0)
    fine_sum.put(512, t_dot(hidden_f[...], pair_slope[:, :D]))
    fine_sum.put(1024, t_dot(hidden_f[...], pair_slope[:, D:]))
    fine_sum.pair_start()
    hidden_slope = dot_t(query_slope_f[...], fine_attend[:, :D]) + dot_t(pair_slope, fine_attend[:, D:])
    slope = input_back(slope_f[...].astype(F32), hidden_slope, field_f[...], gain_f)
    for row in range(12):
        for half in range(2):
            place_of = (row // 6 * 2 + half) * UNIT + row % 6 * 8
            strip[row, 6 * half : 6 * half + 6] = slope[place_of : place_of + 6]
    for row in range(12):
        token_gradient[0, row] = strip[row, :12].astype(BF16)

    fine_sum.pair_finish()
    fine_sum.first_start()
    coarse_sum.third_finish()
    coarse_sum.last_start()
    fine_sum.first_finish()
    fine_sum.second_start()
    coarse_sum.last_finish()

    def gain_back(total, weight, gain):
        own = weight[pl.ds(pl.multiple_of(lon * lay.depth, lay.depth), lay.depth), :].astype(F32)
        column = jnp.sum(total * own, axis=1, keepdims=True)
        row = lax.broadcasted_iota(jnp.int32, (lay.depth, D), 0) + lon * lay.depth
        at = lax.broadcasted_iota(jnp.int32, (lay.depth, D), 1) == row
        column = column / jnp.sum(jnp.where(at, gain, 0.0), axis=1, keepdims=True)
        square = (lay.depth, lay.depth)
        same = lax.broadcasted_iota(jnp.int32, square, 0) == lax.broadcasted_iota(jnp.int32, square, 1)
        return jnp.sum(jnp.where(same, column, 0.0), axis=0, keepdims=True)

    total = coarse_sum.column(0, 1536)
    coarse_attend_out[...] = total
    coarse_gain_out[...] = gain_back(total, coarse_attend, gain_c)
    coarse_output_out[...] = coarse_sum.column(1536, D)
    for run in range(4):
        merge_out[run * lay.depth : (run + 1) * lay.depth, :] = coarse_sum.column(2048 + run * D, D)

    fine_sum.second_finish()
    fine_sum.third_start()
    fine_sum.third_finish()
    fine_sum.last_start()
    fine_sum.last_finish()
    total = fine_sum.column(0, 1536)
    fine_attend_out[...] = total
    fine_gain_out[...] = gain_back(total, fine_attend, gain_f)
    fine_output_out[...] = fine_sum.column(1536, D)


def reducer_scratch(lay, width):
    y, x, z, low = lay.y, lay.x, lay.z, lay.z_low
    high = z - low
    end = (lay.depth, width)
    shapes = (
        (2, y, x, z), (y, x, z), (y, x, z),
        (x - 1, y, low), (y - 1, x, high), (y, low), (x, high),
        (y - 1, low), (x - 1, high), (z,), (z - 1,), (2, y),
    )
    return [pltpu.VMEM(shape + end, BF16) for shape in shapes]


def per_device(
    lay,
    tokens,
    cotangent,
    fine_gain,
    fine_attend,
    fine_output,
    merge_weight,
    coarse_gain,
    coarse_attend,
    coarse_output,
):
    vmem = pl.BlockSpec(memory_space=pltpu.VMEM)
    hbm = pl.BlockSpec(memory_space=pl.ANY)
    select = merge_matrix()
    per_batch = 1 + 2 * (lay.x - 1 + lay.y - 1) + lay.z - 1 + 2 * lay.y - 1
    copies = 4 * 8 + 2 * per_batch
    depth = lay.depth
    outs = pl.pallas_call(
        functools.partial(kernel, lay),
        out_shape=(
            jax.ShapeDtypeStruct(cotangent.shape, BF16),
            jax.ShapeDtypeStruct(tokens.shape, BF16),
            jax.ShapeDtypeStruct((1, depth), F32),
            jax.ShapeDtypeStruct((depth, 3 * D), F32),
            jax.ShapeDtypeStruct((depth, D), F32),
            jax.ShapeDtypeStruct((4 * depth, D), F32),
            jax.ShapeDtypeStruct((1, depth), F32),
            jax.ShapeDtypeStruct((depth, 3 * D), F32),
            jax.ShapeDtypeStruct((depth, D), F32),
        ),
        in_specs=[vmem] * 7 + [hbm] * 5,
        out_specs=[vmem] * 9,
        scratch_shapes=[
            pltpu.VMEM((D, 3 * D), BF16),
            pltpu.VMEM((D, D), BF16),
            pltpu.VMEM((4 * D, D), BF16),
            pltpu.VMEM((D, 3 * D), BF16),
            pltpu.VMEM((D, D), BF16),
            pltpu.VMEM((12, 16, D), F32),
            pltpu.VMEM((4 * UNIT, D), F32),
            pltpu.VMEM((4, 4, UNIT, D), BF16),
            pltpu.VMEM((16 * UNIT, 2 * D), BF16),
            pltpu.VMEM((4 * UNIT, D), BF16),
            pltpu.VMEM((4 * UNIT, D), BF16),
            pltpu.VMEM((4, PAIRS, 2 * UNIT, 9 * UNIT), F32),
            pltpu.VMEM((4 * UNIT, D), BF16),
            pltpu.VMEM((4 * UNIT, D), BF16),
            pltpu.VMEM((4 * UNIT, D), BF16),
            pltpu.VMEM((4 * UNIT, D), BF16),
            pltpu.VMEM((16 * UNIT, 2 * D), F32),
            pltpu.VMEM((4, 4, UNIT, 2 * D), BF16),
            pltpu.VMEM((4 * UNIT, D), BF16),
            pltpu.VMEM((2, 2, UNIT, 2 * D), BF16),
            pltpu.VMEM((2, 2, UNIT, 2 * D), BF16),
            pltpu.VMEM((4, UNIT, 2 * D), BF16),
            pltpu.VMEM((UNIT, D), F32),
            pltpu.VMEM((3, 3, UNIT, D), BF16),
            pltpu.VMEM((9 * UNIT, 2 * D), BF16),
            pltpu.VMEM((UNIT, D), BF16),
            pltpu.VMEM((UNIT, D), BF16),
            pltpu.VMEM((2 * UNIT, 9 * UNIT), F32),
            pltpu.VMEM((UNIT, D), BF16),
            pltpu.VMEM((UNIT, D), F32),
            pltpu.VMEM((9, UNIT, 2 * D), BF16),
            pltpu.VMEM((UNIT, D), BF16),
            pltpu.VMEM((UNIT, 2 * D), F32),
            pltpu.VMEM((8, UNIT, 2 * D), BF16),
            *reducer_scratch(lay, lay.coarse_width),
            *reducer_scratch(lay, lay.fine_width),
            pltpu.SemaphoreType.DMA((5,)),
            pltpu.SemaphoreType.DMA((copies,)),
            pltpu.SemaphoreType.DMA((copies,)),
        ],
        compiler_params=pltpu.CompilerParams(
            collective_id=0, has_side_effects=True, vmem_limit_bytes=56 * 1024 * 1024
        ),
    )(
        tokens,
        cotangent,
        fine_gain.reshape(1, D),
        coarse_gain.reshape(1, D),
        jnp.asarray(window_bias()),
        jnp.asarray(select, BF16),
        jnp.asarray(select.T, BF16),
        fine_attend,
        fine_output,
        merge_weight,
        coarse_attend,
        coarse_output,
    )
    outs = list(outs)
    outs[2] = outs[2].reshape(depth)
    outs[6] = outs[6].reshape(depth)
    return tuple(outs)


def solution(mesh):
    return jax.shard_map(
        functools.partial(per_device, Layout(mesh)),
        mesh=mesh,
        in_specs=(
            P("sec", "lat", "lon", None),
            P("sec", "lat", "lon", None),
            P(),
            P(),
            P(),
            P(),
            P(),
            P(),
            P(),
        ),
        out_specs=(
            P("sec", "lat", "lon", None),
            P("sec", "lat", "lon", None),
            P("lon"),
            P("lon", None),
            P("lon", None),
            P("lon", None),
            P("lon"),
            P("lon", None),
            P("lon", None),
        ),
        check_vma=False,
    )
```

```python
import functools

import jax
import jax.numpy as jnp
import numpy as np
from jax import lax
from jax.experimental import pallas as pl
from jax.experimental.pallas import tpu as pltpu
from jax.sharding import PartitionSpec as P

HEADS = 8
RADIUS = 6
EPSILON = 1e-06
NEGATIVE = -1e30
UNIT = 48
D = 512
PAIRS = 4
MESH = pl.DeviceIdType.MESH
F32 = jnp.float32
BF16 = jnp.bfloat16
AROUND = ((0, 1), (0, -1), (1, 0), (-1, 0), (1, 1), (1, -1), (-1, 1), (-1, -1))


def dot(left, right):
    return jnp.dot(left, right, preferred_element_type=F32)


def dot_t(left, right):
    return lax.dot_general(left, right, (((1,), (1,)), ((), ())), preferred_element_type=F32)


def t_dot(left, right):
    return lax.dot_general(left, right, (((0,), (0,)), ((), ())), preferred_element_type=F32)


def near_window():
    query = np.arange(UNIT)
    row, col = query // 8, query % 8
    key = np.arange(9 * UNIT)
    unit, cell = key // UNIT, key % UNIT
    key_row = unit // 3 * RADIUS + cell // 8
    key_col = unit % 3 * RADIUS + cell % 8
    return (
        (key_row[None] >= row[:, None])
        & (key_row[None] <= row[:, None] + 2 * RADIUS)
        & (key_col[None] >= col[:, None])
        & (key_col[None] <= col[:, None] + 2 * RADIUS)
        & (cell % 8 < RADIUS)[None]
    )


def window_bias():
    bias = np.where(near_window(), 0.0, NEGATIVE).astype(np.float32)
    return np.concatenate([bias, bias], 0)


def window_bias_back():
    used = (np.arange(UNIT) % 8 < RADIUS)[:, None]
    bias = np.where(near_window() & used, 0.0, NEGATIVE).astype(np.float32).T
    return np.concatenate([bias, bias], 1)


def head_columns():
    matrix = np.zeros((D, 128), np.float32)
    for head in range(HEADS):
        matrix[head * 64 : head * 64 + 64, head * 8 : head * 8 + 6] = 1.0
    return matrix


def statistic_columns():
    matrix = np.zeros((2, PAIRS, 2 * UNIT, 128), np.float32)
    for which in range(2):
        for head in range(HEADS):
            pair, side = divmod(head, 2)
            start = head * 8 + 3 * which
            matrix[which, pair, side * UNIT : (side + 1) * UNIT, start : start + 3] = 1.0
    return matrix


def merge_matrix():
    matrix = np.zeros((4 * UNIT, 4 * UNIT), np.float32)
    for a in range(2):
        for b in range(2):
            for i in range(RADIUS):
                for j in range(RADIUS):
                    r, c = 2 * i + a, 2 * j + b
                    place = (r // 6 * 2 + c // 6) * UNIT + r % 6 * 8 + c % 6
                    matrix[(a * 2 + b) * UNIT + i * 8 + j, place] = 1.0
    return matrix


class Layout:
    def __init__(self, mesh):
        self.sec, self.lat, self.lon = (mesh.shape[k] for k in ("sec", "lat", "lon"))
        self.x = 4 if self.lon == 32 else 2
        self.z = self.lon // self.x
        self.y_hi = self.lat // 2
        self.y = self.y_hi * self.sec
        self.blocks = self.lon
        self.depth = D // self.blocks
        self.z_low = self.z // 2
        self.fine_width = 1024 // (2 * self.y)
        self.coarse_width = 4096 // (2 * self.y)


def unit_window(width, starts, ref, column):
    return jnp.concatenate([ref[pl.ds(s, width), pl.ds(column, 128)] for s in starts], 0)


def low_lanes(rows):
    return lax.broadcasted_iota(jnp.int32, (rows, 128), 1) < 64


def stack_heads(part):
    part = part.astype(F32)
    low = low_lanes(UNIT)
    return jnp.concatenate([jnp.where(low, part, 0.0), jnp.where(low, 0.0, part)], 0).astype(BF16)


def merge_heads(both):
    return jnp.where(low_lanes(UNIT), both[:UNIT], both[UNIT:])


def attend(query, keys, values, bias):
    scores = dot_t(query, keys) * 0.125 + bias
    peak = jnp.max(scores, axis=-1, keepdims=True)
    expo = jnp.exp(scores - peak)
    total = jnp.sum(expo, axis=-1, keepdims=True)
    attention = expo / total
    return attention, merge_heads(dot(attention.astype(BF16), values)), peak + jnp.log(total)


def query_back(keys, values, attention, slope):
    prob = dot_t(slope, values)
    mean = jnp.sum(attention * prob, axis=-1, keepdims=True)
    score = (attention * (prob - mean) * 0.125).astype(BF16)
    return merge_heads(dot(score, keys))


def pair_back(queries, slopes, statistics, keys, values, bias):
    scores = dot_t(jnp.concatenate([queries, statistics], 1), keys) * 0.125 + bias
    attention = jnp.exp(scores)
    prob = dot_t(jnp.concatenate([slopes, statistics], 1), values)
    score = (attention * prob * 0.125).astype(BF16)
    return merge_heads(t_dot(score, queries)), merge_heads(t_dot(attention.astype(BF16), slopes))


def put_head_columns(total, pair, column):
    head = lax.broadcasted_iota(jnp.int32, total.shape, 1) // 8
    total = jnp.where(head == 2 * pair, column[:UNIT], total)
    return jnp.where(head == 2 * pair + 1, column[UNIT:], total)


def statistics_of(lse, slope, mixed, heads):
    product = slope.astype(F32) * mixed
    high = product.astype(BF16)
    low = (product - high.astype(F32)).astype(BF16)
    mean = dot(high, heads) + dot(low, heads)
    lane = lax.broadcasted_iota(jnp.int32, lse.shape, 1)
    part = lane % 8
    value = jnp.where(part < 3, lse * -8.0, -mean)
    first = value.astype(BF16)
    rest = value - first.astype(F32)
    second = rest.astype(BF16)
    third = rest - second.astype(F32)
    value = jnp.where(part % 3 == 0, first.astype(F32), jnp.where(part % 3 == 1, second.astype(F32), third))
    return jnp.where((part < 6) & (lane < 64), value, 0.0).astype(BF16)


def norm(field, gain):
    factor = lax.rsqrt(jnp.mean(field * field, axis=-1, keepdims=True) + EPSILON)
    normed = field * factor
    return factor, normed, (normed * gain).astype(BF16)


def input_back(slope, hidden_slope, field, gain):
    factor = lax.rsqrt(jnp.mean(field * field, axis=-1, keepdims=True) + EPSILON)
    normed = field * factor
    scaled = hidden_slope * gain
    return slope + factor * (scaled - normed * jnp.mean(scaled * normed, axis=-1, keepdims=True))


class Reducer:
    def __init__(self, lay, place, wires, refs):
        self.lay, self.place, self.wires = lay, place, wires
        (
            self.given, self.in_1a, self.in_1b, self.sum_2a, self.sum_2b,
            self.in_2a, self.in_2b, self.sum_3, self.in_3, self.full,
        ) = refs
        self.copies = []

    def device(self, core=None, y=None, x=None, z=None):
        here = self.place
        core = here["core"] if core is None else core
        y = here["y"] if y is None else y
        x = here["x"] if x is None else x
        z = here["z"] if z is None else z
        return (y % self.lay.sec, y // self.lay.sec * 2 + core, x * self.lay.z + z)

    def send(self, source, target, device):
        copy = self.wires(source, target, device)
        copy.start()
        self.copies.append(copy)

    def arrive(self):
        for copy in self.copies:
            copy.wait()
        self.copies = []

    def first_start(self):
        lay, here = self.lay, self.place
        low = pl.ds(0, lay.z_low)
        high = pl.ds(lay.z_low, lay.z - lay.z_low)
        for step in range(1, lay.x):
            x = (here["x"] + step) % lay.x
            self.send(self.given.at[:, x, low], self.in_1a.at[step - 1], self.device(x=x))
        for step in range(1, lay.y):
            y = (here["y"] + step) % lay.y
            self.send(self.given.at[y, :, high], self.in_1b.at[step - 1], self.device(y=y))

    def first_finish(self):
        self.arrive()
        lay, here = self.lay, self.place
        low = pl.ds(0, lay.z_low)
        high = pl.ds(lay.z_low, lay.z - lay.z_low)

        @pl.loop(0, lay.y)
        def _(y):
            total = self.given[y, here["x"], low].astype(F32)
            for k in range(lay.x - 1):
                total += self.in_1a[k, y].astype(F32)
            self.sum_2a[y] = total.astype(BF16)

        @pl.loop(0, lay.x)
        def _(x):
            total = self.given[here["y"], x, high].astype(F32)
            for k in range(lay.y - 1):
                total += self.in_1b[k, x].astype(F32)
            self.sum_2b[x] = total.astype(BF16)

    def second_start(self):
        lay, here = self.lay, self.place
        for step in range(1, lay.y):
            y = (here["y"] + step) % lay.y
            self.send(self.sum_2a.at[y], self.in_2a.at[step - 1], self.device(y=y))
        for step in range(1, lay.x):
            x = (here["x"] + step) % lay.x
            self.send(self.sum_2b.at[x], self.in_2b.at[step - 1], self.device(x=x))

    def second_finish(self):
        self.arrive()
        lay, here = self.lay, self.place
        total = self.sum_2a[here["y"]].astype(F32)
        for k in range(lay.y - 1):
            total += self.in_2a[k].astype(F32)
        self.sum_3[pl.ds(0, lay.z_low)] = total.astype(BF16)
        total = self.sum_2b[here["x"]].astype(F32)
        for k in range(lay.x - 1):
            total += self.in_2b[k].astype(F32)
        self.sum_3[pl.ds(lay.z_low, lay.z - lay.z_low)] = total.astype(BF16)

    def third_start(self):
        lay, here = self.lay, self.place
        for step in range(1, lay.z):
            z = (here["z"] + step) % lay.z
            self.send(self.sum_3.at[z], self.in_3.at[step - 1], self.device(z=z))

    def third_finish(self):
        self.arrive()
        lay, here = self.lay, self.place
        total = self.sum_3[here["z"]].astype(F32)
        for k in range(lay.z - 1):
            total += self.in_3[k].astype(F32)
        self.full[here["core"], here["y"]] = total.astype(BF16)

    def last_start(self):
        lay, here = self.lay, self.place
        own = self.full.at[here["core"], here["y"]]
        for across in range(2):
            for step in range(lay.y):
                if across or step:
                    core = (here["core"] + across) % 2
                    y = (here["y"] + step) % lay.y
                    self.send(own, own, self.device(core=core, y=y))

    def last_finish(self):
        self.arrive()

    def column(self, start, width):
        size = self.full.shape[-1]
        parts = []
        while width > 0:
            group, offset = divmod(start, size)
            take = min(width, size - offset)
            parts.append(self.full[group // self.lay.y, group % self.lay.y, :, offset : offset + take])
            start, width = start + take, width - take
        return (parts[0] if len(parts) == 1 else jnp.concatenate(parts, 1)).astype(F32)

    def put(self, start, product):
        lay = self.lay
        size = self.given.shape[-1]
        done, width = 0, product.shape[1]
        while done < width:
            group, offset = divmod(start + done, size)
            take = min(width - done, size - offset)
            piece = product[:, done : done + take].astype(BF16)
            self.given[group, :, :, :, offset : offset + take] = piece.reshape(lay.x, lay.z, lay.depth, take)
            done += take

    def put_merged(self, part, product):
        lay = self.lay
        size = self.given.shape[-1]
        count = lay.blocks // 4
        shaped = product.astype(BF16).reshape(count, 4, lay.depth, D)
        for run in range(4):
            group, offset = divmod(run * D, size)
            for block in range(count):
                x, z = divmod(part * count + block, lay.z)
                self.given[group, x, z, :, offset : offset + D] = shaped[block, run]


def gain_back(lay, lon, total, weight, gain):
    own = weight[pl.ds(pl.multiple_of(lon * lay.depth, lay.depth), lay.depth), :].astype(F32)
    column = jnp.sum(total * own, axis=1, keepdims=True)
    row = lax.broadcasted_iota(jnp.int32, (lay.depth, D), 0) + lon * lay.depth
    at = lax.broadcasted_iota(jnp.int32, (lay.depth, D), 1) == row
    column = column / jnp.sum(jnp.where(at, gain, 0.0), axis=1, keepdims=True)
    square = (lay.depth, lay.depth)
    same = lax.broadcasted_iota(jnp.int32, square, 0) == lax.broadcasted_iota(jnp.int32, square, 1)
    return jnp.sum(jnp.where(same, column, 0.0), axis=0, keepdims=True)


def kernel(
    lay,
    tokens, cotangent, fine_gain, coarse_gain, bias_ref, bias_back_ref, heads_ref, columns_ref, merge_ref, split_ref,
    fine_attend_hbm, fine_output_hbm, merge_hbm, coarse_attend_hbm, coarse_output_hbm,
    coarse_field, token_gradient, fine_gain_out, coarse_gain_out, coarse_full, early_full, late_full,
    fine_attend, fine_output, merge_weight, coarse_attend, coarse_output,
    strip, field_f, wide_f, projected_f, attention_f, exact_f, lse_f, slope_wide_f, left_f, right_f, merged,
    field_c, wide_c, slope_wide_c, projected_c, mixed_slope_c, attention_c, exact_c, lse_c, statistics_c, factors_c,
    *rest,
):
    load_sem, send_sem, recv_sem = rest[30:]
    sec, lat, lon = (lax.axis_index(k) for k in ("sec", "lat", "lon"))
    core = lat % 2
    place = {"core": core, "y": lat // 2 * lay.sec + sec, "x": lon // lay.z, "z": lon % lay.z}
    used = [0]

    def wires(source, target, device):
        index = used[0]
        used[0] += 1
        return pltpu.make_async_remote_copy(
            src_ref=source,
            dst_ref=target,
            send_sem=send_sem.at[index],
            recv_sem=recv_sem.at[index],
            device_id=device,
            device_id_type=MESH,
        )

    def neighbour(step):
        return (sec, (lat + step[0] + lay.lat) % lay.lat, (lon + step[1] + lay.lon) % lay.lon)

    def start_rims(source, target):
        copies = []
        for step in AROUND:
            copy = wires(source(step), target(step), neighbour(step))
            if step[0]:
                last = lay.lat - 1
                sends = lat != (last if step[0] > 0 else 0)
                takes = lat != (0 if step[0] > 0 else last)
                pl.when(sends)(copy.start)
                copies.append((copy, sends, takes))
            else:
                copy.start()
                copies.append((copy, None, None))
        return copies

    def wait_rims(copies):
        for copy, sends, takes in copies:
            if sends is None:
                copy.wait()
            else:
                pl.when(sends)(copy.wait_send)
                pl.when(takes)(copy.wait_recv)

    def start_twin(source, target):
        copy = wires(source, target, coarse_sum.device(core=1 - core))
        copy.start()
        return copy

    coarse_sum = Reducer(lay, place, wires, rest[:10])
    early_sum = Reducer(lay, place, wires, rest[10:20])
    late_sum = Reducer(lay, place, wires, rest[20:30])

    loads = [
        pltpu.make_async_copy(source, target, load_sem.at[i])
        for i, (source, target) in enumerate(
            (
                (fine_attend_hbm, fine_attend),
                (fine_output_hbm, fine_output),
                (merge_hbm, merge_weight),
                (coarse_attend_hbm, coarse_attend),
                (coarse_output_hbm, coarse_output),
            )
        )
    ]
    for load in loads:
        load.start()

    for ref in (wide_f, slope_wide_f, wide_c, slope_wide_c, statistics_c):
        for row in (0, ref.shape[0] - 1):
            ref[row] = jnp.zeros(ref.shape[1:], ref.dtype)

    barrier = pltpu.get_barrier_semaphore()
    peers = [neighbour(step) for step in AROUND]
    peers += [coarse_sum.device(x=(place["x"] + s) % lay.x) for s in range(1, lay.x)]
    peers += [coarse_sum.device(z=(place["z"] + s) % lay.z) for s in range(1, lay.z)]
    peers += [
        coarse_sum.device(core=(core + c) % 2, y=(place["y"] + s) % lay.y)
        for c in range(2)
        for s in range(lay.y)
        if c or s
    ]
    for peer in peers:
        pl.semaphore_signal(barrier, inc=1, device_id=peer, device_id_type=MESH)

    field_f[...] = jnp.zeros_like(field_f)
    field_c[...] = jnp.zeros_like(field_c)
    for row in range(12):
        strip[row, :12] = tokens[0, row].astype(F32)
    for row in range(12):
        for half in range(2):
            start = (row // 6 * 2 + half) * UNIT + row % 6 * 8
            field_f[start : start + 6] = strip[row, 6 * half : 6 * half + 6]
    for unit in range(4):
        wide_f[1 + unit // 2, 1 + unit % 2] = field_f[unit * UNIT : (unit + 1) * UNIT].astype(BF16)
    for row in range(6):
        field_c[row * 8 : row * 8 + 6] = cotangent[0, row].astype(F32)
    slope_wide_c[1, 1] = field_c[...].astype(BF16)
    factors_c[5, 0] = field_c[...].astype(BF16)

    pl.semaphore_wait(barrier, len(peers))

    def part(step, mine):
        index = []
        for way in step:
            if way == 0:
                index.append(pl.ds(1, 2))
            elif way > 0:
                index.append(2 if mine else 3)
            else:
                index.append(1 if mine else 0)
        return tuple(index)

    def opposite(step):
        return (-step[0], -step[1])

    def fine_rims(ref):
        return start_rims(lambda step: ref.at[part(step, True)], lambda step: ref.at[part(opposite(step), False)])

    def coarse_rims(ref):
        return start_rims(lambda step: ref.at[1, 1], lambda step: ref.at[1 - step[0], 1 - step[1]])

    rims = fine_rims(wide_f)
    slope_rims = coarse_rims(slope_wide_c)

    top = jnp.where(lat == 0, NEGATIVE, 0.0)
    bottom = jnp.where(lat == lay.lat - 1, NEGATIVE, 0.0)
    lanes = lax.broadcasted_iota(jnp.int32, (1, 9 * UNIT), 1)

    def bias_at(is_first, is_last):
        above = jnp.where(is_first, top, 0.0)
        below = jnp.where(is_last, bottom, 0.0)
        rim = jnp.where(lanes < 3 * UNIT, above, 0.0) + jnp.where(lanes >= 6 * UNIT, below, 0.0)
        return bias_ref[...] + rim

    gain_f = fine_gain[...]
    gain_c = coarse_gain[...]
    loads[0].wait()
    for run in range(2):
        hidden = norm(field_f[run * 96 : run * 96 + 96], gain_f)[2]
        left_f[0, 0, run * 96 : run * 96 + 96] = hidden
        projected_f[240 + run * 192 : 336 + run * 192, :] = dot(hidden, fine_attend[...]).astype(BF16)
    twin_hidden = start_twin(left_f.at[0, 0], left_f.at[0, 1])
    wait_rims(rims)
    for start, units in (
        (0, (wide_f[0].reshape(4 * UNIT, D), wide_f[1, 0])),
        (336, (wide_f[1, 3], wide_f[2, 0])),
        (528, (wide_f[2, 3], wide_f[3].reshape(4 * UNIT, D))),
    ):
        field = jnp.concatenate([unit.astype(F32) for unit in units], 0)
        hidden = norm(field, gain_f)[2]
        projected_f[start : start + field.shape[0], :] = dot(hidden, fine_attend[...]).astype(BF16)

    def starts_of(quad):
        first, second = quad // 2, quad % 2
        return [pl.multiple_of(((first + i) * 4 + second) * UNIT, UNIT) for i in range(3)]

    def middle_of(quad):
        return pl.ds(pl.multiple_of(((1 + quad // 2) * 4 + 1 + quad % 2) * UNIT, UNIT), UNIT)

    def own_of(quad):
        return pl.ds(pl.multiple_of(quad * UNIT, UNIT), UNIT)

    @pl.loop(0, 4)
    def _(quad):
        first = quad // 2
        own, middle, starts = own_of(quad), middle_of(quad), starts_of(quad)
        bias = bias_at(first == 0, first == 1)
        lse = jnp.zeros((UNIT, 128), F32)
        for pair in range(PAIRS):
            low, high = pair * 128, pair * 128 + 128
            query = stack_heads(projected_f[middle, low:high])
            keys = unit_window(3 * UNIT, starts, projected_f, D + low)
            values = unit_window(3 * UNIT, starts, projected_f, 2 * D + low)
            attention, mixed, column = attend(query, keys, values, bias)
            attention_f[quad, pair] = attention
            exact_f[own, low:high] = mixed
            left_f[1, 0, own, low:high] = mixed.astype(BF16)
            lse = put_head_columns(lse, pair, column)
        lse_f[own, :] = lse

    twin_mixed = start_twin(left_f.at[1, 0], left_f.at[1, 1])
    loads[1].wait()
    fine_field = (field_f[...] + dot(left_f[1, 0], fine_output[...])).astype(BF16)
    merged[0] = dot(merge_ref[...], fine_field).astype(BF16)
    loads[2].wait()
    coarse_in = jnp.zeros((UNIT, D), F32)
    for quarter in range(4):
        rows = slice(quarter * UNIT, (quarter + 1) * UNIT)
        coarse_in += dot(merged[0, rows], merge_weight[quarter * D : (quarter + 1) * D])
    wide_c[1, 1] = coarse_in.astype(BF16)
    rims = coarse_rims(wide_c)
    twin_merged = start_twin(merged.at[0], merged.at[1])

    loads[3].wait()
    loads[4].wait()
    field_c[...] = wide_c[1, 1].astype(F32)
    factors_c[0, 0] = norm(field_c[...], gain_c)[2]
    wait_rims(slope_rims)
    mixed_slope_c[...] = dot_t(slope_wide_c[...].reshape(9 * UNIT, D), coarse_output[...]).astype(BF16)
    wait_rims(rims)
    hidden = norm(wide_c[...].reshape(9 * UNIT, D).astype(F32), gain_c)[2]
    projected_c[...] = dot(hidden, coarse_attend[...]).astype(BF16)
    bias = bias_at(True, True)
    middle = slice(4 * UNIT, 5 * UNIT)
    lse = jnp.zeros((UNIT, 128), F32)
    for pair in range(PAIRS):
        low, high = pair * 128, pair * 128 + 128
        query = stack_heads(projected_c[middle, low:high])
        keys, values = projected_c[:, D + low : D + high], projected_c[:, 2 * D + low : 2 * D + high]
        attention, mixed, column = attend(query, keys, values, bias)
        attention_c[pair] = attention
        exact_c[:, low:high] = mixed
        lse = put_head_columns(lse, pair, column)
    statistics_c[1, 1] = statistics_of(lse, mixed_slope_c[middle, :], exact_c[...], heads_ref[...])
    rims = coarse_rims(statistics_c)
    factors_c[4, 0] = exact_c[...].astype(BF16)
    moved = field_c[...] + dot(factors_c[4, 0], coarse_output[...])
    for row in range(6):
        coarse_field[0, row] = moved[row * 8 : row * 8 + 6].astype(BF16)
    for pair in range(PAIRS):
        low, high = pair * 128, pair * 128 + 128
        keys, values = projected_c[:, D + low : D + high], projected_c[:, 2 * D + low : 2 * D + high]
        slope = stack_heads(mixed_slope_c[middle, low:high])
        factors_c[1, 0, :, low:high] = query_back(keys, values, attention_c[pair], slope).astype(BF16)
    wait_rims(rims)
    statistics = statistics_c[...].reshape(9 * UNIT, 128)
    for pair in range(PAIRS):
        low, high = pair * 128, pair * 128 + 128
        keys = jnp.concatenate([stack_heads(projected_c[middle, D + low : D + high]), columns_ref[0, pair]], 1)
        values = jnp.concatenate(
            [stack_heads(projected_c[middle, 2 * D + low : 2 * D + high]), columns_ref[1, pair]], 1
        )
        key_slope, value_slope = pair_back(
            projected_c[:, low:high], mixed_slope_c[:, low:high], statistics, keys, values, bias_back_ref[...]
        )
        factors_c[2, 0, :, low:high] = key_slope.astype(BF16)
        factors_c[3, 0, :, low:high] = value_slope.astype(BF16)
    hidden_slope = sum(
        dot_t(factors_c[1 + k, 0], coarse_attend[:, k * D : (k + 1) * D]) for k in range(3)
    )
    slope = factors_c[5, 0].astype(F32)
    coarse_slope = input_back(slope, hidden_slope, field_c[...], gain_c).astype(BF16)
    factors_c[6, 0] = coarse_slope
    twin_factors = start_twin(factors_c.at[:, 0], factors_c.at[:, 1])

    merged_slope = jnp.concatenate(
        [dot_t(coarse_slope, merge_weight[k * D : (k + 1) * D]).astype(BF16) for k in range(4)], 0
    )
    slope_f = dot(split_ref[...], merged_slope).astype(BF16)
    right_f[1, 0] = slope_f
    mixed_slope = dot_t(slope_f, fine_output[...]).astype(BF16)
    statistics = statistics_of(lse_f[...], mixed_slope, exact_f[...], heads_ref[...])
    for unit in range(4):
        rows = slice(unit * UNIT, (unit + 1) * UNIT)
        slope_wide_f[1 + unit // 2, 1 + unit % 2, :, :D] = mixed_slope[rows]
        slope_wide_f[1 + unit // 2, 1 + unit % 2, :, D:] = statistics[rows]
    rims = fine_rims(slope_wide_f)
    twin_slope = start_twin(right_f.at[1, 0], right_f.at[1, 1])

    twin_factors.wait()
    twin_merged.wait()

    def both(index):
        return factors_c[index].reshape(2 * UNIT, D)

    @pl.when(core == 0)
    def _():
        for k in range(3):
            coarse_sum.put(k * D, t_dot(both(0), both(1 + k)))
        coarse_sum.put(3 * D, t_dot(both(4), both(5)))

    @pl.when(core == 1)
    def _():
        for k in range(4):
            rows = slice(k * UNIT, (k + 1) * UNIT)
            coarse_sum.put_merged(k, t_dot(merged[:, rows].reshape(2 * UNIT, D), both(6)))

    @pl.loop(0, 4)
    def _(quad):
        own, starts = own_of(quad), starts_of(quad)
        for pair in range(PAIRS):
            low, high = pair * 128, pair * 128 + 128
            slope = stack_heads(slope_wide_f[1 + quad // 2, 1 + quad % 2, :, low:high])
            keys = unit_window(3 * UNIT, starts, projected_f, D + low)
            values = unit_window(3 * UNIT, starts, projected_f, 2 * D + low)
            query_slope = query_back(keys, values, attention_f[quad, pair], slope)
            right_f[0, 0, own, low:high] = query_slope.astype(BF16)

    twin_query = start_twin(right_f.at[0, 0], right_f.at[0, 1])
    coarse_sum.first_start()
    twin_hidden.wait()
    twin_mixed.wait()
    twin_slope.wait()
    twin_query.wait()
    early_sum.put(0, t_dot(left_f[core].reshape(8 * UNIT, D), right_f[core].reshape(8 * UNIT, D)))
    wait_rims(rims)
    early_sum.first_start()

    @pl.loop(0, 4)
    def _(quad):
        own, middle, starts = own_of(quad), middle_of(quad), starts_of(quad)
        first, second = quad // 2, quad % 2

        def around(low, high):
            rows = [slope_wide_f[first + i, pl.ds(second, 3), :, low:high] for i in range(3)]
            return jnp.concatenate([r.reshape(3 * UNIT, high - low) for r in rows], 0)

        statistics = around(D, D + 128)
        for pair in range(PAIRS):
            low, high = pair * 128, pair * 128 + 128
            keys = jnp.concatenate([stack_heads(projected_f[middle, D + low : D + high]), columns_ref[0, pair]], 1)
            values = jnp.concatenate(
                [stack_heads(projected_f[middle, 2 * D + low : 2 * D + high]), columns_ref[1, pair]], 1
            )
            key_slope, value_slope = pair_back(
                unit_window(3 * UNIT, starts, projected_f, low),
                around(low, high),
                statistics,
                keys,
                values,
                bias_back_ref[...],
            )
            right_f[2, 0, own, low:high] = key_slope.astype(BF16)
            right_f[3, 0, own, low:high] = value_slope.astype(BF16)

    other = 3 - core
    twin_pair = start_twin(right_f.at[other, 0], right_f.at[other, 1])
    hidden_slope = dot_t(right_f[0, 0], fine_attend[:, :D])
    hidden_slope += dot_t(right_f[2, 0], fine_attend[:, D : 2 * D])
    hidden_slope += dot_t(right_f[3, 0], fine_attend[:, 2 * D :])
    twin_pair.wait()
    late_sum.put(0, t_dot(left_f[0].reshape(8 * UNIT, D), right_f[2 + core].reshape(8 * UNIT, D)))
    late_sum.first_start()
    coarse_sum.first_finish()
    coarse_sum.second_start()
    early_sum.first_finish()
    early_sum.second_start()
    slope = input_back(right_f[1, 0].astype(F32), hidden_slope, field_f[...], gain_f)
    for row in range(12):
        for half in range(2):
            start = (row // 6 * 2 + half) * UNIT + row % 6 * 8
            strip[row, 6 * half : 6 * half + 6] = slope[start : start + 6]
    for row in range(12):
        token_gradient[0, row] = strip[row, :12].astype(BF16)
    late_sum.first_finish()
    late_sum.second_start()
    coarse_sum.second_finish()
    coarse_sum.third_start()
    early_sum.second_finish()
    early_sum.third_start()
    late_sum.second_finish()
    late_sum.third_start()
    coarse_sum.third_finish()
    coarse_sum.last_start()
    early_sum.third_finish()
    early_sum.last_start()
    late_sum.third_finish()
    late_sum.last_start()
    coarse_sum.last_finish()
    coarse_full[...] = coarse_sum.full[...]
    coarse_gain_out[...] = gain_back(lay, lon, coarse_sum.column(0, 3 * D), coarse_attend, gain_c)
    early_sum.last_finish()
    early_full[...] = early_sum.full[...]
    late_sum.last_finish()
    late_full[...] = late_sum.full[...]
    total = jnp.concatenate([early_sum.column(0, D), late_sum.column(0, 2 * D)], 1)
    fine_gain_out[...] = gain_back(lay, lon, total, fine_attend, gain_f)


def finish(lay, *refs):
    field, gradient, fine_gain, coarse_gain, coarse_full, early_full, late_full = refs[:7]
    (
        field_out, gradient_out, fine_gain_out, fine_attend, fine_output, merge,
        coarse_gain_out, coarse_attend, coarse_output,
    ) = refs[7:]
    field_out[...] = field[...]
    gradient_out[...] = gradient[...]
    fine_gain_out[...] = fine_gain[...]
    coarse_gain_out[...] = coarse_gain[...]

    def column(full, start, width):
        return Reducer(lay, None, None, (None,) * 9 + (full,)).column(start, width)

    for k in range(3):
        fine_attend[:, k * D : (k + 1) * D] = column(late_full, (k - 1) * D, D) if k else column(early_full, 0, D)
        coarse_attend[:, k * D : (k + 1) * D] = column(coarse_full, k * D, D)
    fine_output[...] = column(early_full, D, D)
    coarse_output[...] = column(coarse_full, 3 * D, D)
    for run in range(4):
        merge[run * lay.depth : (run + 1) * lay.depth, :] = column(coarse_full, (4 + run) * D, D)


def reducer_scratch(lay, width):
    y, x, z, low = lay.y, lay.x, lay.z, lay.z_low
    high = z - low
    end = (lay.depth, width)
    shapes = (
        (y, x, z), (x - 1, y, low), (y - 1, x, high), (y, low), (x, high),
        (y - 1, low), (x - 1, high), (z,), (z - 1,), (2, y),
    )
    return [pltpu.VMEM(shape + end, BF16) for shape in shapes]


def per_device(
    lay,
    tokens,
    cotangent,
    fine_gain,
    fine_attend,
    fine_output,
    merge_weight,
    coarse_gain,
    coarse_attend,
    coarse_output,
):
    vmem = pl.BlockSpec(memory_space=pltpu.VMEM)
    hbm = pl.BlockSpec(memory_space=pl.ANY)
    select = merge_matrix()
    per_batch = 2 * (lay.x - 1 + lay.y - 1) + lay.z - 1 + 2 * lay.y - 1
    copies = 5 * 8 + 7 + 3 * per_batch
    depth = lay.depth
    fine_shape = jax.ShapeDtypeStruct((2, lay.y, depth, lay.fine_width), BF16)
    between = pl.pallas_call(
        functools.partial(kernel, lay),
        out_shape=(
            jax.ShapeDtypeStruct(cotangent.shape, BF16),
            jax.ShapeDtypeStruct(tokens.shape, BF16),
            jax.ShapeDtypeStruct((1, depth), F32),
            jax.ShapeDtypeStruct((1, depth), F32),
            jax.ShapeDtypeStruct((2, lay.y, depth, lay.coarse_width), BF16),
            fine_shape,
            fine_shape,
        ),
        in_specs=[vmem] * 10 + [hbm] * 5,
        out_specs=[vmem] * 7,
        scratch_shapes=[
            pltpu.VMEM((D, 3 * D), BF16),
            pltpu.VMEM((D, D), BF16),
            pltpu.VMEM((4 * D, D), BF16),
            pltpu.VMEM((D, 3 * D), BF16),
            pltpu.VMEM((D, D), BF16),
            pltpu.VMEM((12, 16, D), F32),
            pltpu.VMEM((4 * UNIT, D), F32),
            pltpu.VMEM((4, 4, UNIT, D), BF16),
            pltpu.VMEM((16 * UNIT, 3 * D), BF16),
            pltpu.VMEM((4, PAIRS, 2 * UNIT, 9 * UNIT), F32),
            pltpu.VMEM((4 * UNIT, D), F32),
            pltpu.VMEM((4 * UNIT, 128), F32),
            pltpu.VMEM((4, 4, UNIT, D + 128), BF16),
            pltpu.VMEM((2, 2, 4 * UNIT, D), BF16),
            pltpu.VMEM((4, 2, 4 * UNIT, D), BF16),
            pltpu.VMEM((2, 4 * UNIT, D), BF16),
            pltpu.VMEM((UNIT, D), F32),
            pltpu.VMEM((3, 3, UNIT, D), BF16),
            pltpu.VMEM((3, 3, UNIT, D), BF16),
            pltpu.VMEM((9 * UNIT, 3 * D), BF16),
            pltpu.VMEM((9 * UNIT, D), BF16),
            pltpu.VMEM((PAIRS, 2 * UNIT, 9 * UNIT), F32),
            pltpu.VMEM((UNIT, D), F32),
            pltpu.VMEM((UNIT, 128), F32),
            pltpu.VMEM((3, 3, UNIT, 128), BF16),
            pltpu.VMEM((7, 2, UNIT, D), BF16),
            *reducer_scratch(lay, lay.coarse_width),
            *reducer_scratch(lay, lay.fine_width),
            *reducer_scratch(lay, lay.fine_width),
            pltpu.SemaphoreType.DMA((5,)),
            pltpu.SemaphoreType.DMA((copies,)),
            pltpu.SemaphoreType.DMA((copies,)),
        ],
        compiler_params=pltpu.CompilerParams(
            collective_id=0, has_side_effects=True, vmem_limit_bytes=56 * 1024 * 1024
        ),
    )(
        tokens,
        cotangent,
        fine_gain.reshape(1, D),
        coarse_gain.reshape(1, D),
        jnp.asarray(window_bias()),
        jnp.asarray(window_bias_back()),
        jnp.asarray(head_columns(), BF16),
        jnp.asarray(statistic_columns(), BF16),
        jnp.asarray(select, BF16),
        jnp.asarray(select.T, BF16),
        fine_attend,
        fine_output,
        merge_weight,
        coarse_attend,
        coarse_output,
    )
    outs = pl.pallas_call(
        functools.partial(finish, lay),
        out_shape=(
            jax.ShapeDtypeStruct(cotangent.shape, BF16),
            jax.ShapeDtypeStruct(tokens.shape, BF16),
            jax.ShapeDtypeStruct((1, depth), F32),
            jax.ShapeDtypeStruct((depth, 3 * D), F32),
            jax.ShapeDtypeStruct((depth, D), F32),
            jax.ShapeDtypeStruct((4 * depth, D), F32),
            jax.ShapeDtypeStruct((1, depth), F32),
            jax.ShapeDtypeStruct((depth, 3 * D), F32),
            jax.ShapeDtypeStruct((depth, D), F32),
        ),
        in_specs=[vmem] * 7,
        out_specs=[vmem] * 9,
    )(*between)
    outs = list(outs)
    outs[2] = outs[2].reshape(depth)
    outs[6] = outs[6].reshape(depth)
    return tuple(outs)


def solution(mesh):
    return jax.shard_map(
        functools.partial(per_device, Layout(mesh)),
        mesh=mesh,
        in_specs=(
            P("sec", "lat", "lon", None),
            P("sec", "lat", "lon", None),
            P(),
            P(),
            P(),
            P(),
            P(),
            P(),
            P(),
        ),
        out_specs=(
            P("sec", "lat", "lon", None),
            P("sec", "lat", "lon", None),
            P("lon"),
            P("lon", None),
            P("lon", None),
            P("lon", None),
            P("lon"),
            P("lon", None),
            P("lon", None),
        ),
        check_vma=False,
    )
```

```python
import functools

import jax
import jax.numpy as jnp
import numpy as np
from jax import lax
from jax.experimental import pallas as pl
from jax.experimental.pallas import tpu as pltpu
from jax.sharding import PartitionSpec as P

HEADS = 8
RADIUS = 6
EPSILON = 1e-06
NEGATIVE = -1e30
UNIT = 48
D = 512
PAIRS = 4
MESH = pl.DeviceIdType.MESH
F32 = jnp.float32
BF16 = jnp.bfloat16
AROUND = ((0, 1), (0, -1), (1, 0), (-1, 0), (1, 1), (1, -1), (-1, 1), (-1, -1))


def dot(left, right):
    return jnp.dot(left, right, preferred_element_type=F32)


def dot_t(left, right):
    return lax.dot_general(left, right, (((1,), (1,)), ((), ())), preferred_element_type=F32)


def t_dot(left, right):
    return lax.dot_general(left, right, (((0,), (0,)), ((), ())), preferred_element_type=F32)


def near_window():
    query = np.arange(UNIT)
    row, col = query // 8, query % 8
    key = np.arange(9 * UNIT)
    unit, cell = key // UNIT, key % UNIT
    key_row = unit // 3 * RADIUS + cell // 8
    key_col = unit % 3 * RADIUS + cell % 8
    return (
        (key_row[None] >= row[:, None])
        & (key_row[None] <= row[:, None] + 2 * RADIUS)
        & (key_col[None] >= col[:, None])
        & (key_col[None] <= col[:, None] + 2 * RADIUS)
        & (cell % 8 < RADIUS)[None]
    )


def window_bias():
    bias = np.where(near_window(), 0.0, NEGATIVE).astype(np.float32)
    return np.concatenate([bias, bias], 0)


def window_bias_back():
    used = (np.arange(UNIT) % 8 < RADIUS)[:, None]
    bias = np.where(near_window() & used, 0.0, NEGATIVE).astype(np.float32).T
    return np.concatenate([bias, bias], 1)


def head_columns():
    matrix = np.zeros((D, 128), np.float32)
    for head in range(HEADS):
        matrix[head * 64 : head * 64 + 64, head * 8 : head * 8 + 6] = 1.0
    return matrix


def statistic_columns():
    matrix = np.zeros((2, PAIRS, 2 * UNIT, 128), np.float32)
    for which in range(2):
        for head in range(HEADS):
            pair, side = divmod(head, 2)
            start = head * 8 + 3 * which
            matrix[which, pair, side * UNIT : (side + 1) * UNIT, start : start + 3] = 0.125
    return matrix


def merge_matrix():
    matrix = np.zeros((4 * UNIT, 4 * UNIT), np.float32)
    for a in range(2):
        for b in range(2):
            for i in range(RADIUS):
                for j in range(RADIUS):
                    r, c = 2 * i + a, 2 * j + b
                    place = (r // 6 * 2 + c // 6) * UNIT + r % 6 * 8 + c % 6
                    matrix[(a * 2 + b) * UNIT + i * 8 + j, place] = 1.0
    return matrix


class Layout:
    def __init__(self, mesh):
        self.sec, self.lat, self.lon = (mesh.shape[k] for k in ("sec", "lat", "lon"))
        self.x = 4 if self.lon == 32 else 2
        self.z = self.lon // self.x
        self.y_hi = self.lat // 2
        self.y = self.y_hi * self.sec
        self.blocks = self.lon
        self.depth = D // self.blocks
        self.z_low = self.z // 2
        self.fine_width = 1024 // (2 * self.y)
        self.coarse_width = 4096 // (2 * self.y)


def unit_window(width, starts, ref, column):
    return jnp.concatenate([ref[pl.ds(s, width), pl.ds(column, 128)] for s in starts], 0)


def low_lanes(rows):
    return lax.broadcasted_iota(jnp.int32, (rows, 128), 1) < 64


def stack_heads(part):
    part = part.astype(F32) * 0.125
    low = low_lanes(UNIT)
    return jnp.concatenate([jnp.where(low, part, 0.0), jnp.where(low, 0.0, part)], 0).astype(BF16)


def merge_heads(both):
    return jnp.where(low_lanes(UNIT), both[:UNIT], both[UNIT:])


def attend(queries, keys, values, bias):
    scores = [dot_t(q, k) + bias for q, k in zip(queries, keys)]
    peaks = [jnp.max(s, axis=-1, keepdims=True) for s in scores]
    expos = [jnp.exp(s - m) for s, m in zip(scores, peaks)]
    totals = [jnp.sum(e, axis=-1, keepdims=True) for e in expos]
    attentions = [e * (1.0 / t) for e, t in zip(expos, totals)]
    mixed = [merge_heads(dot(a.astype(BF16), v)) for a, v in zip(attentions, values)]
    return attentions, mixed, [m + jnp.log(t) for m, t in zip(peaks, totals)]


def query_back(keys, values, attentions, slopes):
    probs = [dot_t(s, v) for s, v in zip(slopes, values)]
    means = [jnp.sum(a * p, axis=-1, keepdims=True) for a, p in zip(attentions, probs)]
    scores = [(a * (p - m)).astype(BF16) for a, p, m in zip(attentions, probs, means)]
    return [merge_heads(dot(s, k)) for s, k in zip(scores, keys)]


def pair_back(queries, slopes, statistics, keys, values, bias):
    scores = [dot_t(jnp.concatenate([q, statistics], 1), k) + bias for q, k in zip(queries, keys)]
    probs = [dot_t(jnp.concatenate([s, statistics], 1), v) for s, v in zip(slopes, values)]
    attentions = [jnp.exp(s) for s in scores]
    scores = [(a * p).astype(BF16) for a, p in zip(attentions, probs)]
    return (
        [merge_heads(t_dot(s, q)) for s, q in zip(scores, queries)],
        [merge_heads(t_dot(a.astype(BF16), s)) for a, s in zip(attentions, slopes)],
    )


def put_head_columns(total, pair, column):
    head = lax.broadcasted_iota(jnp.int32, total.shape, 1) // 8
    total = jnp.where(head == 2 * pair, column[:UNIT], total)
    return jnp.where(head == 2 * pair + 1, column[UNIT:], total)


def statistics_of(lse, slope, mixed, heads):
    product = slope.astype(F32) * mixed
    high = product.astype(BF16)
    low = (product - high.astype(F32)).astype(BF16)
    mean = dot(high, heads) + dot(low, heads)
    lane = lax.broadcasted_iota(jnp.int32, lse.shape, 1)
    part = lane % 8
    value = jnp.where(part < 3, lse * -8.0, -mean)
    first = value.astype(BF16)
    rest = value - first.astype(F32)
    second = rest.astype(BF16)
    third = rest - second.astype(F32)
    value = jnp.where(part % 3 == 0, first.astype(F32), jnp.where(part % 3 == 1, second.astype(F32), third))
    return jnp.where((part < 6) & (lane < 64), value, 0.0).astype(BF16)


def norm(field, gain):
    factor = lax.rsqrt(jnp.mean(field * field, axis=-1, keepdims=True) + EPSILON)
    normed = field * factor
    return factor, normed, (normed * gain).astype(BF16)


def input_back(slope, hidden_slope, field, gain):
    factor = lax.rsqrt(jnp.mean(field * field, axis=-1, keepdims=True) + EPSILON)
    normed = field * factor
    scaled = hidden_slope * gain
    return slope + factor * (scaled - normed * jnp.mean(scaled * normed, axis=-1, keepdims=True))


class Reducer:
    def __init__(self, lay, place, wires, refs):
        self.lay, self.place, self.wires = lay, place, wires
        (
            self.given, self.in_1a, self.in_1b, self.sum_2a, self.sum_2b,
            self.in_2a, self.in_2b, self.sum_3, self.in_3, self.full,
        ) = refs
        self.copies = []

    def device(self, core=None, y=None, x=None, z=None):
        here = self.place
        core = here["core"] if core is None else core
        y = here["y"] if y is None else y
        x = here["x"] if x is None else x
        z = here["z"] if z is None else z
        return (y % self.lay.sec, y // self.lay.sec * 2 + core, x * self.lay.z + z)

    def send(self, source, target, device):
        copy = self.wires(source, target, device)
        copy.start()
        self.copies.append(copy)

    def arrive(self):
        for copy in self.copies:
            copy.wait()
        self.copies = []

    def first_start(self):
        lay, here = self.lay, self.place
        low = pl.ds(0, lay.z_low)
        high = pl.ds(lay.z_low, lay.z - lay.z_low)
        for step in range(1, lay.x):
            x = (here["x"] + step) % lay.x
            self.send(self.given.at[:, x, low], self.in_1a.at[step - 1], self.device(x=x))
        for step in range(1, lay.y):
            y = (here["y"] + step) % lay.y
            self.send(self.given.at[y, :, high], self.in_1b.at[step - 1], self.device(y=y))

    def first_finish(self):
        self.arrive()
        lay, here = self.lay, self.place
        low = pl.ds(0, lay.z_low)
        high = pl.ds(lay.z_low, lay.z - lay.z_low)

        @pl.loop(0, lay.y)
        def _(y):
            total = self.given[y, here["x"], low].astype(F32)
            for k in range(lay.x - 1):
                total += self.in_1a[k, y].astype(F32)
            self.sum_2a[y] = total.astype(BF16)

        @pl.loop(0, lay.x)
        def _(x):
            total = self.given[here["y"], x, high].astype(F32)
            for k in range(lay.y - 1):
                total += self.in_1b[k, x].astype(F32)
            self.sum_2b[x] = total.astype(BF16)

    def second_start(self):
        lay, here = self.lay, self.place
        for step in range(1, lay.y):
            y = (here["y"] + step) % lay.y
            self.send(self.sum_2a.at[y], self.in_2a.at[step - 1], self.device(y=y))
        for step in range(1, lay.x):
            x = (here["x"] + step) % lay.x
            self.send(self.sum_2b.at[x], self.in_2b.at[step - 1], self.device(x=x))

    def second_finish(self):
        self.arrive()
        lay, here = self.lay, self.place
        total = self.sum_2a[here["y"]].astype(F32)
        for k in range(lay.y - 1):
            total += self.in_2a[k].astype(F32)
        self.sum_3[pl.ds(0, lay.z_low)] = total.astype(BF16)
        total = self.sum_2b[here["x"]].astype(F32)
        for k in range(lay.x - 1):
            total += self.in_2b[k].astype(F32)
        self.sum_3[pl.ds(lay.z_low, lay.z - lay.z_low)] = total.astype(BF16)

    def third_start(self):
        lay, here = self.lay, self.place
        for step in range(1, lay.z):
            z = (here["z"] + step) % lay.z
            self.send(self.sum_3.at[z], self.in_3.at[step - 1], self.device(z=z))

    def third_finish(self):
        self.arrive()
        lay, here = self.lay, self.place
        total = self.sum_3[here["z"]].astype(F32)
        for k in range(lay.z - 1):
            total += self.in_3[k].astype(F32)
        self.full[here["core"], here["y"]] = total.astype(BF16)

    def last_start(self):
        lay, here = self.lay, self.place
        own = self.full.at[here["core"], here["y"]]
        for across in range(2):
            for step in range(lay.y):
                if across or step:
                    core = (here["core"] + across) % 2
                    y = (here["y"] + step) % lay.y
                    self.send(own, own, self.device(core=core, y=y))

    def last_finish(self):
        self.arrive()

    def column(self, start, width):
        size = self.full.shape[-1]
        parts = []
        while width > 0:
            group, offset = divmod(start, size)
            take = min(width, size - offset)
            parts.append(self.full[group // self.lay.y, group % self.lay.y, :, offset : offset + take])
            start, width = start + take, width - take
        return (parts[0] if len(parts) == 1 else jnp.concatenate(parts, 1)).astype(F32)

    def put(self, start, product):
        lay = self.lay
        size = self.given.shape[-1]
        done, width = 0, product.shape[1]
        while done < width:
            group, offset = divmod(start + done, size)
            take = min(width - done, size - offset)
            piece = product[:, done : done + take].astype(BF16)
            self.given[group, :, :, :, offset : offset + take] = piece.reshape(lay.x, lay.z, lay.depth, take)
            done += take

    def put_merged(self, part, product):
        lay = self.lay
        size = self.given.shape[-1]
        count = lay.blocks // 4
        shaped = product.astype(BF16).reshape(count, 4, lay.depth, D)
        for run in range(4):
            group, offset = divmod(run * D, size)
            for block in range(count):
                x, z = divmod(part * count + block, lay.z)
                self.given[group, x, z, :, offset : offset + D] = shaped[block, run]


GROUPS = ((0, 1, 2, 3),)


def lanes_of(pair, start=0):
    return slice(start + pair * 128, start + pair * 128 + 128)


def with_columns(part, columns):
    return jnp.concatenate([stack_heads(part), columns], 1)


def gain_back(lay, lon, total, weight, gain):
    own = weight[pl.ds(pl.multiple_of(lon * lay.depth, lay.depth), lay.depth), :].astype(F32)
    column = jnp.sum(total * own, axis=1, keepdims=True)
    row = lax.broadcasted_iota(jnp.int32, (lay.depth, D), 0) + lon * lay.depth
    at = lax.broadcasted_iota(jnp.int32, (lay.depth, D), 1) == row
    column = column / jnp.sum(jnp.where(at, gain, 0.0), axis=1, keepdims=True)
    square = (lay.depth, lay.depth)
    same = lax.broadcasted_iota(jnp.int32, square, 0) == lax.broadcasted_iota(jnp.int32, square, 1)
    return jnp.sum(jnp.where(same, column, 0.0), axis=0, keepdims=True)


def kernel(
    lay,
    tokens, cotangent, fine_gain, coarse_gain,
    fine_attend_hbm, fine_output_hbm, merge_hbm, coarse_attend_hbm, coarse_output_hbm,
    bias_hbm, bias_back_hbm, heads_hbm, columns_hbm, merge_ref_hbm, split_hbm,
    coarse_field, token_gradient, fine_gain_out, coarse_gain_out, coarse_full, early_full, late_full,
    fine_attend, fine_output, merge_weight, coarse_attend, coarse_output,
    bias_ref, bias_back_ref, heads_ref, columns_ref, merge_ref, split_ref,
    strip, field_f, wide_f, projected_f, attention_f, exact_f, lse_f, slope_wide_f, left_f, right_f, merged,
    field_c, wide_c, slope_wide_c, projected_c, mixed_slope_c, attention_c, exact_c, lse_c, statistics_c, factors_c,
    *rest,
):
    load_sem, send_sem, recv_sem = rest[30:]
    sec, lat, lon = (lax.axis_index(k) for k in ("sec", "lat", "lon"))
    core = lat % 2
    place = {"core": core, "y": lat // 2 * lay.sec + sec, "x": lon // lay.z, "z": lon % lay.z}
    used = [0]

    def wires(source, target, device):
        index = used[0]
        used[0] += 1
        return pltpu.make_async_remote_copy(
            src_ref=source,
            dst_ref=target,
            send_sem=send_sem.at[index],
            recv_sem=recv_sem.at[index],
            device_id=device,
            device_id_type=MESH,
        )

    def neighbour(step):
        return (sec, (lat + step[0] + lay.lat) % lay.lat, (lon + step[1] + lay.lon) % lay.lon)

    def start_rims(source, target):
        copies = []
        for step in AROUND:
            copy = wires(source(step), target(step), neighbour(step))
            if step[0]:
                last = lay.lat - 1
                sends = lat != (last if step[0] > 0 else 0)
                takes = lat != (0 if step[0] > 0 else last)
                pl.when(sends)(copy.start)
                copies.append((copy, sends, takes))
            else:
                copy.start()
                copies.append((copy, None, None))
        return copies

    def wait_rims(copies):
        for copy, sends, takes in copies:
            if sends is None:
                copy.wait()
            else:
                pl.when(sends)(copy.wait_send)
                pl.when(takes)(copy.wait_recv)

    def start_twin(source, target):
        copy = wires(source, target, coarse_sum.device(core=1 - core))
        copy.start()
        return copy

    coarse_sum = Reducer(lay, place, wires, rest[:10])
    early_sum = Reducer(lay, place, wires, rest[10:20])
    late_sum = Reducer(lay, place, wires, rest[20:30])

    barrier = pltpu.get_barrier_semaphore()
    peers = [neighbour(step) for step in AROUND]
    peers += [coarse_sum.device(x=(place["x"] + s) % lay.x) for s in range(1, lay.x)]
    peers += [coarse_sum.device(z=(place["z"] + s) % lay.z) for s in range(1, lay.z)]
    peers += [
        coarse_sum.device(core=(core + c) % 2, y=(place["y"] + s) % lay.y)
        for c in range(2)
        for s in range(lay.y)
        if c or s
    ]
    for peer in peers:
        pl.semaphore_signal(barrier, inc=1, device_id=peer, device_id_type=MESH)

    loads = {
        name: pltpu.make_async_copy(source, target, load_sem.at[i])
        for i, (name, source, target) in enumerate(
            (
                ("fine_attend", fine_attend_hbm, fine_attend),
                ("bias_ref", bias_hbm, bias_ref),
                ("fine_output", fine_output_hbm, fine_output),
                ("merge_ref", merge_ref_hbm, merge_ref),
                ("merge_weight", merge_hbm, merge_weight),
                ("coarse_output", coarse_output_hbm, coarse_output),
                ("coarse_attend", coarse_attend_hbm, coarse_attend),
                ("heads_ref", heads_hbm, heads_ref),
                ("columns_ref", columns_hbm, columns_ref),
                ("bias_back_ref", bias_back_hbm, bias_back_ref),
                ("split_ref", split_hbm, split_ref),
            )
        )
    }
    for load in loads.values():
        load.start()

    field_f[...] = jnp.zeros_like(field_f)
    field_c[...] = jnp.zeros_like(field_c)
    for row in range(12):
        strip[row, :12] = tokens[0, row].astype(F32)
    for row in range(12):
        for half in range(2):
            start = (row // 6 * 2 + half) * UNIT + row % 6 * 8
            field_f[start : start + 6] = strip[row, 6 * half : 6 * half + 6]
    for unit in range(4):
        wide_f[1 + unit // 2, 1 + unit % 2] = field_f[unit * UNIT : (unit + 1) * UNIT].astype(BF16)
    for row in range(6):
        field_c[row * 8 : row * 8 + 6] = cotangent[0, row].astype(F32)
    slope_wide_c[1, 1] = field_c[...].astype(BF16)
    factors_c[5, 0] = field_c[...].astype(BF16)

    pl.semaphore_wait(barrier, len(peers))

    def part(step, mine):
        index = []
        for way in step:
            if way == 0:
                index.append(pl.ds(1, 2))
            elif way > 0:
                index.append(2 if mine else 3)
            else:
                index.append(1 if mine else 0)
        return tuple(index)

    def opposite(step):
        return (-step[0], -step[1])

    def fine_rims(ref):
        return start_rims(lambda step: ref.at[part(step, True)], lambda step: ref.at[part(opposite(step), False)])

    def coarse_rims(ref):
        return start_rims(lambda step: ref.at[1, 1], lambda step: ref.at[1 - step[0], 1 - step[1]])

    rims = fine_rims(wide_f)

    def clear(row):
        for ref in (wide_f, slope_wide_f, wide_c, slope_wide_c, statistics_c):
            ref[row if row == 0 else ref.shape[0] - 1] = jnp.zeros(ref.shape[1:], ref.dtype)

    pl.when(lat == 0)(lambda: clear(0))
    pl.when(lat == lay.lat - 1)(lambda: clear(-1))

    top = jnp.where(lat == 0, NEGATIVE, 0.0)
    bottom = jnp.where(lat == lay.lat - 1, NEGATIVE, 0.0)
    lanes = lax.broadcasted_iota(jnp.int32, (1, 9 * UNIT), 1)

    def bias_at(is_first, is_last):
        above = jnp.where(is_first, top, 0.0)
        below = jnp.where(is_last, bottom, 0.0)
        rim = jnp.where(lanes < 3 * UNIT, above, 0.0) + jnp.where(lanes >= 6 * UNIT, below, 0.0)
        return bias_ref[...] + rim

    gain_f = fine_gain[...]
    gain_c = coarse_gain[...]
    loads["fine_attend"].wait()
    for run in range(2):
        hidden = norm(field_f[run * 96 : run * 96 + 96], gain_f)[2]
        left_f[0, 0, run * 96 : run * 96 + 96] = hidden
        projected_f[240 + run * 192 : 336 + run * 192, :] = dot(hidden, fine_attend[...]).astype(BF16)
    twin_hidden = start_twin(left_f.at[0, 0], left_f.at[0, 1])
    wait_rims(rims)
    slope_rims = coarse_rims(slope_wide_c)
    for start, units in (
        (0, (wide_f[0].reshape(4 * UNIT, D), wide_f[1, 0])),
        (336, (wide_f[1, 3], wide_f[2, 0])),
        (528, (wide_f[2, 3], wide_f[3].reshape(4 * UNIT, D))),
    ):
        field = jnp.concatenate([unit.astype(F32) for unit in units], 0)
        hidden = norm(field, gain_f)[2]
        projected_f[start : start + field.shape[0], :] = dot(hidden, fine_attend[...]).astype(BF16)

    loads["bias_ref"].wait()

    def starts_of(quad):
        first, second = quad // 2, quad % 2
        return [pl.multiple_of(((first + i) * 4 + second) * UNIT, UNIT) for i in range(3)]

    def middle_of(quad):
        return pl.ds(pl.multiple_of(((1 + quad // 2) * 4 + 1 + quad % 2) * UNIT, UNIT), UNIT)

    def own_of(quad):
        return pl.ds(pl.multiple_of(quad * UNIT, UNIT), UNIT)

    @pl.loop(0, 4)
    def _(quad):
        first = quad // 2
        own, middle, starts = own_of(quad), middle_of(quad), starts_of(quad)
        bias = bias_at(first == 0, first == 1)
        lse = jnp.zeros((UNIT, 128), F32)
        for pairs in GROUPS:
            results = attend(
                [stack_heads(projected_f[middle, lanes_of(pair)]) for pair in pairs],
                [unit_window(3 * UNIT, starts, projected_f, D + pair * 128) for pair in pairs],
                [unit_window(3 * UNIT, starts, projected_f, 2 * D + pair * 128) for pair in pairs],
                bias,
            )
            for pair, attention, mixed, column in zip(pairs, *results):
                attention_f[quad, pair] = attention
                exact_f[own, lanes_of(pair)] = mixed
                left_f[1, 0, own, lanes_of(pair)] = mixed.astype(BF16)
                lse = put_head_columns(lse, pair, column)
        lse_f[own, :] = lse

    twin_mixed = start_twin(left_f.at[1, 0], left_f.at[1, 1])
    loads["fine_output"].wait()
    loads["merge_ref"].wait()
    fine_field = (field_f[...] + dot(left_f[1, 0], fine_output[...])).astype(BF16)
    merged[0] = dot(merge_ref[...], fine_field).astype(BF16)
    loads["merge_weight"].wait()
    coarse_in = jnp.zeros((UNIT, D), F32)
    for quarter in range(4):
        rows = slice(quarter * UNIT, (quarter + 1) * UNIT)
        coarse_in += dot(merged[0, rows], merge_weight[quarter * D : (quarter + 1) * D])
    wide_c[1, 1] = coarse_in.astype(BF16)
    rims = coarse_rims(wide_c)
    twin_merged = start_twin(merged.at[0], merged.at[1])

    for name in ("coarse_output", "coarse_attend", "heads_ref", "columns_ref", "bias_back_ref", "split_ref"):
        loads[name].wait()
    field_c[...] = wide_c[1, 1].astype(F32)
    factors_c[0, 0] = norm(field_c[...], gain_c)[2]
    wait_rims(slope_rims)
    mixed_slope_c[...] = dot_t(slope_wide_c[...].reshape(9 * UNIT, D), coarse_output[...]).astype(BF16)
    wait_rims(rims)
    hidden = norm(wide_c[...].reshape(9 * UNIT, D).astype(F32), gain_c)[2]
    projected_c[...] = dot(hidden, coarse_attend[...]).astype(BF16)
    bias = bias_at(True, True)
    middle = slice(4 * UNIT, 5 * UNIT)
    lse = jnp.zeros((UNIT, 128), F32)
    for pairs in GROUPS:
        results = attend(
            [stack_heads(projected_c[middle, lanes_of(pair)]) for pair in pairs],
            [projected_c[:, lanes_of(pair, D)] for pair in pairs],
            [projected_c[:, lanes_of(pair, 2 * D)] for pair in pairs],
            bias,
        )
        for pair, attention, mixed, column in zip(pairs, *results):
            attention_c[pair] = attention
            exact_c[:, lanes_of(pair)] = mixed
            lse = put_head_columns(lse, pair, column)
    statistics_c[1, 1] = statistics_of(lse, mixed_slope_c[middle, :], exact_c[...], heads_ref[...])
    rims = coarse_rims(statistics_c)
    factors_c[4, 0] = exact_c[...].astype(BF16)
    moved = field_c[...] + dot(factors_c[4, 0], coarse_output[...])
    for row in range(6):
        coarse_field[0, row] = moved[row * 8 : row * 8 + 6].astype(BF16)
    for pairs in GROUPS:
        results = query_back(
            [projected_c[:, lanes_of(pair, D)] for pair in pairs],
            [projected_c[:, lanes_of(pair, 2 * D)] for pair in pairs],
            [attention_c[pair] for pair in pairs],
            [stack_heads(mixed_slope_c[middle, lanes_of(pair)]) for pair in pairs],
        )
        for pair, query_slope in zip(pairs, results):
            factors_c[1, 0, :, lanes_of(pair)] = query_slope.astype(BF16)
    wait_rims(rims)
    statistics = statistics_c[...].reshape(9 * UNIT, 128)
    for pairs in GROUPS:
        results = pair_back(
            [projected_c[:, lanes_of(pair)] for pair in pairs],
            [mixed_slope_c[:, lanes_of(pair)] for pair in pairs],
            statistics,
            [with_columns(projected_c[middle, lanes_of(pair, D)], columns_ref[0, pair]) for pair in pairs],
            [with_columns(projected_c[middle, lanes_of(pair, 2 * D)], columns_ref[1, pair]) for pair in pairs],
            bias_back_ref[...],
        )
        for pair, key_slope, value_slope in zip(pairs, *results):
            factors_c[2, 0, :, lanes_of(pair)] = key_slope.astype(BF16)
            factors_c[3, 0, :, lanes_of(pair)] = value_slope.astype(BF16)
    hidden_slope = sum(
        dot_t(factors_c[1 + k, 0], coarse_attend[:, k * D : (k + 1) * D]) for k in range(3)
    )
    slope = factors_c[5, 0].astype(F32)
    coarse_slope = input_back(slope, hidden_slope, field_c[...], gain_c).astype(BF16)
    factors_c[6, 0] = coarse_slope
    twin_factors = start_twin(factors_c.at[:, 0], factors_c.at[:, 1])

    merged_slope = jnp.concatenate(
        [dot_t(coarse_slope, merge_weight[k * D : (k + 1) * D]).astype(BF16) for k in range(4)], 0
    )
    slope_f = dot(split_ref[...], merged_slope).astype(BF16)
    right_f[1, 0] = slope_f
    mixed_slope = dot_t(slope_f, fine_output[...]).astype(BF16)
    statistics = statistics_of(lse_f[...], mixed_slope, exact_f[...], heads_ref[...])
    for unit in range(4):
        rows = slice(unit * UNIT, (unit + 1) * UNIT)
        slope_wide_f[1 + unit // 2, 1 + unit % 2, :, :D] = mixed_slope[rows]
        slope_wide_f[1 + unit // 2, 1 + unit % 2, :, D:] = statistics[rows]
    rims = fine_rims(slope_wide_f)
    twin_slope = start_twin(right_f.at[1, 0], right_f.at[1, 1])

    twin_factors.wait()
    twin_merged.wait()

    def both(index):
        return factors_c[index].reshape(2 * UNIT, D)

    @pl.when(core == 0)
    def _():
        for k in range(3):
            coarse_sum.put(k * D, t_dot(both(0), both(1 + k)))
        coarse_sum.put(3 * D, t_dot(both(4), both(5)))

    @pl.when(core == 1)
    def _():
        for k in range(4):
            rows = slice(k * UNIT, (k + 1) * UNIT)
            coarse_sum.put_merged(k, t_dot(merged[:, rows].reshape(2 * UNIT, D), both(6)))

    coarse_sum.first_start()

    @pl.loop(0, 4)
    def _(quad):
        own, starts = own_of(quad), starts_of(quad)
        for pairs in GROUPS:
            results = query_back(
                [unit_window(3 * UNIT, starts, projected_f, D + pair * 128) for pair in pairs],
                [unit_window(3 * UNIT, starts, projected_f, 2 * D + pair * 128) for pair in pairs],
                [attention_f[quad, pair] for pair in pairs],
                [stack_heads(slope_wide_f[1 + quad // 2, 1 + quad % 2, :, lanes_of(pair)]) for pair in pairs],
            )
            for pair, query_slope in zip(pairs, results):
                right_f[0, 0, own, lanes_of(pair)] = query_slope.astype(BF16)

    twin_query = start_twin(right_f.at[0, 0], right_f.at[0, 1])
    twin_hidden.wait()
    twin_mixed.wait()
    twin_slope.wait()
    twin_query.wait()
    early_sum.put(0, t_dot(left_f[core].reshape(8 * UNIT, D), right_f[core].reshape(8 * UNIT, D)))
    wait_rims(rims)
    early_sum.first_start()

    @pl.loop(0, 4)
    def _(quad):
        own, middle, starts = own_of(quad), middle_of(quad), starts_of(quad)
        first, second = quad // 2, quad % 2

        def around(lanes):
            rows = [slope_wide_f[first + i, pl.ds(second, 3), :, lanes] for i in range(3)]
            return jnp.concatenate([r.reshape(3 * UNIT, 128) for r in rows], 0)

        statistics = around(slice(D, D + 128))
        for pairs in GROUPS:
            results = pair_back(
                [unit_window(3 * UNIT, starts, projected_f, pair * 128) for pair in pairs],
                [around(lanes_of(pair)) for pair in pairs],
                statistics,
                [with_columns(projected_f[middle, lanes_of(pair, D)], columns_ref[0, pair]) for pair in pairs],
                [with_columns(projected_f[middle, lanes_of(pair, 2 * D)], columns_ref[1, pair]) for pair in pairs],
                bias_back_ref[...],
            )
            for pair, key_slope, value_slope in zip(pairs, *results):
                right_f[2, 0, own, lanes_of(pair)] = key_slope.astype(BF16)
                right_f[3, 0, own, lanes_of(pair)] = value_slope.astype(BF16)

    other = 3 - core
    twin_pair = start_twin(right_f.at[other, 0], right_f.at[other, 1])
    hidden_slope = dot_t(right_f[0, 0], fine_attend[:, :D])
    hidden_slope += dot_t(right_f[2, 0], fine_attend[:, D : 2 * D])
    hidden_slope += dot_t(right_f[3, 0], fine_attend[:, 2 * D :])
    twin_pair.wait()
    late_sum.put(0, t_dot(left_f[0].reshape(8 * UNIT, D), right_f[2 + core].reshape(8 * UNIT, D)))
    late_sum.first_start()
    coarse_sum.first_finish()
    coarse_sum.second_start()
    early_sum.first_finish()
    early_sum.second_start()
    slope = input_back(right_f[1, 0].astype(F32), hidden_slope, field_f[...], gain_f)
    for row in range(12):
        for half in range(2):
            start = (row // 6 * 2 + half) * UNIT + row % 6 * 8
            strip[row, 6 * half : 6 * half + 6] = slope[start : start + 6]
    for row in range(12):
        token_gradient[0, row] = strip[row, :12].astype(BF16)
    late_sum.first_finish()
    late_sum.second_start()
    coarse_sum.second_finish()
    coarse_sum.third_start()
    early_sum.second_finish()
    early_sum.third_start()
    late_sum.second_finish()
    late_sum.third_start()
    coarse_sum.third_finish()
    coarse_sum.last_start()
    early_sum.third_finish()
    early_sum.last_start()
    late_sum.third_finish()
    late_sum.last_start()
    coarse_sum.last_finish()
    coarse_full[...] = coarse_sum.full[...]
    coarse_gain_out[...] = gain_back(lay, lon, coarse_sum.column(0, 3 * D), coarse_attend, gain_c)
    early_sum.last_finish()
    early_full[...] = early_sum.full[...]
    late_sum.last_finish()
    late_full[...] = late_sum.full[...]
    total = jnp.concatenate([early_sum.column(0, D), late_sum.column(0, 2 * D)], 1)
    fine_gain_out[...] = gain_back(lay, lon, total, fine_attend, gain_f)


def finish(lay, *refs):
    field, gradient, fine_gain, coarse_gain, coarse_full, early_full, late_full = refs[:7]
    (
        field_out, gradient_out, fine_gain_out, fine_attend, fine_output, merge,
        coarse_gain_out, coarse_attend, coarse_output,
    ) = refs[7:]
    field_out[...] = field[...]
    gradient_out[...] = gradient[...]
    fine_gain_out[...] = fine_gain[...]
    coarse_gain_out[...] = coarse_gain[...]

    def column(full, start, width):
        return Reducer(lay, None, None, (None,) * 9 + (full,)).column(start, width)

    for k in range(3):
        fine_attend[:, k * D : (k + 1) * D] = column(late_full, (k - 1) * D, D) if k else column(early_full, 0, D)
        coarse_attend[:, k * D : (k + 1) * D] = column(coarse_full, k * D, D)
    fine_output[...] = column(early_full, D, D)
    coarse_output[...] = column(coarse_full, 3 * D, D)
    for run in range(4):
        merge[run * lay.depth : (run + 1) * lay.depth, :] = column(coarse_full, (4 + run) * D, D)


def reducer_scratch(lay, width):
    y, x, z, low = lay.y, lay.x, lay.z, lay.z_low
    high = z - low
    end = (lay.depth, width)
    shapes = (
        (y, x, z), (x - 1, y, low), (y - 1, x, high), (y, low), (x, high),
        (y - 1, low), (x - 1, high), (z,), (z - 1,), (2, y),
    )
    return [pltpu.VMEM(shape + end, BF16) for shape in shapes]


def per_device(
    lay,
    tokens,
    cotangent,
    fine_gain,
    fine_attend,
    fine_output,
    merge_weight,
    coarse_gain,
    coarse_attend,
    coarse_output,
):
    vmem = pl.BlockSpec(memory_space=pltpu.VMEM)
    hbm = pl.BlockSpec(memory_space=pl.ANY)
    select = merge_matrix()
    constants = (
        jnp.asarray(window_bias()),
        jnp.asarray(window_bias_back()),
        jnp.asarray(head_columns(), BF16),
        jnp.asarray(statistic_columns(), BF16),
        jnp.asarray(select, BF16),
        jnp.asarray(select.T, BF16),
    )
    per_batch = 2 * (lay.x - 1 + lay.y - 1) + lay.z - 1 + 2 * lay.y - 1
    copies = 5 * 8 + 7 + 3 * per_batch
    depth = lay.depth
    fine_shape = jax.ShapeDtypeStruct((2, lay.y, depth, lay.fine_width), BF16)
    between = pl.pallas_call(
        functools.partial(kernel, lay),
        out_shape=(
            jax.ShapeDtypeStruct(cotangent.shape, BF16),
            jax.ShapeDtypeStruct(tokens.shape, BF16),
            jax.ShapeDtypeStruct((1, depth), F32),
            jax.ShapeDtypeStruct((1, depth), F32),
            jax.ShapeDtypeStruct((2, lay.y, depth, lay.coarse_width), BF16),
            fine_shape,
            fine_shape,
        ),
        in_specs=[vmem] * 4 + [hbm] * 11,
        out_specs=[vmem] * 7,
        scratch_shapes=[
            pltpu.VMEM((D, 3 * D), BF16),
            pltpu.VMEM((D, D), BF16),
            pltpu.VMEM((4 * D, D), BF16),
            pltpu.VMEM((D, 3 * D), BF16),
            pltpu.VMEM((D, D), BF16),
            *(pltpu.VMEM(c.shape, c.dtype) for c in constants),
            pltpu.VMEM((12, 16, D), F32),
            pltpu.VMEM((4 * UNIT, D), F32),
            pltpu.VMEM((4, 4, UNIT, D), BF16),
            pltpu.VMEM((16 * UNIT, 3 * D), BF16),
            pltpu.VMEM((4, PAIRS, 2 * UNIT, 9 * UNIT), F32),
            pltpu.VMEM((4 * UNIT, D), F32),
            pltpu.VMEM((4 * UNIT, 128), F32),
            pltpu.VMEM((4, 4, UNIT, D + 128), BF16),
            pltpu.VMEM((2, 2, 4 * UNIT, D), BF16),
            pltpu.VMEM((4, 2, 4 * UNIT, D), BF16),
            pltpu.VMEM((2, 4 * UNIT, D), BF16),
            pltpu.VMEM((UNIT, D), F32),
            pltpu.VMEM((3, 3, UNIT, D), BF16),
            pltpu.VMEM((3, 3, UNIT, D), BF16),
            pltpu.VMEM((9 * UNIT, 3 * D), BF16),
            pltpu.VMEM((9 * UNIT, D), BF16),
            pltpu.VMEM((PAIRS, 2 * UNIT, 9 * UNIT), F32),
            pltpu.VMEM((UNIT, D), F32),
            pltpu.VMEM((UNIT, 128), F32),
            pltpu.VMEM((3, 3, UNIT, 128), BF16),
            pltpu.VMEM((7, 2, UNIT, D), BF16),
            *reducer_scratch(lay, lay.coarse_width),
            *reducer_scratch(lay, lay.fine_width),
            *reducer_scratch(lay, lay.fine_width),
            pltpu.SemaphoreType.DMA((11,)),
            pltpu.SemaphoreType.DMA((copies,)),
            pltpu.SemaphoreType.DMA((copies,)),
        ],
        compiler_params=pltpu.CompilerParams(
            collective_id=0, has_side_effects=True, vmem_limit_bytes=56 * 1024 * 1024
        ),
    )(
        tokens,
        cotangent,
        fine_gain.reshape(1, D),
        coarse_gain.reshape(1, D),
        fine_attend,
        fine_output,
        merge_weight,
        coarse_attend,
        coarse_output,
        *constants,
    )
    outs = pl.pallas_call(
        functools.partial(finish, lay),
        out_shape=(
            jax.ShapeDtypeStruct(cotangent.shape, BF16),
            jax.ShapeDtypeStruct(tokens.shape, BF16),
            jax.ShapeDtypeStruct((1, depth), F32),
            jax.ShapeDtypeStruct((depth, 3 * D), F32),
            jax.ShapeDtypeStruct((depth, D), F32),
            jax.ShapeDtypeStruct((4 * depth, D), F32),
            jax.ShapeDtypeStruct((1, depth), F32),
            jax.ShapeDtypeStruct((depth, 3 * D), F32),
            jax.ShapeDtypeStruct((depth, D), F32),
        ),
        in_specs=[vmem] * 7,
        out_specs=[vmem] * 9,
    )(*between)
    outs = list(outs)
    outs[2] = outs[2].reshape(depth)
    outs[6] = outs[6].reshape(depth)
    return tuple(outs)


def solution(mesh):
    return jax.shard_map(
        functools.partial(per_device, Layout(mesh)),
        mesh=mesh,
        in_specs=(
            P("sec", "lat", "lon", None),
            P("sec", "lat", "lon", None),
            P(),
            P(),
            P(),
            P(),
            P(),
            P(),
            P(),
        ),
        out_specs=(
            P("sec", "lat", "lon", None),
            P("sec", "lat", "lon", None),
            P("lon"),
            P("lon", None),
            P("lon", None),
            P("lon", None),
            P("lon"),
            P("lon", None),
            P("lon", None),
        ),
        check_vma=False,
    )
```

```python
import functools

import jax
import jax.numpy as jnp
import numpy as np
from jax import lax
from jax.experimental import pallas as pl
from jax.experimental.pallas import tpu as pltpu
from jax.sharding import PartitionSpec as P

HEADS = 8
RADIUS = 6
EPSILON = 1e-06
NEGATIVE = -1e30
UNIT = 48
D = 512
PAIRS = 4
MESH = pl.DeviceIdType.MESH
F32 = jnp.float32
BF16 = jnp.bfloat16
AROUND = ((0, 1), (0, -1), (1, 0), (-1, 0), (1, 1), (1, -1), (-1, 1), (-1, -1))


def dot(left, right):
    return jnp.dot(left, right, preferred_element_type=F32)


def dot_t(left, right):
    return lax.dot_general(left, right, (((1,), (1,)), ((), ())), preferred_element_type=F32)


def t_dot(left, right):
    return lax.dot_general(left, right, (((0,), (0,)), ((), ())), preferred_element_type=F32)


def near_window():
    query = np.arange(UNIT)
    row, col = query // 8, query % 8
    key = np.arange(9 * UNIT)
    unit, cell = key // UNIT, key % UNIT
    key_row = unit // 3 * RADIUS + cell // 8
    key_col = unit % 3 * RADIUS + cell % 8
    return (
        (key_row[None] >= row[:, None])
        & (key_row[None] <= row[:, None] + 2 * RADIUS)
        & (key_col[None] >= col[:, None])
        & (key_col[None] <= col[:, None] + 2 * RADIUS)
        & (cell % 8 < RADIUS)[None]
    )


def window_bias():
    bias = np.where(near_window(), 0.0, NEGATIVE).astype(np.float32)
    return np.concatenate([bias, bias], 0)


def window_bias_back():
    used = (np.arange(UNIT) % 8 < RADIUS)[:, None]
    bias = np.where(near_window() & used, 0.0, NEGATIVE).astype(np.float32).T
    return np.concatenate([bias, bias], 1)


def head_columns():
    matrix = np.zeros((D, 128), np.float32)
    for head in range(HEADS):
        matrix[head * 64 : head * 64 + 64, head * 8 : head * 8 + 6] = 1.0
    return matrix


def statistic_columns():
    matrix = np.zeros((2, PAIRS, 2 * UNIT, 128), np.float32)
    for which in range(2):
        for head in range(HEADS):
            pair, side = divmod(head, 2)
            start = head * 8 + 3 * which
            matrix[which, pair, side * UNIT : (side + 1) * UNIT, start : start + 3] = 0.125
    return matrix


def merge_matrix():
    matrix = np.zeros((4 * UNIT, 4 * UNIT), np.float32)
    for a in range(2):
        for b in range(2):
            for i in range(RADIUS):
                for j in range(RADIUS):
                    r, c = 2 * i + a, 2 * j + b
                    place = (r // 6 * 2 + c // 6) * UNIT + r % 6 * 8 + c % 6
                    matrix[(a * 2 + b) * UNIT + i * 8 + j, place] = 1.0
    return matrix


class Layout:
    def __init__(self, mesh):
        self.sec, self.lat, self.lon = (mesh.shape[k] for k in ("sec", "lat", "lon"))
        self.x = 4 if self.lon == 32 else 2
        self.z = self.lon // self.x
        self.y_hi = self.lat // 2
        self.y = self.y_hi * self.sec
        self.blocks = self.lon
        self.depth = D // self.blocks
        self.z_low = self.z // 2
        self.fine_width = 1024 // (2 * self.y)
        self.coarse_width = 4096 // (2 * self.y)


def unit_window(width, starts, ref, column):
    return jnp.concatenate([ref[pl.ds(s, width), pl.ds(column, 128)] for s in starts], 0)


def low_lanes(rows):
    return lax.broadcasted_iota(jnp.int32, (rows, 128), 1) < 64


def stack_heads(part):
    part = part.astype(F32) * 0.125
    low = low_lanes(UNIT)
    return jnp.concatenate([jnp.where(low, part, 0.0), jnp.where(low, 0.0, part)], 0).astype(BF16)


def merge_heads(both):
    return jnp.where(low_lanes(UNIT), both[:UNIT], both[UNIT:])


def attend(queries, keys, values, bias):
    scores = [dot_t(q, k) + bias for q, k in zip(queries, keys)]
    peaks = [jnp.max(s, axis=-1, keepdims=True) for s in scores]
    expos = [jnp.exp(s - m) for s, m in zip(scores, peaks)]
    totals = [jnp.sum(e, axis=-1, keepdims=True) for e in expos]
    attentions = [e * (1.0 / t) for e, t in zip(expos, totals)]
    mixed = [merge_heads(dot(a.astype(BF16), v)) for a, v in zip(attentions, values)]
    return attentions, mixed, [m + jnp.log(t) for m, t in zip(peaks, totals)]


def query_back(keys, values, attentions, slopes):
    probs = [dot_t(s, v) for s, v in zip(slopes, values)]
    means = [jnp.sum(a * p, axis=-1, keepdims=True) for a, p in zip(attentions, probs)]
    scores = [(a * (p - m)).astype(BF16) for a, p, m in zip(attentions, probs, means)]
    return [merge_heads(dot(s, k)) for s, k in zip(scores, keys)]


def pair_back(queries, slopes, statistics, keys, values, bias):
    scores = [dot_t(jnp.concatenate([q, statistics], 1), k) + bias for q, k in zip(queries, keys)]
    probs = [dot_t(jnp.concatenate([s, statistics], 1), v) for s, v in zip(slopes, values)]
    attentions = [jnp.exp(s) for s in scores]
    scores = [(a * p).astype(BF16) for a, p in zip(attentions, probs)]
    return (
        [merge_heads(t_dot(s, q)) for s, q in zip(scores, queries)],
        [merge_heads(t_dot(a.astype(BF16), s)) for a, s in zip(attentions, slopes)],
    )


def put_head_columns(total, pair, column):
    head = lax.broadcasted_iota(jnp.int32, total.shape, 1) // 8
    total = jnp.where(head == 2 * pair, column[:UNIT], total)
    return jnp.where(head == 2 * pair + 1, column[UNIT:], total)


def statistics_of(lse, slope, mixed, heads):
    product = slope.astype(F32) * mixed
    high = product.astype(BF16)
    low = (product - high.astype(F32)).astype(BF16)
    mean = dot(high, heads) + dot(low, heads)
    lane = lax.broadcasted_iota(jnp.int32, lse.shape, 1)
    part = lane % 8
    value = jnp.where(part < 3, lse * -8.0, -mean)
    first = value.astype(BF16)
    rest = value - first.astype(F32)
    second = rest.astype(BF16)
    third = rest - second.astype(F32)
    value = jnp.where(part % 3 == 0, first.astype(F32), jnp.where(part % 3 == 1, second.astype(F32), third))
    return jnp.where((part < 6) & (lane < 64), value, 0.0).astype(BF16)


def norm(field, gain):
    factor = lax.rsqrt(jnp.mean(field * field, axis=-1, keepdims=True) + EPSILON)
    normed = field * factor
    return factor, normed, (normed * gain).astype(BF16)


def input_back(slope, hidden_slope, field, gain):
    factor = lax.rsqrt(jnp.mean(field * field, axis=-1, keepdims=True) + EPSILON)
    normed = field * factor
    scaled = hidden_slope * gain
    return slope + factor * (scaled - normed * jnp.mean(scaled * normed, axis=-1, keepdims=True))


class Reducer:
    def __init__(self, lay, place, wires, refs):
        self.lay, self.place, self.wires = lay, place, wires
        (
            self.given, self.in_1a, self.in_1b, self.sum_2a, self.sum_2b,
            self.in_2a, self.in_2b, self.sum_3, self.in_3, self.full,
        ) = refs
        self.copies = []

    def device(self, core=None, y=None, x=None, z=None):
        here = self.place
        core = here["core"] if core is None else core
        y = here["y"] if y is None else y
        x = here["x"] if x is None else x
        z = here["z"] if z is None else z
        return (y % self.lay.sec, y // self.lay.sec * 2 + core, x * self.lay.z + z)

    def send(self, source, target, device):
        copy = self.wires(source, target, device)
        copy.start()
        self.copies.append(copy)

    def arrive(self):
        for copy in self.copies:
            copy.wait()
        self.copies = []

    def first_start(self):
        lay, here = self.lay, self.place
        low = pl.ds(0, lay.z_low)
        high = pl.ds(lay.z_low, lay.z - lay.z_low)
        for step in range(1, lay.x):
            x = (here["x"] + step) % lay.x
            self.send(self.given.at[:, x, low], self.in_1a.at[step - 1], self.device(x=x))
        for step in range(1, lay.y):
            y = (here["y"] + step) % lay.y
            self.send(self.given.at[y, :, high], self.in_1b.at[step - 1], self.device(y=y))

    def first_finish(self):
        self.arrive()
        lay, here = self.lay, self.place
        low = pl.ds(0, lay.z_low)
        high = pl.ds(lay.z_low, lay.z - lay.z_low)

        @pl.loop(0, lay.y)
        def _(y):
            total = self.given[y, here["x"], low].astype(F32)
            for k in range(lay.x - 1):
                total += self.in_1a[k, y].astype(F32)
            self.sum_2a[y] = total.astype(BF16)

        @pl.loop(0, lay.x)
        def _(x):
            total = self.given[here["y"], x, high].astype(F32)
            for k in range(lay.y - 1):
                total += self.in_1b[k, x].astype(F32)
            self.sum_2b[x] = total.astype(BF16)

    def second_start(self):
        lay, here = self.lay, self.place
        for step in range(1, lay.y):
            y = (here["y"] + step) % lay.y
            self.send(self.sum_2a.at[y], self.in_2a.at[step - 1], self.device(y=y))
        for step in range(1, lay.x):
            x = (here["x"] + step) % lay.x
            self.send(self.sum_2b.at[x], self.in_2b.at[step - 1], self.device(x=x))

    def second_finish(self):
        self.arrive()
        lay, here = self.lay, self.place
        total = self.sum_2a[here["y"]].astype(F32)
        for k in range(lay.y - 1):
            total += self.in_2a[k].astype(F32)
        self.sum_3[pl.ds(0, lay.z_low)] = total.astype(BF16)
        total = self.sum_2b[here["x"]].astype(F32)
        for k in range(lay.x - 1):
            total += self.in_2b[k].astype(F32)
        self.sum_3[pl.ds(lay.z_low, lay.z - lay.z_low)] = total.astype(BF16)

    def third_start(self):
        lay, here = self.lay, self.place
        for step in range(1, lay.z):
            z = (here["z"] + step) % lay.z
            self.send(self.sum_3.at[z], self.in_3.at[step - 1], self.device(z=z))

    def third_finish(self):
        self.arrive()
        lay, here = self.lay, self.place
        total = self.sum_3[here["z"]].astype(F32)
        for k in range(lay.z - 1):
            total += self.in_3[k].astype(F32)
        self.full[here["core"], here["y"]] = total.astype(BF16)

    def last_start(self):
        lay, here = self.lay, self.place
        own = self.full.at[here["core"], here["y"]]
        for across in range(2):
            for step in range(lay.y):
                if across or step:
                    core = (here["core"] + across) % 2
                    y = (here["y"] + step) % lay.y
                    self.send(own, own, self.device(core=core, y=y))

    def last_finish(self):
        self.arrive()

    def column(self, start, width):
        size = self.full.shape[-1]
        parts = []
        while width > 0:
            group, offset = divmod(start, size)
            take = min(width, size - offset)
            parts.append(self.full[group // self.lay.y, group % self.lay.y, :, offset : offset + take])
            start, width = start + take, width - take
        return (parts[0] if len(parts) == 1 else jnp.concatenate(parts, 1)).astype(F32)

    def put(self, start, product):
        lay = self.lay
        size = self.given.shape[-1]
        done, width = 0, product.shape[1]
        while done < width:
            group, offset = divmod(start + done, size)
            take = min(width - done, size - offset)
            piece = product[:, done : done + take].astype(BF16)
            self.given[group, :, :, :, offset : offset + take] = piece.reshape(lay.x, lay.z, lay.depth, take)
            done += take

    def put_merged(self, part, product):
        lay = self.lay
        size = self.given.shape[-1]
        count = lay.blocks // 4
        shaped = product.astype(BF16).reshape(count, 4, lay.depth, D)
        for run in range(4):
            group, offset = divmod(run * D, size)
            for block in range(count):
                x, z = divmod(part * count + block, lay.z)
                self.given[group, x, z, :, offset : offset + D] = shaped[block, run]


class DeepReducer(Reducer):
    def __init__(self, lay, place, wires, refs):
        self.lay, self.place, self.wires = lay, place, wires
        self.given, self.in_1, self.sum_2, self.in_2, self.sum_3, self.in_3, self.full = refs
        self.copies = []

    def first_start(self):
        lay, here = self.lay, self.place
        for step in range(1, lay.z):
            z = (here["z"] + step) % lay.z
            self.send(self.given.at[:, :, z], self.in_1.at[step - 1], self.device(z=z))

    def first_finish(self):
        self.arrive()
        lay, here = self.lay, self.place

        @pl.loop(0, lay.y)
        def _(y):
            total = self.given[y, :, here["z"]].astype(F32)
            for k in range(lay.z - 1):
                total += self.in_1[k, y].astype(F32)
            self.sum_2[y] = total.astype(BF16)

    def second_start(self):
        lay, here = self.lay, self.place
        for step in range(1, lay.x):
            x = (here["x"] + step) % lay.x
            self.send(self.sum_2.at[:, x], self.in_2.at[step - 1], self.device(x=x))

    def second_finish(self):
        self.arrive()
        total = self.sum_2[:, self.place["x"]].astype(F32)
        for k in range(self.lay.x - 1):
            total += self.in_2[k].astype(F32)
        self.sum_3[...] = total.astype(BF16)

    def third_start(self):
        lay, here = self.lay, self.place
        for step in range(1, lay.y):
            y = (here["y"] + step) % lay.y
            self.send(self.sum_3.at[y], self.in_3.at[step - 1], self.device(y=y))

    def third_finish(self):
        self.arrive()
        here = self.place
        total = self.sum_3[here["y"]].astype(F32)
        for k in range(self.lay.y - 1):
            total += self.in_3[k].astype(F32)
        self.full[here["core"], here["y"]] = total.astype(BF16)


GROUPS = ((0, 1, 2, 3),)


def lanes_of(pair, start=0):
    return slice(start + pair * 128, start + pair * 128 + 128)


def with_columns(part, columns):
    return jnp.concatenate([stack_heads(part), columns], 1)


def gain_back(lay, lon, total, weight, gain):
    own = weight[pl.ds(pl.multiple_of(lon * lay.depth, lay.depth), lay.depth), :].astype(F32)
    column = jnp.sum(total * own, axis=1, keepdims=True)
    row = lax.broadcasted_iota(jnp.int32, (lay.depth, D), 0) + lon * lay.depth
    at = lax.broadcasted_iota(jnp.int32, (lay.depth, D), 1) == row
    column = column / jnp.sum(jnp.where(at, gain, 0.0), axis=1, keepdims=True)
    square = (lay.depth, lay.depth)
    same = lax.broadcasted_iota(jnp.int32, square, 0) == lax.broadcasted_iota(jnp.int32, square, 1)
    return jnp.sum(jnp.where(same, column, 0.0), axis=0, keepdims=True)


def kernel(
    lay,
    tokens, cotangent, fine_gain, coarse_gain,
    fine_attend_hbm, fine_output_hbm, merge_hbm, coarse_attend_hbm, coarse_output_hbm,
    bias_hbm, bias_back_hbm, heads_hbm, columns_hbm, merge_ref_hbm, split_hbm,
    coarse_field, token_gradient, fine_gain_out, coarse_gain_out, coarse_full, early_full, late_full,
    fine_attend, fine_output, merge_weight, coarse_attend, coarse_output,
    bias_ref, bias_back_ref, heads_ref, columns_ref, merge_ref, split_ref,
    strip, field_f, wide_f, projected_f, attention_f, exact_f, lse_f, slope_wide_f, left_f, right_f, merged,
    field_c, wide_c, slope_wide_c, projected_c, mixed_slope_c, attention_c, exact_c, lse_c, statistics_c, factors_c,
    *rest,
):
    load_sem, send_sem, recv_sem = rest[27:]
    sec, lat, lon = (lax.axis_index(k) for k in ("sec", "lat", "lon"))
    core = lat % 2
    place = {"core": core, "y": lat // 2 * lay.sec + sec, "x": lon // lay.z, "z": lon % lay.z}
    used = [0]

    def wires(source, target, device):
        index = used[0]
        used[0] += 1
        return pltpu.make_async_remote_copy(
            src_ref=source,
            dst_ref=target,
            send_sem=send_sem.at[index],
            recv_sem=recv_sem.at[index],
            device_id=device,
            device_id_type=MESH,
        )

    def neighbour(step):
        return (sec, (lat + step[0] + lay.lat) % lay.lat, (lon + step[1] + lay.lon) % lay.lon)

    def start_rims(source, target):
        copies = []
        for step in AROUND:
            copy = wires(source(step), target(step), neighbour(step))
            if step[0]:
                last = lay.lat - 1
                sends = lat != (last if step[0] > 0 else 0)
                takes = lat != (0 if step[0] > 0 else last)
                pl.when(sends)(copy.start)
                copies.append((copy, sends, takes))
            else:
                copy.start()
                copies.append((copy, None, None))
        return copies

    def wait_rims(copies):
        for copy, sends, takes in copies:
            if sends is None:
                copy.wait()
            else:
                pl.when(sends)(copy.wait_send)
                pl.when(takes)(copy.wait_recv)

    def start_twin(source, target):
        copy = wires(source, target, coarse_sum.device(core=1 - core))
        copy.start()
        return copy

    coarse_sum = Reducer(lay, place, wires, rest[:10])
    early_sum = DeepReducer(lay, place, wires, rest[10:17])
    late_sum = Reducer(lay, place, wires, rest[17:27])

    barrier = pltpu.get_barrier_semaphore()
    peers = [neighbour(step) for step in AROUND]
    peers += [coarse_sum.device(x=(place["x"] + s) % lay.x) for s in range(1, lay.x)]
    peers += [coarse_sum.device(z=(place["z"] + s) % lay.z) for s in range(1, lay.z)]
    peers += [
        coarse_sum.device(core=(core + c) % 2, y=(place["y"] + s) % lay.y)
        for c in range(2)
        for s in range(lay.y)
        if c or s
    ]
    for peer in peers:
        pl.semaphore_signal(barrier, inc=1, device_id=peer, device_id_type=MESH)

    loads = {
        name: pltpu.make_async_copy(source, target, load_sem.at[i])
        for i, (name, source, target) in enumerate(
            (
                ("fine_attend", fine_attend_hbm, fine_attend),
                ("bias_ref", bias_hbm, bias_ref),
                ("fine_output", fine_output_hbm, fine_output),
                ("merge_ref", merge_ref_hbm, merge_ref),
                ("merge_weight", merge_hbm, merge_weight),
                ("coarse_output", coarse_output_hbm, coarse_output),
                ("coarse_attend", coarse_attend_hbm, coarse_attend),
                ("heads_ref", heads_hbm, heads_ref),
                ("columns_ref", columns_hbm, columns_ref),
                ("bias_back_ref", bias_back_hbm, bias_back_ref),
                ("split_ref", split_hbm, split_ref),
            )
        )
    }
    for load in loads.values():
        load.start()

    field_f[...] = jnp.zeros_like(field_f)
    field_c[...] = jnp.zeros_like(field_c)
    for row in range(12):
        strip[row, :12] = tokens[0, row].astype(F32)
    for row in range(12):
        for half in range(2):
            start = (row // 6 * 2 + half) * UNIT + row % 6 * 8
            field_f[start : start + 6] = strip[row, 6 * half : 6 * half + 6]
    for unit in range(4):
        wide_f[1 + unit // 2, 1 + unit % 2] = field_f[unit * UNIT : (unit + 1) * UNIT].astype(BF16)
    for row in range(6):
        field_c[row * 8 : row * 8 + 6] = cotangent[0, row].astype(F32)
    slope_wide_c[1, 1] = field_c[...].astype(BF16)
    factors_c[5, 0] = field_c[...].astype(BF16)

    pl.semaphore_wait(barrier, len(peers))

    def part(step, mine):
        index = []
        for way in step:
            if way == 0:
                index.append(pl.ds(1, 2))
            elif way > 0:
                index.append(2 if mine else 3)
            else:
                index.append(1 if mine else 0)
        return tuple(index)

    def opposite(step):
        return (-step[0], -step[1])

    def fine_rims(ref):
        return start_rims(lambda step: ref.at[part(step, True)], lambda step: ref.at[part(opposite(step), False)])

    def coarse_rims(ref):
        return start_rims(lambda step: ref.at[1, 1], lambda step: ref.at[1 - step[0], 1 - step[1]])

    rims = fine_rims(wide_f)

    def clear(row):
        for ref in (wide_f, slope_wide_f, wide_c, slope_wide_c, statistics_c):
            ref[row if row == 0 else ref.shape[0] - 1] = jnp.zeros(ref.shape[1:], ref.dtype)

    pl.when(lat == 0)(lambda: clear(0))
    pl.when(lat == lay.lat - 1)(lambda: clear(-1))

    top = jnp.where(lat == 0, NEGATIVE, 0.0)
    bottom = jnp.where(lat == lay.lat - 1, NEGATIVE, 0.0)
    lanes = lax.broadcasted_iota(jnp.int32, (1, 9 * UNIT), 1)

    def bias_at(is_first, is_last):
        above = jnp.where(is_first, top, 0.0)
        below = jnp.where(is_last, bottom, 0.0)
        rim = jnp.where(lanes < 3 * UNIT, above, 0.0) + jnp.where(lanes >= 6 * UNIT, below, 0.0)
        return bias_ref[...] + rim

    gain_f = fine_gain[...]
    gain_c = coarse_gain[...]
    loads["fine_attend"].wait()
    for run in range(2):
        hidden = norm(field_f[run * 96 : run * 96 + 96], gain_f)[2]
        left_f[0, 0, run * 96 : run * 96 + 96] = hidden
        projected_f[240 + run * 192 : 336 + run * 192, :] = dot(hidden, fine_attend[...]).astype(BF16)
    twin_hidden = start_twin(left_f.at[0, 0], left_f.at[0, 1])
    wait_rims(rims)
    slope_rims = coarse_rims(slope_wide_c)
    for start, units in (
        (0, (wide_f[0].reshape(4 * UNIT, D), wide_f[1, 0])),
        (336, (wide_f[1, 3], wide_f[2, 0])),
        (528, (wide_f[2, 3], wide_f[3].reshape(4 * UNIT, D))),
    ):
        field = jnp.concatenate([unit.astype(F32) for unit in units], 0)
        hidden = norm(field, gain_f)[2]
        projected_f[start : start + field.shape[0], :] = dot(hidden, fine_attend[...]).astype(BF16)

    loads["bias_ref"].wait()

    def starts_of(quad):
        first, second = quad // 2, quad % 2
        return [pl.multiple_of(((first + i) * 4 + second) * UNIT, UNIT) for i in range(3)]

    def middle_of(quad):
        return pl.ds(pl.multiple_of(((1 + quad // 2) * 4 + 1 + quad % 2) * UNIT, UNIT), UNIT)

    def own_of(quad):
        return pl.ds(pl.multiple_of(quad * UNIT, UNIT), UNIT)

    @pl.loop(0, 4)
    def _(quad):
        first = quad // 2
        own, middle, starts = own_of(quad), middle_of(quad), starts_of(quad)
        bias = bias_at(first == 0, first == 1)
        lse = jnp.zeros((UNIT, 128), F32)
        for pairs in GROUPS:
            results = attend(
                [stack_heads(projected_f[middle, lanes_of(pair)]) for pair in pairs],
                [unit_window(3 * UNIT, starts, projected_f, D + pair * 128) for pair in pairs],
                [unit_window(3 * UNIT, starts, projected_f, 2 * D + pair * 128) for pair in pairs],
                bias,
            )
            for pair, attention, mixed, column in zip(pairs, *results):
                attention_f[quad, pair] = attention
                exact_f[own, lanes_of(pair)] = mixed
                left_f[1, 0, own, lanes_of(pair)] = mixed.astype(BF16)
                lse = put_head_columns(lse, pair, column)
        lse_f[own, :] = lse

    twin_mixed = start_twin(left_f.at[1, 0], left_f.at[1, 1])
    loads["fine_output"].wait()
    loads["merge_ref"].wait()
    fine_field = (field_f[...] + dot(left_f[1, 0], fine_output[...])).astype(BF16)
    merged[0] = dot(merge_ref[...], fine_field).astype(BF16)
    loads["merge_weight"].wait()
    coarse_in = jnp.zeros((UNIT, D), F32)
    for quarter in range(4):
        rows = slice(quarter * UNIT, (quarter + 1) * UNIT)
        coarse_in += dot(merged[0, rows], merge_weight[quarter * D : (quarter + 1) * D])
    wide_c[1, 1] = coarse_in.astype(BF16)
    rims = coarse_rims(wide_c)
    twin_merged = start_twin(merged.at[0], merged.at[1])

    for name in ("coarse_output", "coarse_attend", "heads_ref", "columns_ref", "bias_back_ref", "split_ref"):
        loads[name].wait()
    field_c[...] = wide_c[1, 1].astype(F32)
    factors_c[0, 0] = norm(field_c[...], gain_c)[2]
    wait_rims(slope_rims)
    mixed_slope_c[...] = dot_t(slope_wide_c[...].reshape(9 * UNIT, D), coarse_output[...]).astype(BF16)
    wait_rims(rims)
    hidden = norm(wide_c[...].reshape(9 * UNIT, D).astype(F32), gain_c)[2]
    projected_c[...] = dot(hidden, coarse_attend[...]).astype(BF16)
    bias = bias_at(True, True)
    middle = slice(4 * UNIT, 5 * UNIT)
    lse = jnp.zeros((UNIT, 128), F32)
    for pairs in GROUPS:
        results = attend(
            [stack_heads(projected_c[middle, lanes_of(pair)]) for pair in pairs],
            [projected_c[:, lanes_of(pair, D)] for pair in pairs],
            [projected_c[:, lanes_of(pair, 2 * D)] for pair in pairs],
            bias,
        )
        for pair, attention, mixed, column in zip(pairs, *results):
            attention_c[pair] = attention
            exact_c[:, lanes_of(pair)] = mixed
            lse = put_head_columns(lse, pair, column)
    statistics_c[1, 1] = statistics_of(lse, mixed_slope_c[middle, :], exact_c[...], heads_ref[...])
    rims = coarse_rims(statistics_c)
    factors_c[4, 0] = exact_c[...].astype(BF16)
    moved = field_c[...] + dot(factors_c[4, 0], coarse_output[...])
    for row in range(6):
        coarse_field[0, row] = moved[row * 8 : row * 8 + 6].astype(BF16)
    for pairs in GROUPS:
        results = query_back(
            [projected_c[:, lanes_of(pair, D)] for pair in pairs],
            [projected_c[:, lanes_of(pair, 2 * D)] for pair in pairs],
            [attention_c[pair] for pair in pairs],
            [stack_heads(mixed_slope_c[middle, lanes_of(pair)]) for pair in pairs],
        )
        for pair, query_slope in zip(pairs, results):
            factors_c[1, 0, :, lanes_of(pair)] = query_slope.astype(BF16)
    wait_rims(rims)
    statistics = statistics_c[...].reshape(9 * UNIT, 128)
    for pairs in GROUPS:
        results = pair_back(
            [projected_c[:, lanes_of(pair)] for pair in pairs],
            [mixed_slope_c[:, lanes_of(pair)] for pair in pairs],
            statistics,
            [with_columns(projected_c[middle, lanes_of(pair, D)], columns_ref[0, pair]) for pair in pairs],
            [with_columns(projected_c[middle, lanes_of(pair, 2 * D)], columns_ref[1, pair]) for pair in pairs],
            bias_back_ref[...],
        )
        for pair, key_slope, value_slope in zip(pairs, *results):
            factors_c[2, 0, :, lanes_of(pair)] = key_slope.astype(BF16)
            factors_c[3, 0, :, lanes_of(pair)] = value_slope.astype(BF16)
    hidden_slope = sum(
        dot_t(factors_c[1 + k, 0], coarse_attend[:, k * D : (k + 1) * D]) for k in range(3)
    )
    slope = factors_c[5, 0].astype(F32)
    coarse_slope = input_back(slope, hidden_slope, field_c[...], gain_c).astype(BF16)
    factors_c[6, 0] = coarse_slope
    twin_factors = start_twin(factors_c.at[:, 0], factors_c.at[:, 1])

    merged_slope = jnp.concatenate(
        [dot_t(coarse_slope, merge_weight[k * D : (k + 1) * D]).astype(BF16) for k in range(4)], 0
    )
    slope_f = dot(split_ref[...], merged_slope).astype(BF16)
    right_f[1, 0] = slope_f
    mixed_slope = dot_t(slope_f, fine_output[...]).astype(BF16)
    statistics = statistics_of(lse_f[...], mixed_slope, exact_f[...], heads_ref[...])
    for unit in range(4):
        rows = slice(unit * UNIT, (unit + 1) * UNIT)
        slope_wide_f[1 + unit // 2, 1 + unit % 2, :, :D] = mixed_slope[rows]
        slope_wide_f[1 + unit // 2, 1 + unit % 2, :, D:] = statistics[rows]
    rims = fine_rims(slope_wide_f)
    twin_slope = start_twin(right_f.at[1, 0], right_f.at[1, 1])

    @pl.loop(0, 4)
    def _(quad):
        own, starts = own_of(quad), starts_of(quad)
        for pairs in GROUPS:
            results = query_back(
                [unit_window(3 * UNIT, starts, projected_f, D + pair * 128) for pair in pairs],
                [unit_window(3 * UNIT, starts, projected_f, 2 * D + pair * 128) for pair in pairs],
                [attention_f[quad, pair] for pair in pairs],
                [stack_heads(slope_wide_f[1 + quad // 2, 1 + quad % 2, :, lanes_of(pair)]) for pair in pairs],
            )
            for pair, query_slope in zip(pairs, results):
                right_f[0, 0, own, lanes_of(pair)] = query_slope.astype(BF16)

    twin_query = start_twin(right_f.at[0, 0], right_f.at[0, 1])
    twin_factors.wait()
    twin_merged.wait()

    def both(index):
        return factors_c[index].reshape(2 * UNIT, D)

    @pl.when(core == 0)
    def _():
        for k in range(3):
            coarse_sum.put(k * D, t_dot(both(0), both(1 + k)))
        coarse_sum.put(3 * D, t_dot(both(4), both(5)))

    @pl.when(core == 1)
    def _():
        for k in range(4):
            rows = slice(k * UNIT, (k + 1) * UNIT)
            coarse_sum.put_merged(k, t_dot(merged[:, rows].reshape(2 * UNIT, D), both(6)))

    coarse_sum.first_start()
    twin_hidden.wait()
    twin_mixed.wait()
    twin_slope.wait()
    twin_query.wait()
    early_sum.put(0, t_dot(left_f[core].reshape(8 * UNIT, D), right_f[core].reshape(8 * UNIT, D)))
    wait_rims(rims)
    early_sum.first_start()

    @pl.loop(0, 4)
    def _(quad):
        own, middle, starts = own_of(quad), middle_of(quad), starts_of(quad)
        first, second = quad // 2, quad % 2

        def around(lanes):
            rows = [slope_wide_f[first + i, pl.ds(second, 3), :, lanes] for i in range(3)]
            return jnp.concatenate([r.reshape(3 * UNIT, 128) for r in rows], 0)

        statistics = around(slice(D, D + 128))
        for pairs in GROUPS:
            results = pair_back(
                [unit_window(3 * UNIT, starts, projected_f, pair * 128) for pair in pairs],
                [around(lanes_of(pair)) for pair in pairs],
                statistics,
                [with_columns(projected_f[middle, lanes_of(pair, D)], columns_ref[0, pair]) for pair in pairs],
                [with_columns(projected_f[middle, lanes_of(pair, 2 * D)], columns_ref[1, pair]) for pair in pairs],
                bias_back_ref[...],
            )
            for pair, key_slope, value_slope in zip(pairs, *results):
                right_f[2, 0, own, lanes_of(pair)] = key_slope.astype(BF16)
                right_f[3, 0, own, lanes_of(pair)] = value_slope.astype(BF16)

    other = 3 - core
    twin_pair = start_twin(right_f.at[other, 0], right_f.at[other, 1])
    hidden_slope = dot_t(right_f[0, 0], fine_attend[:, :D])
    hidden_slope += dot_t(right_f[2, 0], fine_attend[:, D : 2 * D])
    hidden_slope += dot_t(right_f[3, 0], fine_attend[:, 2 * D :])
    twin_pair.wait()
    late_sum.put(0, t_dot(left_f[0].reshape(8 * UNIT, D), right_f[2 + core].reshape(8 * UNIT, D)))
    late_sum.first_start()
    coarse_sum.first_finish()
    coarse_sum.second_start()
    early_sum.first_finish()
    early_sum.second_start()
    slope = input_back(right_f[1, 0].astype(F32), hidden_slope, field_f[...], gain_f)
    for row in range(12):
        for half in range(2):
            start = (row // 6 * 2 + half) * UNIT + row % 6 * 8
            strip[row, 6 * half : 6 * half + 6] = slope[start : start + 6]
    for row in range(12):
        token_gradient[0, row] = strip[row, :12].astype(BF16)
    late_sum.first_finish()
    late_sum.second_start()
    coarse_sum.second_finish()
    coarse_sum.third_start()
    early_sum.second_finish()
    early_sum.third_start()
    late_sum.second_finish()
    late_sum.third_start()
    coarse_sum.third_finish()
    coarse_sum.last_start()
    early_sum.third_finish()
    early_sum.last_start()
    late_sum.third_finish()
    late_sum.last_start()
    coarse_sum.last_finish()
    coarse_full[...] = coarse_sum.full[...]
    coarse_gain_out[...] = gain_back(lay, lon, coarse_sum.column(0, 3 * D), coarse_attend, gain_c)
    early_sum.last_finish()
    early_full[...] = early_sum.full[...]
    late_sum.last_finish()
    late_full[...] = late_sum.full[...]
    total = jnp.concatenate([early_sum.column(0, D), late_sum.column(0, 2 * D)], 1)
    fine_gain_out[...] = gain_back(lay, lon, total, fine_attend, gain_f)


def finish(lay, *refs):
    field, gradient, fine_gain, coarse_gain, coarse_full, early_full, late_full = refs[:7]
    (
        field_out, gradient_out, fine_gain_out, fine_attend, fine_output, merge,
        coarse_gain_out, coarse_attend, coarse_output,
    ) = refs[7:]
    field_out[...] = field[...]
    gradient_out[...] = gradient[...]
    fine_gain_out[...] = fine_gain[...]
    coarse_gain_out[...] = coarse_gain[...]

    def column(full, start, width):
        return Reducer(lay, None, None, (None,) * 9 + (full,)).column(start, width)

    for k in range(3):
        fine_attend[:, k * D : (k + 1) * D] = column(late_full, (k - 1) * D, D) if k else column(early_full, 0, D)
        coarse_attend[:, k * D : (k + 1) * D] = column(coarse_full, k * D, D)
    fine_output[...] = column(early_full, D, D)
    coarse_output[...] = column(coarse_full, 3 * D, D)
    for run in range(4):
        merge[run * lay.depth : (run + 1) * lay.depth, :] = column(coarse_full, (4 + run) * D, D)


def reducer_scratch(lay, width):
    y, x, z, low = lay.y, lay.x, lay.z, lay.z_low
    high = z - low
    end = (lay.depth, width)
    shapes = (
        (y, x, z), (x - 1, y, low), (y - 1, x, high), (y, low), (x, high),
        (y - 1, low), (x - 1, high), (z,), (z - 1,), (2, y),
    )
    return [pltpu.VMEM(shape + end, BF16) for shape in shapes]


def deep_scratch(lay, width):
    y, x, z = lay.y, lay.x, lay.z
    end = (lay.depth, width)
    shapes = ((y, x, z), (z - 1, y, x), (y, x), (x - 1, y), (y,), (y - 1,), (2, y))
    return [pltpu.VMEM(shape + end, BF16) for shape in shapes]


def per_device(
    lay,
    tokens,
    cotangent,
    fine_gain,
    fine_attend,
    fine_output,
    merge_weight,
    coarse_gain,
    coarse_attend,
    coarse_output,
):
    vmem = pl.BlockSpec(memory_space=pltpu.VMEM)
    hbm = pl.BlockSpec(memory_space=pl.ANY)
    select = merge_matrix()
    constants = (
        jnp.asarray(window_bias()),
        jnp.asarray(window_bias_back()),
        jnp.asarray(head_columns(), BF16),
        jnp.asarray(statistic_columns(), BF16),
        jnp.asarray(select, BF16),
        jnp.asarray(select.T, BF16),
    )
    per_batch = 2 * (lay.x - 1 + lay.y - 1) + lay.z - 1 + 2 * lay.y - 1
    deep_batch = lay.z - 1 + lay.x - 1 + lay.y - 1 + 2 * lay.y - 1
    copies = 5 * 8 + 7 + 2 * per_batch + deep_batch
    depth = lay.depth
    fine_shape = jax.ShapeDtypeStruct((2, lay.y, depth, lay.fine_width), BF16)
    between = pl.pallas_call(
        functools.partial(kernel, lay),
        out_shape=(
            jax.ShapeDtypeStruct(cotangent.shape, BF16),
            jax.ShapeDtypeStruct(tokens.shape, BF16),
            jax.ShapeDtypeStruct((1, depth), F32),
            jax.ShapeDtypeStruct((1, depth), F32),
            jax.ShapeDtypeStruct((2, lay.y, depth, lay.coarse_width), BF16),
            fine_shape,
            fine_shape,
        ),
        in_specs=[vmem] * 4 + [hbm] * 11,
        out_specs=[vmem] * 7,
        scratch_shapes=[
            pltpu.VMEM((D, 3 * D), BF16),
            pltpu.VMEM((D, D), BF16),
            pltpu.VMEM((4 * D, D), BF16),
            pltpu.VMEM((D, 3 * D), BF16),
            pltpu.VMEM((D, D), BF16),
            *(pltpu.VMEM(c.shape, c.dtype) for c in constants),
            pltpu.VMEM((12, 16, D), F32),
            pltpu.VMEM((4 * UNIT, D), F32),
            pltpu.VMEM((4, 4, UNIT, D), BF16),
            pltpu.VMEM((16 * UNIT, 3 * D), BF16),
            pltpu.VMEM((4, PAIRS, 2 * UNIT, 9 * UNIT), F32),
            pltpu.VMEM((4 * UNIT, D), F32),
            pltpu.VMEM((4 * UNIT, 128), F32),
            pltpu.VMEM((4, 4, UNIT, D + 128), BF16),
            pltpu.VMEM((2, 2, 4 * UNIT, D), BF16),
            pltpu.VMEM((4, 2, 4 * UNIT, D), BF16),
            pltpu.VMEM((2, 4 * UNIT, D), BF16),
            pltpu.VMEM((UNIT, D), F32),
            pltpu.VMEM((3, 3, UNIT, D), BF16),
            pltpu.VMEM((3, 3, UNIT, D), BF16),
            pltpu.VMEM((9 * UNIT, 3 * D), BF16),
            pltpu.VMEM((9 * UNIT, D), BF16),
            pltpu.VMEM((PAIRS, 2 * UNIT, 9 * UNIT), F32),
            pltpu.VMEM((UNIT, D), F32),
            pltpu.VMEM((UNIT, 128), F32),
            pltpu.VMEM((3, 3, UNIT, 128), BF16),
            pltpu.VMEM((7, 2, UNIT, D), BF16),
            *reducer_scratch(lay, lay.coarse_width),
            *deep_scratch(lay, lay.fine_width),
            *reducer_scratch(lay, lay.fine_width),
            pltpu.SemaphoreType.DMA((11,)),
            pltpu.SemaphoreType.DMA((copies,)),
            pltpu.SemaphoreType.DMA((copies,)),
        ],
        compiler_params=pltpu.CompilerParams(
            collective_id=0, has_side_effects=True, vmem_limit_bytes=56 * 1024 * 1024
        ),
    )(
        tokens,
        cotangent,
        fine_gain.reshape(1, D),
        coarse_gain.reshape(1, D),
        fine_attend,
        fine_output,
        merge_weight,
        coarse_attend,
        coarse_output,
        *constants,
    )
    outs = pl.pallas_call(
        functools.partial(finish, lay),
        out_shape=(
            jax.ShapeDtypeStruct(cotangent.shape, BF16),
            jax.ShapeDtypeStruct(tokens.shape, BF16),
            jax.ShapeDtypeStruct((1, depth), F32),
            jax.ShapeDtypeStruct((depth, 3 * D), F32),
            jax.ShapeDtypeStruct((depth, D), F32),
            jax.ShapeDtypeStruct((4 * depth, D), F32),
            jax.ShapeDtypeStruct((1, depth), F32),
            jax.ShapeDtypeStruct((depth, 3 * D), F32),
            jax.ShapeDtypeStruct((depth, D), F32),
        ),
        in_specs=[vmem] * 7,
        out_specs=[vmem] * 9,
    )(*between)
    outs = list(outs)
    outs[2] = outs[2].reshape(depth)
    outs[6] = outs[6].reshape(depth)
    return tuple(outs)


def solution(mesh):
    return jax.shard_map(
        functools.partial(per_device, Layout(mesh)),
        mesh=mesh,
        in_specs=(
            P("sec", "lat", "lon", None),
            P("sec", "lat", "lon", None),
            P(),
            P(),
            P(),
            P(),
            P(),
            P(),
            P(),
        ),
        out_specs=(
            P("sec", "lat", "lon", None),
            P("sec", "lat", "lon", None),
            P("lon"),
            P("lon", None),
            P("lon", None),
            P("lon", None),
            P("lon"),
            P("lon", None),
            P("lon", None),
        ),
        check_vma=False,
    )
```

```python
import functools

import jax
import jax.numpy as jnp
import numpy as np
from jax import lax
from jax.experimental import pallas as pl
from jax.experimental.pallas import tpu as pltpu
from jax.sharding import PartitionSpec as P

HEADS = 8
RADIUS = 6
EPSILON = 1e-06
NEGATIVE = -1e30
UNIT = 48
D = 512
PAIRS = 4
MESH = pl.DeviceIdType.MESH
F32 = jnp.float32
BF16 = jnp.bfloat16
AROUND = ((0, 1), (0, -1), (1, 0), (-1, 0), (1, 1), (1, -1), (-1, 1), (-1, -1))


def dot(left, right):
    return jnp.dot(left, right, preferred_element_type=F32)


def dot_t(left, right):
    return lax.dot_general(left, right, (((1,), (1,)), ((), ())), preferred_element_type=F32)


def t_dot(left, right):
    return lax.dot_general(left, right, (((0,), (0,)), ((), ())), preferred_element_type=F32)


def near_window():
    query = np.arange(UNIT)
    row, col = query // 8, query % 8
    key = np.arange(9 * UNIT)
    unit, cell = key // UNIT, key % UNIT
    key_row = unit // 3 * RADIUS + cell // 8
    key_col = unit % 3 * RADIUS + cell % 8
    return (
        (key_row[None] >= row[:, None])
        & (key_row[None] <= row[:, None] + 2 * RADIUS)
        & (key_col[None] >= col[:, None])
        & (key_col[None] <= col[:, None] + 2 * RADIUS)
        & (cell % 8 < RADIUS)[None]
    )


def window_bias():
    bias = np.where(near_window(), 0.0, NEGATIVE).astype(np.float32)
    return np.concatenate([bias, bias], 0)


def window_bias_back():
    used = (np.arange(UNIT) % 8 < RADIUS)[:, None]
    bias = np.where(near_window() & used, 0.0, NEGATIVE).astype(np.float32).T
    return np.concatenate([bias, bias], 1)


def head_columns():
    matrix = np.zeros((D, 128), np.float32)
    for head in range(HEADS):
        matrix[head * 64 : head * 64 + 64, head * 8 : head * 8 + 6] = 1.0
    return matrix


def statistic_columns():
    matrix = np.zeros((2, PAIRS, 2 * UNIT, 128), np.float32)
    for which in range(2):
        for head in range(HEADS):
            pair, side = divmod(head, 2)
            start = head * 8 + 3 * which
            matrix[which, pair, side * UNIT : (side + 1) * UNIT, start : start + 3] = 0.125
    return matrix


def merge_matrix():
    matrix = np.zeros((4 * UNIT, 4 * UNIT), np.float32)
    for a in range(2):
        for b in range(2):
            for i in range(RADIUS):
                for j in range(RADIUS):
                    r, c = 2 * i + a, 2 * j + b
                    place = (r // 6 * 2 + c // 6) * UNIT + r % 6 * 8 + c % 6
                    matrix[(a * 2 + b) * UNIT + i * 8 + j, place] = 1.0
    return matrix


class Layout:
    def __init__(self, mesh):
        self.sec, self.lat, self.lon = (mesh.shape[k] for k in ("sec", "lat", "lon"))
        self.x = 4 if self.lon == 32 else 2
        self.z = self.lon // self.x
        self.y_hi = self.lat // 2
        self.y = self.y_hi * self.sec
        self.blocks = self.lon
        self.depth = D // self.blocks
        self.z_low = self.z // 2
        self.fine_width = 1024 // (2 * self.y)
        self.coarse_width = 4096 // (2 * self.y)


def unit_window(width, starts, ref, column):
    return jnp.concatenate([ref[pl.ds(s, width), pl.ds(column, 128)] for s in starts], 0)


def low_lanes(rows):
    return lax.broadcasted_iota(jnp.int32, (rows, 128), 1) < 64


def stack_heads(part):
    part = part.astype(F32) * 0.125
    low = low_lanes(UNIT)
    return jnp.concatenate([jnp.where(low, part, 0.0), jnp.where(low, 0.0, part)], 0).astype(BF16)


def merge_heads(both):
    return jnp.where(low_lanes(UNIT), both[:UNIT], both[UNIT:])


def attend(queries, keys, values, bias):
    scores = [dot_t(q, k) + bias for q, k in zip(queries, keys)]
    peaks = [jnp.max(s, axis=-1, keepdims=True) for s in scores]
    expos = [jnp.exp(s - m) for s, m in zip(scores, peaks)]
    totals = [jnp.sum(e, axis=-1, keepdims=True) for e in expos]
    attentions = [e * (1.0 / t) for e, t in zip(expos, totals)]
    mixed = [merge_heads(dot(a.astype(BF16), v)) for a, v in zip(attentions, values)]
    return attentions, mixed, [m + jnp.log(t) for m, t in zip(peaks, totals)]


def query_back(keys, values, attentions, slopes):
    probs = [dot_t(s, v) for s, v in zip(slopes, values)]
    means = [jnp.sum(a * p, axis=-1, keepdims=True) for a, p in zip(attentions, probs)]
    scores = [(a * (p - m)).astype(BF16) for a, p, m in zip(attentions, probs, means)]
    return [merge_heads(dot(s, k)) for s, k in zip(scores, keys)]


def pair_back(queries, slopes, statistics, keys, values, bias):
    scores = [dot_t(jnp.concatenate([q, statistics], 1), k) + bias for q, k in zip(queries, keys)]
    probs = [dot_t(jnp.concatenate([s, statistics], 1), v) for s, v in zip(slopes, values)]
    attentions = [jnp.exp(s) for s in scores]
    scores = [(a * p).astype(BF16) for a, p in zip(attentions, probs)]
    return (
        [merge_heads(t_dot(s, q)) for s, q in zip(scores, queries)],
        [merge_heads(t_dot(a.astype(BF16), s)) for a, s in zip(attentions, slopes)],
    )


def put_head_columns(total, pair, column):
    head = lax.broadcasted_iota(jnp.int32, total.shape, 1) // 8
    total = jnp.where(head == 2 * pair, column[:UNIT], total)
    return jnp.where(head == 2 * pair + 1, column[UNIT:], total)


def statistics_of(lse, slope, mixed, heads):
    product = slope.astype(F32) * mixed
    high = product.astype(BF16)
    low = (product - high.astype(F32)).astype(BF16)
    mean = dot(high, heads) + dot(low, heads)
    lane = lax.broadcasted_iota(jnp.int32, lse.shape, 1)
    part = lane % 8
    value = jnp.where(part < 3, lse * -8.0, -mean)
    first = value.astype(BF16)
    rest = value - first.astype(F32)
    second = rest.astype(BF16)
    third = rest - second.astype(F32)
    value = jnp.where(part % 3 == 0, first.astype(F32), jnp.where(part % 3 == 1, second.astype(F32), third))
    return jnp.where((part < 6) & (lane < 64), value, 0.0).astype(BF16)


def norm(field, gain):
    factor = lax.rsqrt(jnp.mean(field * field, axis=-1, keepdims=True) + EPSILON)
    normed = field * factor
    return factor, normed, (normed * gain).astype(BF16)


def input_back(slope, hidden_slope, field, gain):
    factor = lax.rsqrt(jnp.mean(field * field, axis=-1, keepdims=True) + EPSILON)
    normed = field * factor
    scaled = hidden_slope * gain
    return slope + factor * (scaled - normed * jnp.mean(scaled * normed, axis=-1, keepdims=True))


class Reducer:
    def __init__(self, lay, place, wires, refs):
        self.lay, self.place, self.wires = lay, place, wires
        (
            self.given, self.in_1a, self.in_1b, self.sum_2a, self.sum_2b,
            self.in_2a, self.in_2b, self.sum_3, self.in_3, self.full,
        ) = refs
        self.copies = []

    def device(self, core=None, y=None, x=None, z=None):
        here = self.place
        core = here["core"] if core is None else core
        y = here["y"] if y is None else y
        x = here["x"] if x is None else x
        z = here["z"] if z is None else z
        return (y % self.lay.sec, y // self.lay.sec * 2 + core, x * self.lay.z + z)

    def send(self, source, target, device):
        copy = self.wires(source, target, device)
        copy.start()
        self.copies.append(copy)

    def arrive(self):
        for copy in self.copies:
            copy.wait()
        self.copies = []

    def first_start(self):
        lay, here = self.lay, self.place
        low = pl.ds(0, lay.z_low)
        high = pl.ds(lay.z_low, lay.z - lay.z_low)
        for step in range(1, lay.x):
            x = (here["x"] + step) % lay.x
            self.send(self.given.at[:, x, low], self.in_1a.at[step - 1], self.device(x=x))
        for step in range(1, lay.y):
            y = (here["y"] + step) % lay.y
            self.send(self.given.at[y, :, high], self.in_1b.at[step - 1], self.device(y=y))

    def first_finish(self):
        self.arrive()
        lay, here = self.lay, self.place
        low = pl.ds(0, lay.z_low)
        high = pl.ds(lay.z_low, lay.z - lay.z_low)

        @pl.loop(0, lay.y)
        def _(y):
            total = self.given[y, here["x"], low].astype(F32)
            for k in range(lay.x - 1):
                total += self.in_1a[k, y].astype(F32)
            self.sum_2a[y] = total.astype(BF16)

        @pl.loop(0, lay.x)
        def _(x):
            total = self.given[here["y"], x, high].astype(F32)
            for k in range(lay.y - 1):
                total += self.in_1b[k, x].astype(F32)
            self.sum_2b[x] = total.astype(BF16)

    def second_start(self):
        lay, here = self.lay, self.place
        for step in range(1, lay.y):
            y = (here["y"] + step) % lay.y
            self.send(self.sum_2a.at[y], self.in_2a.at[step - 1], self.device(y=y))
        for step in range(1, lay.x):
            x = (here["x"] + step) % lay.x
            self.send(self.sum_2b.at[x], self.in_2b.at[step - 1], self.device(x=x))

    def second_finish(self):
        self.arrive()
        lay, here = self.lay, self.place
        total = self.sum_2a[here["y"]].astype(F32)
        for k in range(lay.y - 1):
            total += self.in_2a[k].astype(F32)
        self.sum_3[pl.ds(0, lay.z_low)] = total.astype(BF16)
        total = self.sum_2b[here["x"]].astype(F32)
        for k in range(lay.x - 1):
            total += self.in_2b[k].astype(F32)
        self.sum_3[pl.ds(lay.z_low, lay.z - lay.z_low)] = total.astype(BF16)

    def third_start(self):
        lay, here = self.lay, self.place
        for step in range(1, lay.z):
            z = (here["z"] + step) % lay.z
            self.send(self.sum_3.at[z], self.in_3.at[step - 1], self.device(z=z))

    def third_finish(self):
        self.arrive()
        lay, here = self.lay, self.place
        total = self.sum_3[here["z"]].astype(F32)
        for k in range(lay.z - 1):
            total += self.in_3[k].astype(F32)
        self.full[here["core"], here["y"]] = total.astype(BF16)

    def last_start(self):
        self.spread(self.full)

    def spread(self, ref):
        lay, here = self.lay, self.place
        own = ref.at[here["core"], here["y"]]
        for across in range(2):
            for step in range(lay.y):
                if across or step:
                    core = (here["core"] + across) % 2
                    y = (here["y"] + step) % lay.y
                    self.send(own, own, self.device(core=core, y=y))

    def last_finish(self):
        self.arrive()

    def column(self, start, width):
        size = self.full.shape[-1]
        parts = []
        while width > 0:
            group, offset = divmod(start, size)
            take = min(width, size - offset)
            parts.append(self.full[group // self.lay.y, group % self.lay.y, :, offset : offset + take])
            start, width = start + take, width - take
        return (parts[0] if len(parts) == 1 else jnp.concatenate(parts, 1)).astype(F32)

    def put(self, start, product):
        lay = self.lay
        size = self.given.shape[-1]
        done, width = 0, product.shape[1]
        while done < width:
            group, offset = divmod(start + done, size)
            take = min(width - done, size - offset)
            piece = product[:, done : done + take].astype(BF16)
            self.given[group, :, :, :, offset : offset + take] = piece.reshape(lay.x, lay.z, lay.depth, take)
            done += take

    def put_merged(self, part, product):
        lay = self.lay
        size = self.given.shape[-1]
        count = lay.blocks // 4
        shaped = product.astype(BF16).reshape(count, 4, lay.depth, D)
        for run in range(4):
            group, offset = divmod(run * D, size)
            for block in range(count):
                x, z = divmod(part * count + block, lay.z)
                self.given[group, x, z, :, offset : offset + D] = shaped[block, run]


class DeepReducer(Reducer):
    def __init__(self, lay, place, wires, refs):
        self.lay, self.place, self.wires = lay, place, wires
        self.given, self.in_1, self.sum_2, self.in_2, self.parts, self.full = refs
        self.copies = []

    def first_start(self):
        lay, here = self.lay, self.place
        for step in range(1, lay.z):
            z = (here["z"] + step) % lay.z
            self.send(self.given.at[:, :, z], self.in_1.at[step - 1], self.device(z=z))

    def first_finish(self):
        self.arrive()
        lay, here = self.lay, self.place

        @pl.loop(0, lay.y)
        def _(y):
            total = self.given[y, :, here["z"]].astype(F32)
            for k in range(lay.z - 1):
                total += self.in_1[k, y].astype(F32)
            self.sum_2[y] = total.astype(BF16)

    def second_start(self):
        lay, here = self.lay, self.place
        for step in range(1, lay.x):
            x = (here["x"] + step) % lay.x
            self.send(self.sum_2.at[:, x], self.in_2.at[step - 1], self.device(x=x))

    def second_finish(self):
        self.arrive()
        here = self.place
        total = self.sum_2[:, here["x"]].astype(F32)
        for k in range(self.lay.x - 1):
            total += self.in_2[k].astype(F32)
        self.parts[here["core"], here["y"]] = total.astype(BF16)

    def last_start(self):
        self.spread(self.parts)

    def last_finish(self):
        self.arrive()

        @pl.loop(0, 2)
        def _(core):
            total = self.parts[core, 0].astype(F32)
            for y in range(1, self.lay.y):
                total += self.parts[core, y].astype(F32)
            self.full[core] = total.astype(BF16)


GROUPS = ((0, 1, 2, 3),)


def lanes_of(pair, start=0):
    return slice(start + pair * 128, start + pair * 128 + 128)


def with_columns(part, columns):
    return jnp.concatenate([stack_heads(part), columns], 1)


def gain_back(lay, lon, total, weight, gain):
    own = weight[pl.ds(pl.multiple_of(lon * lay.depth, lay.depth), lay.depth), :].astype(F32)
    column = jnp.sum(total * own, axis=1, keepdims=True)
    row = lax.broadcasted_iota(jnp.int32, (lay.depth, D), 0) + lon * lay.depth
    at = lax.broadcasted_iota(jnp.int32, (lay.depth, D), 1) == row
    column = column / jnp.sum(jnp.where(at, gain, 0.0), axis=1, keepdims=True)
    square = (lay.depth, lay.depth)
    same = lax.broadcasted_iota(jnp.int32, square, 0) == lax.broadcasted_iota(jnp.int32, square, 1)
    return jnp.sum(jnp.where(same, column, 0.0), axis=0, keepdims=True)


def kernel(
    lay,
    tokens_hbm, cotangent_hbm, fine_gain, coarse_gain,
    fine_attend_hbm, fine_output_hbm, merge_hbm, coarse_attend_hbm, coarse_output_hbm,
    bias_hbm, bias_back_hbm, heads_hbm, columns_hbm, merge_ref_hbm, split_hbm,
    coarse_field_hbm, token_gradient_hbm, fine_gain_out, coarse_gain_out, coarse_full, early_full, late_full,
    tokens, cotangent, coarse_field, token_gradient,
    fine_attend, fine_output, merge_weight, coarse_attend, coarse_output,
    bias_ref, bias_back_ref, heads_ref, columns_ref, merge_ref, split_ref,
    strip, field_f, wide_f, projected_f, attention_f, exact_f, lse_f, slope_wide_f, left_f, right_f, merged,
    field_c, wide_c, slope_wide_c, projected_c, mixed_slope_c, attention_c, exact_c, lse_c, statistics_c, factors_c,
    *rest,
):
    load_sem, send_sem, recv_sem = rest[26:]
    sec, lat, lon = (lax.axis_index(k) for k in ("sec", "lat", "lon"))
    core = lat % 2
    place = {"core": core, "y": lat // 2 * lay.sec + sec, "x": lon // lay.z, "z": lon % lay.z}
    used = [0]

    def wires(source, target, device):
        index = used[0]
        used[0] += 1
        return pltpu.make_async_remote_copy(
            src_ref=source,
            dst_ref=target,
            send_sem=send_sem.at[index],
            recv_sem=recv_sem.at[index],
            device_id=device,
            device_id_type=MESH,
        )

    def neighbour(step):
        return (sec, (lat + step[0] + lay.lat) % lay.lat, (lon + step[1] + lay.lon) % lay.lon)

    def start_rims(source, target):
        copies = []
        for step in AROUND:
            copy = wires(source(step), target(step), neighbour(step))
            if step[0]:
                last = lay.lat - 1
                sends = lat != (last if step[0] > 0 else 0)
                takes = lat != (0 if step[0] > 0 else last)
                pl.when(sends)(copy.start)
                copies.append((copy, sends, takes))
            else:
                copy.start()
                copies.append((copy, None, None))
        return copies

    def wait_rims(copies):
        for copy, sends, takes in copies:
            if sends is None:
                copy.wait()
            else:
                pl.when(sends)(copy.wait_send)
                pl.when(takes)(copy.wait_recv)

    def start_twin(source, target):
        copy = wires(source, target, coarse_sum.device(core=1 - core))
        copy.start()
        return copy

    coarse_sum = Reducer(lay, place, wires, rest[:10])
    early_sum = DeepReducer(lay, place, wires, rest[10:16])
    late_sum = Reducer(lay, place, wires, rest[16:26])

    barrier = pltpu.get_barrier_semaphore()
    peers = [neighbour(step) for step in AROUND]
    peers += [coarse_sum.device(x=(place["x"] + s) % lay.x) for s in range(1, lay.x)]
    peers += [coarse_sum.device(z=(place["z"] + s) % lay.z) for s in range(1, lay.z)]
    peers += [
        coarse_sum.device(core=(core + c) % 2, y=(place["y"] + s) % lay.y)
        for c in range(2)
        for s in range(lay.y)
        if c or s
    ]
    for peer in peers:
        pl.semaphore_signal(barrier, inc=1, device_id=peer, device_id_type=MESH)

    loads = {
        name: pltpu.make_async_copy(source, target, load_sem.at[i])
        for i, (name, source, target) in enumerate(
            (
                ("tokens", tokens_hbm, tokens),
                ("cotangent", cotangent_hbm, cotangent),
                ("fine_attend", fine_attend_hbm, fine_attend),
                ("bias_ref", bias_hbm, bias_ref),
                ("fine_output", fine_output_hbm, fine_output),
                ("merge_ref", merge_ref_hbm, merge_ref),
                ("merge_weight", merge_hbm, merge_weight),
                ("coarse_output", coarse_output_hbm, coarse_output),
                ("coarse_attend", coarse_attend_hbm, coarse_attend),
                ("heads_ref", heads_hbm, heads_ref),
                ("columns_ref", columns_hbm, columns_ref),
                ("bias_back_ref", bias_back_hbm, bias_back_ref),
                ("split_ref", split_hbm, split_ref),
            )
        )
    }
    for load in loads.values():
        load.start()

    field_f[...] = jnp.zeros_like(field_f)
    field_c[...] = jnp.zeros_like(field_c)
    loads["tokens"].wait()
    for row in range(12):
        strip[row, :12] = tokens[0, row].astype(F32)
    for row in range(12):
        for half in range(2):
            start = (row // 6 * 2 + half) * UNIT + row % 6 * 8
            field_f[start : start + 6] = strip[row, 6 * half : 6 * half + 6]
    for unit in range(4):
        wide_f[1 + unit // 2, 1 + unit % 2] = field_f[unit * UNIT : (unit + 1) * UNIT].astype(BF16)
    loads["cotangent"].wait()
    for row in range(6):
        field_c[row * 8 : row * 8 + 6] = cotangent[0, row].astype(F32)
    slope_wide_c[1, 1] = field_c[...].astype(BF16)
    factors_c[5, 0] = field_c[...].astype(BF16)

    pl.semaphore_wait(barrier, len(peers))

    def part(step, mine):
        index = []
        for way in step:
            if way == 0:
                index.append(pl.ds(1, 2))
            elif way > 0:
                index.append(2 if mine else 3)
            else:
                index.append(1 if mine else 0)
        return tuple(index)

    def opposite(step):
        return (-step[0], -step[1])

    def fine_rims(ref):
        return start_rims(lambda step: ref.at[part(step, True)], lambda step: ref.at[part(opposite(step), False)])

    def coarse_rims(ref):
        return start_rims(lambda step: ref.at[1, 1], lambda step: ref.at[1 - step[0], 1 - step[1]])

    rims = fine_rims(wide_f)

    def clear(row):
        for ref in (wide_f, slope_wide_f, wide_c, slope_wide_c, statistics_c):
            ref[row if row == 0 else ref.shape[0] - 1] = jnp.zeros(ref.shape[1:], ref.dtype)

    pl.when(lat == 0)(lambda: clear(0))
    pl.when(lat == lay.lat - 1)(lambda: clear(-1))

    top = jnp.where(lat == 0, NEGATIVE, 0.0)
    bottom = jnp.where(lat == lay.lat - 1, NEGATIVE, 0.0)
    lanes = lax.broadcasted_iota(jnp.int32, (1, 9 * UNIT), 1)

    def bias_at(is_first, is_last):
        above = jnp.where(is_first, top, 0.0)
        below = jnp.where(is_last, bottom, 0.0)
        rim = jnp.where(lanes < 3 * UNIT, above, 0.0) + jnp.where(lanes >= 6 * UNIT, below, 0.0)
        return bias_ref[...] + rim

    gain_f = fine_gain[...]
    gain_c = coarse_gain[...]
    loads["fine_attend"].wait()
    for run in range(2):
        hidden = norm(field_f[run * 96 : run * 96 + 96], gain_f)[2]
        left_f[0, 0, run * 96 : run * 96 + 96] = hidden
        projected_f[240 + run * 192 : 336 + run * 192, :] = dot(hidden, fine_attend[...]).astype(BF16)
    twin_hidden = start_twin(left_f.at[0, 0], left_f.at[0, 1])
    wait_rims(rims)
    slope_rims = coarse_rims(slope_wide_c)
    for start, units in (
        (0, (wide_f[0].reshape(4 * UNIT, D), wide_f[1, 0])),
        (336, (wide_f[1, 3], wide_f[2, 0])),
        (528, (wide_f[2, 3], wide_f[3].reshape(4 * UNIT, D))),
    ):
        field = jnp.concatenate([unit.astype(F32) for unit in units], 0)
        hidden = norm(field, gain_f)[2]
        projected_f[start : start + field.shape[0], :] = dot(hidden, fine_attend[...]).astype(BF16)

    loads["bias_ref"].wait()

    def starts_of(quad):
        first, second = quad // 2, quad % 2
        return [pl.multiple_of(((first + i) * 4 + second) * UNIT, UNIT) for i in range(3)]

    def middle_of(quad):
        return pl.ds(pl.multiple_of(((1 + quad // 2) * 4 + 1 + quad % 2) * UNIT, UNIT), UNIT)

    def own_of(quad):
        return pl.ds(pl.multiple_of(quad * UNIT, UNIT), UNIT)

    @pl.loop(0, 4, unroll=4)
    def _(quad):
        first = quad // 2
        own, middle, starts = own_of(quad), middle_of(quad), starts_of(quad)
        bias = bias_at(first == 0, first == 1)
        lse = jnp.zeros((UNIT, 128), F32)
        for pairs in GROUPS:
            results = attend(
                [stack_heads(projected_f[middle, lanes_of(pair)]) for pair in pairs],
                [unit_window(3 * UNIT, starts, projected_f, D + pair * 128) for pair in pairs],
                [unit_window(3 * UNIT, starts, projected_f, 2 * D + pair * 128) for pair in pairs],
                bias,
            )
            for pair, attention, mixed, column in zip(pairs, *results):
                attention_f[quad, pair] = attention
                exact_f[own, lanes_of(pair)] = mixed
                left_f[1, 0, own, lanes_of(pair)] = mixed.astype(BF16)
                lse = put_head_columns(lse, pair, column)
        lse_f[own, :] = lse

    twin_mixed = start_twin(left_f.at[1, 0], left_f.at[1, 1])
    loads["fine_output"].wait()
    loads["merge_ref"].wait()
    fine_field = (field_f[...] + dot(left_f[1, 0], fine_output[...])).astype(BF16)
    merged[0] = dot(merge_ref[...], fine_field).astype(BF16)
    loads["merge_weight"].wait()
    coarse_in = jnp.zeros((UNIT, D), F32)
    for quarter in range(4):
        rows = slice(quarter * UNIT, (quarter + 1) * UNIT)
        coarse_in += dot(merged[0, rows], merge_weight[quarter * D : (quarter + 1) * D])
    wide_c[1, 1] = coarse_in.astype(BF16)
    rims = coarse_rims(wide_c)
    twin_merged = start_twin(merged.at[0], merged.at[1])

    for name in ("coarse_output", "coarse_attend", "heads_ref", "columns_ref", "bias_back_ref", "split_ref"):
        loads[name].wait()
    field_c[...] = wide_c[1, 1].astype(F32)
    factors_c[0, 0] = norm(field_c[...], gain_c)[2]
    wait_rims(slope_rims)
    mixed_slope_c[...] = dot_t(slope_wide_c[...].reshape(9 * UNIT, D), coarse_output[...]).astype(BF16)
    wait_rims(rims)
    hidden = norm(wide_c[...].reshape(9 * UNIT, D).astype(F32), gain_c)[2]
    projected_c[...] = dot(hidden, coarse_attend[...]).astype(BF16)
    bias = bias_at(True, True)
    middle = slice(4 * UNIT, 5 * UNIT)
    lse = jnp.zeros((UNIT, 128), F32)
    for pairs in GROUPS:
        results = attend(
            [stack_heads(projected_c[middle, lanes_of(pair)]) for pair in pairs],
            [projected_c[:, lanes_of(pair, D)] for pair in pairs],
            [projected_c[:, lanes_of(pair, 2 * D)] for pair in pairs],
            bias,
        )
        for pair, attention, mixed, column in zip(pairs, *results):
            attention_c[pair] = attention
            exact_c[:, lanes_of(pair)] = mixed
            lse = put_head_columns(lse, pair, column)
    statistics_c[1, 1] = statistics_of(lse, mixed_slope_c[middle, :], exact_c[...], heads_ref[...])
    rims = coarse_rims(statistics_c)
    factors_c[4, 0] = exact_c[...].astype(BF16)
    moved = field_c[...] + dot(factors_c[4, 0], coarse_output[...])
    for row in range(6):
        coarse_field[0, row] = moved[row * 8 : row * 8 + 6].astype(BF16)
    field_store = pltpu.make_async_copy(coarse_field, coarse_field_hbm, load_sem.at[13])
    field_store.start()
    for pairs in GROUPS:
        results = query_back(
            [projected_c[:, lanes_of(pair, D)] for pair in pairs],
            [projected_c[:, lanes_of(pair, 2 * D)] for pair in pairs],
            [attention_c[pair] for pair in pairs],
            [stack_heads(mixed_slope_c[middle, lanes_of(pair)]) for pair in pairs],
        )
        for pair, query_slope in zip(pairs, results):
            factors_c[1, 0, :, lanes_of(pair)] = query_slope.astype(BF16)
    wait_rims(rims)
    statistics = statistics_c[...].reshape(9 * UNIT, 128)
    for pairs in GROUPS:
        results = pair_back(
            [projected_c[:, lanes_of(pair)] for pair in pairs],
            [mixed_slope_c[:, lanes_of(pair)] for pair in pairs],
            statistics,
            [with_columns(projected_c[middle, lanes_of(pair, D)], columns_ref[0, pair]) for pair in pairs],
            [with_columns(projected_c[middle, lanes_of(pair, 2 * D)], columns_ref[1, pair]) for pair in pairs],
            bias_back_ref[...],
        )
        for pair, key_slope, value_slope in zip(pairs, *results):
            factors_c[2, 0, :, lanes_of(pair)] = key_slope.astype(BF16)
            factors_c[3, 0, :, lanes_of(pair)] = value_slope.astype(BF16)
    hidden_slope = sum(
        dot_t(factors_c[1 + k, 0], coarse_attend[:, k * D : (k + 1) * D]) for k in range(3)
    )
    slope = factors_c[5, 0].astype(F32)
    coarse_slope = input_back(slope, hidden_slope, field_c[...], gain_c).astype(BF16)
    factors_c[6, 0] = coarse_slope
    twin_factors = start_twin(factors_c.at[:, 0], factors_c.at[:, 1])

    merged_slope = jnp.concatenate(
        [dot_t(coarse_slope, merge_weight[k * D : (k + 1) * D]).astype(BF16) for k in range(4)], 0
    )
    slope_f = dot(split_ref[...], merged_slope).astype(BF16)
    right_f[1, 0] = slope_f
    mixed_slope = dot_t(slope_f, fine_output[...]).astype(BF16)
    statistics = statistics_of(lse_f[...], mixed_slope, exact_f[...], heads_ref[...])
    for unit in range(4):
        rows = slice(unit * UNIT, (unit + 1) * UNIT)
        slope_wide_f[1 + unit // 2, 1 + unit % 2, :, :D] = mixed_slope[rows]
        slope_wide_f[1 + unit // 2, 1 + unit % 2, :, D:] = statistics[rows]
    rims = fine_rims(slope_wide_f)
    twin_slope = start_twin(right_f.at[1, 0], right_f.at[1, 1])

    @pl.loop(0, 4, unroll=4)
    def _(quad):
        own, starts = own_of(quad), starts_of(quad)
        for pairs in GROUPS:
            results = query_back(
                [unit_window(3 * UNIT, starts, projected_f, D + pair * 128) for pair in pairs],
                [unit_window(3 * UNIT, starts, projected_f, 2 * D + pair * 128) for pair in pairs],
                [attention_f[quad, pair] for pair in pairs],
                [stack_heads(slope_wide_f[1 + quad // 2, 1 + quad % 2, :, lanes_of(pair)]) for pair in pairs],
            )
            for pair, query_slope in zip(pairs, results):
                right_f[0, 0, own, lanes_of(pair)] = query_slope.astype(BF16)

    twin_query = start_twin(right_f.at[0, 0], right_f.at[0, 1])
    twin_factors.wait()
    twin_merged.wait()

    def both(index):
        return factors_c[index].reshape(2 * UNIT, D)

    @pl.when(core == 0)
    def _():
        for k in range(3):
            coarse_sum.put(k * D, t_dot(both(0), both(1 + k)))
        coarse_sum.put(3 * D, t_dot(both(4), both(5)))

    @pl.when(core == 1)
    def _():
        for k in range(4):
            rows = slice(k * UNIT, (k + 1) * UNIT)
            coarse_sum.put_merged(k, t_dot(merged[:, rows].reshape(2 * UNIT, D), both(6)))

    coarse_sum.first_start()
    twin_hidden.wait()
    twin_mixed.wait()
    twin_slope.wait()
    twin_query.wait()
    early_sum.put(0, t_dot(left_f[core].reshape(8 * UNIT, D), right_f[core].reshape(8 * UNIT, D)))
    wait_rims(rims)
    early_sum.first_start()

    @pl.loop(0, 4, unroll=4)
    def _(quad):
        own, middle, starts = own_of(quad), middle_of(quad), starts_of(quad)
        first, second = quad // 2, quad % 2

        def around(lanes):
            rows = [slope_wide_f[first + i, pl.ds(second, 3), :, lanes] for i in range(3)]
            return jnp.concatenate([r.reshape(3 * UNIT, 128) for r in rows], 0)

        statistics = around(slice(D, D + 128))
        for pairs in GROUPS:
            results = pair_back(
                [unit_window(3 * UNIT, starts, projected_f, pair * 128) for pair in pairs],
                [around(lanes_of(pair)) for pair in pairs],
                statistics,
                [with_columns(projected_f[middle, lanes_of(pair, D)], columns_ref[0, pair]) for pair in pairs],
                [with_columns(projected_f[middle, lanes_of(pair, 2 * D)], columns_ref[1, pair]) for pair in pairs],
                bias_back_ref[...],
            )
            for pair, key_slope, value_slope in zip(pairs, *results):
                right_f[2, 0, own, lanes_of(pair)] = key_slope.astype(BF16)
                right_f[3, 0, own, lanes_of(pair)] = value_slope.astype(BF16)

    other = 3 - core
    twin_pair = start_twin(right_f.at[other, 0], right_f.at[other, 1])
    hidden_slope = dot_t(right_f[0, 0], fine_attend[:, :D])
    hidden_slope += dot_t(right_f[2, 0], fine_attend[:, D : 2 * D])
    hidden_slope += dot_t(right_f[3, 0], fine_attend[:, 2 * D :])
    twin_pair.wait()
    late_sum.put(0, t_dot(left_f[0].reshape(8 * UNIT, D), right_f[2 + core].reshape(8 * UNIT, D)))
    late_sum.first_start()
    coarse_sum.first_finish()
    coarse_sum.second_start()
    slope = input_back(right_f[1, 0].astype(F32), hidden_slope, field_f[...], gain_f)
    for row in range(12):
        for half in range(2):
            start = (row // 6 * 2 + half) * UNIT + row % 6 * 8
            strip[row, 6 * half : 6 * half + 6] = slope[start : start + 6]
    for row in range(12):
        token_gradient[0, row] = strip[row, :12].astype(BF16)
    gradient_store = pltpu.make_async_copy(token_gradient, token_gradient_hbm, load_sem.at[14])
    gradient_store.start()
    late_sum.first_finish()
    late_sum.second_start()
    coarse_sum.second_finish()
    coarse_sum.third_start()
    early_sum.first_finish()
    early_sum.second_start()
    late_sum.second_finish()
    late_sum.third_start()
    coarse_sum.third_finish()
    coarse_sum.last_start()
    early_sum.second_finish()
    early_sum.last_start()
    late_sum.third_finish()
    late_sum.last_start()
    coarse_sum.last_finish()
    coarse_full[...] = coarse_sum.full[...]
    coarse_gain_out[...] = gain_back(lay, lon, coarse_sum.column(0, 3 * D), coarse_attend, gain_c)
    early_sum.last_finish()
    early_full[...] = early_sum.full[...]
    late_sum.last_finish()
    late_full[...] = late_sum.full[...]
    field_store.wait()
    gradient_store.wait()
    total = jnp.concatenate([early_sum.column(0, D), late_sum.column(0, 2 * D)], 1)
    fine_gain_out[...] = gain_back(lay, lon, total, fine_attend, gain_f)


def finish(lay, *refs):
    field, gradient, fine_gain, coarse_gain, coarse_full, early_full, late_full = refs[:7]
    (
        field_out, gradient_out, fine_gain_out, fine_attend, fine_output, merge,
        coarse_gain_out, coarse_attend, coarse_output,
    ) = refs[7:]
    field_out[...] = field[...]
    gradient_out[...] = gradient[...]
    fine_gain_out[...] = fine_gain[...]
    coarse_gain_out[...] = coarse_gain[...]

    def column(full, start, width):
        return Reducer(lay, None, None, (None,) * 9 + (full,)).column(start, width)

    for k in range(3):
        fine_attend[:, k * D : (k + 1) * D] = column(late_full, (k - 1) * D, D) if k else column(early_full, 0, D)
        coarse_attend[:, k * D : (k + 1) * D] = column(coarse_full, k * D, D)
    fine_output[...] = column(early_full, D, D)
    coarse_output[...] = column(coarse_full, 3 * D, D)
    for run in range(4):
        merge[run * lay.depth : (run + 1) * lay.depth, :] = column(coarse_full, (4 + run) * D, D)


def reducer_scratch(lay, width):
    y, x, z, low = lay.y, lay.x, lay.z, lay.z_low
    high = z - low
    end = (lay.depth, width)
    shapes = (
        (y, x, z), (x - 1, y, low), (y - 1, x, high), (y, low), (x, high),
        (y - 1, low), (x - 1, high), (z,), (z - 1,), (2, y),
    )
    return [pltpu.VMEM(shape + end, BF16) for shape in shapes]


def deep_scratch(lay, width):
    y, x, z = lay.y, lay.x, lay.z
    end = (lay.depth, width)
    shapes = ((y, x, z), (z - 1, y, x), (y, x), (x - 1, y), (2, y, y), (2, y))
    return [pltpu.VMEM(shape + end, BF16) for shape in shapes]


def per_device(
    lay,
    tokens,
    cotangent,
    fine_gain,
    fine_attend,
    fine_output,
    merge_weight,
    coarse_gain,
    coarse_attend,
    coarse_output,
):
    vmem = pl.BlockSpec(memory_space=pltpu.VMEM)
    hbm = pl.BlockSpec(memory_space=pl.ANY)
    select = merge_matrix()
    constants = (
        jnp.asarray(window_bias()),
        jnp.asarray(window_bias_back()),
        jnp.asarray(head_columns(), BF16),
        jnp.asarray(statistic_columns(), BF16),
        jnp.asarray(select, BF16),
        jnp.asarray(select.T, BF16),
    )
    per_batch = 2 * (lay.x - 1 + lay.y - 1) + lay.z - 1 + 2 * lay.y - 1
    deep_batch = lay.z - 1 + lay.x - 1 + 2 * lay.y - 1
    copies = 5 * 8 + 7 + 2 * per_batch + deep_batch
    depth = lay.depth
    fine_shape = jax.ShapeDtypeStruct((2, lay.y, depth, lay.fine_width), BF16)
    between = pl.pallas_call(
        functools.partial(kernel, lay),
        out_shape=(
            jax.ShapeDtypeStruct(cotangent.shape, BF16),
            jax.ShapeDtypeStruct(tokens.shape, BF16),
            jax.ShapeDtypeStruct((1, depth), F32),
            jax.ShapeDtypeStruct((1, depth), F32),
            jax.ShapeDtypeStruct((2, lay.y, depth, lay.coarse_width), BF16),
            fine_shape,
            fine_shape,
        ),
        in_specs=[hbm] * 2 + [vmem] * 2 + [hbm] * 11,
        out_specs=[hbm] * 2 + [vmem] * 5,
        scratch_shapes=[
            pltpu.VMEM(tokens.shape, BF16),
            pltpu.VMEM(cotangent.shape, BF16),
            pltpu.VMEM(cotangent.shape, BF16),
            pltpu.VMEM(tokens.shape, BF16),
            pltpu.VMEM((D, 3 * D), BF16),
            pltpu.VMEM((D, D), BF16),
            pltpu.VMEM((4 * D, D), BF16),
            pltpu.VMEM((D, 3 * D), BF16),
            pltpu.VMEM((D, D), BF16),
            *(pltpu.VMEM(c.shape, c.dtype) for c in constants),
            pltpu.VMEM((12, 16, D), F32),
            pltpu.VMEM((4 * UNIT, D), F32),
            pltpu.VMEM((4, 4, UNIT, D), BF16),
            pltpu.VMEM((16 * UNIT, 3 * D), BF16),
            pltpu.VMEM((4, PAIRS, 2 * UNIT, 9 * UNIT), F32),
            pltpu.VMEM((4 * UNIT, D), F32),
            pltpu.VMEM((4 * UNIT, 128), F32),
            pltpu.VMEM((4, 4, UNIT, D + 128), BF16),
            pltpu.VMEM((2, 2, 4 * UNIT, D), BF16),
            pltpu.VMEM((4, 2, 4 * UNIT, D), BF16),
            pltpu.VMEM((2, 4 * UNIT, D), BF16),
            pltpu.VMEM((UNIT, D), F32),
            pltpu.VMEM((3, 3, UNIT, D), BF16),
            pltpu.VMEM((3, 3, UNIT, D), BF16),
            pltpu.VMEM((9 * UNIT, 3 * D), BF16),
            pltpu.VMEM((9 * UNIT, D), BF16),
            pltpu.VMEM((PAIRS, 2 * UNIT, 9 * UNIT), F32),
            pltpu.VMEM((UNIT, D), F32),
            pltpu.VMEM((UNIT, 128), F32),
            pltpu.VMEM((3, 3, UNIT, 128), BF16),
            pltpu.VMEM((7, 2, UNIT, D), BF16),
            *reducer_scratch(lay, lay.coarse_width),
            *deep_scratch(lay, lay.fine_width),
            *reducer_scratch(lay, lay.fine_width),
            pltpu.SemaphoreType.DMA((15,)),
            pltpu.SemaphoreType.DMA((copies,)),
            pltpu.SemaphoreType.DMA((copies,)),
        ],
        compiler_params=pltpu.CompilerParams(
            collective_id=0, has_side_effects=True, vmem_limit_bytes=56 * 1024 * 1024
        ),
    )(
        tokens,
        cotangent,
        fine_gain.reshape(1, D),
        coarse_gain.reshape(1, D),
        fine_attend,
        fine_output,
        merge_weight,
        coarse_attend,
        coarse_output,
        *constants,
    )
    outs = pl.pallas_call(
        functools.partial(finish, lay),
        out_shape=(
            jax.ShapeDtypeStruct(cotangent.shape, BF16),
            jax.ShapeDtypeStruct(tokens.shape, BF16),
            jax.ShapeDtypeStruct((1, depth), F32),
            jax.ShapeDtypeStruct((depth, 3 * D), F32),
            jax.ShapeDtypeStruct((depth, D), F32),
            jax.ShapeDtypeStruct((4 * depth, D), F32),
            jax.ShapeDtypeStruct((1, depth), F32),
            jax.ShapeDtypeStruct((depth, 3 * D), F32),
            jax.ShapeDtypeStruct((depth, D), F32),
        ),
        in_specs=[vmem] * 7,
        out_specs=[vmem] * 9,
    )(*between)
    outs = list(outs)
    outs[2] = outs[2].reshape(depth)
    outs[6] = outs[6].reshape(depth)
    return tuple(outs)


def solution(mesh):
    return jax.shard_map(
        functools.partial(per_device, Layout(mesh)),
        mesh=mesh,
        in_specs=(
            P("sec", "lat", "lon", None),
            P("sec", "lat", "lon", None),
            P(),
            P(),
            P(),
            P(),
            P(),
            P(),
            P(),
        ),
        out_specs=(
            P("sec", "lat", "lon", None),
            P("sec", "lat", "lon", None),
            P("lon"),
            P("lon", None),
            P("lon", None),
            P("lon", None),
            P("lon"),
            P("lon", None),
            P("lon", None),
        ),
        check_vma=False,
    )
```

```python
import functools

import jax
import jax.numpy as jnp
import numpy as np
from jax import lax
from jax.experimental import pallas as pl
from jax.experimental.pallas import tpu as pltpu
from jax.sharding import PartitionSpec as P

HEADS = 8
RADIUS = 6
EPSILON = 1e-06
NEGATIVE = -1e30
UNIT = 48
D = 512
PAIRS = 4
MESH = pl.DeviceIdType.MESH
F32 = jnp.float32
BF16 = jnp.bfloat16
AROUND = ((0, 1), (0, -1), (1, 0), (-1, 0), (1, 1), (1, -1), (-1, 1), (-1, -1))


def dot(left, right):
    return jnp.dot(left, right, preferred_element_type=F32)


def dot_t(left, right):
    return lax.dot_general(left, right, (((1,), (1,)), ((), ())), preferred_element_type=F32)


def t_dot(left, right):
    return lax.dot_general(left, right, (((0,), (0,)), ((), ())), preferred_element_type=F32)


def near_window():
    query = np.arange(UNIT)
    row, col = query // 8, query % 8
    key = np.arange(9 * UNIT)
    unit, cell = key // UNIT, key % UNIT
    key_row = unit // 3 * RADIUS + cell // 8
    key_col = unit % 3 * RADIUS + cell % 8
    return (
        (key_row[None] >= row[:, None])
        & (key_row[None] <= row[:, None] + 2 * RADIUS)
        & (key_col[None] >= col[:, None])
        & (key_col[None] <= col[:, None] + 2 * RADIUS)
        & (cell % 8 < RADIUS)[None]
    )


def window_bias():
    bias = np.where(near_window(), 0.0, NEGATIVE).astype(np.float32)
    return np.concatenate([bias, bias], 0)


def window_bias_back():
    used = (np.arange(UNIT) % 8 < RADIUS)[:, None]
    bias = np.where(near_window() & used, 0.0, NEGATIVE).astype(np.float32).T
    return np.concatenate([bias, bias], 1)


def head_columns():
    matrix = np.zeros((D, 128), np.float32)
    for head in range(HEADS):
        matrix[head * 64 : head * 64 + 64, head * 8 : head * 8 + 6] = 1.0
    return matrix


def statistic_columns():
    matrix = np.zeros((2, PAIRS, 2 * UNIT, 128), np.float32)
    for which in range(2):
        for head in range(HEADS):
            pair, side = divmod(head, 2)
            start = head * 8 + 3 * which
            matrix[which, pair, side * UNIT : (side + 1) * UNIT, start : start + 3] = 0.125
    return matrix


def merge_matrix():
    matrix = np.zeros((4 * UNIT, 4 * UNIT), np.float32)
    for a in range(2):
        for b in range(2):
            for i in range(RADIUS):
                for j in range(RADIUS):
                    r, c = 2 * i + a, 2 * j + b
                    place = (r // 6 * 2 + c // 6) * UNIT + r % 6 * 8 + c % 6
                    matrix[(a * 2 + b) * UNIT + i * 8 + j, place] = 1.0
    return matrix


class Layout:
    def __init__(self, mesh):
        self.sec, self.lat, self.lon = (mesh.shape[k] for k in ("sec", "lat", "lon"))
        self.x = 4 if self.lon == 32 else 2
        self.z = self.lon // self.x
        self.y_hi = self.lat // 2
        self.y = self.y_hi * self.sec
        self.blocks = self.lon
        self.depth = D // self.blocks
        self.z_low = self.z // 2
        self.fine_width = 1024 // (2 * self.y)
        self.coarse_width = 4096 // (2 * self.y)


def unit_window(width, starts, ref, column):
    return jnp.concatenate([ref[pl.ds(s, width), pl.ds(column, 128)] for s in starts], 0)


def low_lanes(rows):
    return lax.broadcasted_iota(jnp.int32, (rows, 128), 1) < 64


def stack_heads(part):
    part = part.astype(F32) * 0.125
    low = low_lanes(UNIT)
    return jnp.concatenate([jnp.where(low, part, 0.0), jnp.where(low, 0.0, part)], 0).astype(BF16)


def merge_heads(both):
    return jnp.where(low_lanes(UNIT), both[:UNIT], both[UNIT:])


def attend(queries, keys, values, bias):
    scores = [dot_t(q, k) + bias for q, k in zip(queries, keys)]
    peaks = [jnp.max(s, axis=-1, keepdims=True) for s in scores]
    expos = [jnp.exp(s - m) for s, m in zip(scores, peaks)]
    totals = [jnp.sum(e, axis=-1, keepdims=True) for e in expos]
    attentions = [e * (1.0 / t) for e, t in zip(expos, totals)]
    mixed = [merge_heads(dot(a.astype(BF16), v)) for a, v in zip(attentions, values)]
    return attentions, mixed, [m + jnp.log(t) for m, t in zip(peaks, totals)]


def query_back(keys, values, attentions, slopes):
    probs = [dot_t(s, v) for s, v in zip(slopes, values)]
    means = [jnp.sum(a * p, axis=-1, keepdims=True) for a, p in zip(attentions, probs)]
    scores = [(a * (p - m)).astype(BF16) for a, p, m in zip(attentions, probs, means)]
    return [merge_heads(dot(s, k)) for s, k in zip(scores, keys)]


def pair_back(queries, slopes, statistics, keys, values, bias):
    scores = [dot_t(jnp.concatenate([q, statistics], 1), k) + bias for q, k in zip(queries, keys)]
    probs = [dot_t(jnp.concatenate([s, statistics], 1), v) for s, v in zip(slopes, values)]
    attentions = [jnp.exp(s) for s in scores]
    scores = [(a * p).astype(BF16) for a, p in zip(attentions, probs)]
    return (
        [merge_heads(t_dot(s, q)) for s, q in zip(scores, queries)],
        [merge_heads(t_dot(a.astype(BF16), s)) for a, s in zip(attentions, slopes)],
    )


def put_head_columns(total, pair, column):
    head = lax.broadcasted_iota(jnp.int32, total.shape, 1) // 8
    total = jnp.where(head == 2 * pair, column[:UNIT], total)
    return jnp.where(head == 2 * pair + 1, column[UNIT:], total)


def statistics_of(lse, slope, mixed, heads):
    product = slope.astype(F32) * mixed
    high = product.astype(BF16)
    low = (product - high.astype(F32)).astype(BF16)
    mean = dot(high, heads) + dot(low, heads)
    lane = lax.broadcasted_iota(jnp.int32, lse.shape, 1)
    part = lane % 8
    value = jnp.where(part < 3, lse * -8.0, -mean)
    first = value.astype(BF16)
    rest = value - first.astype(F32)
    second = rest.astype(BF16)
    third = rest - second.astype(F32)
    value = jnp.where(part % 3 == 0, first.astype(F32), jnp.where(part % 3 == 1, second.astype(F32), third))
    return jnp.where((part < 6) & (lane < 64), value, 0.0).astype(BF16)


def norm(field, gain):
    factor = lax.rsqrt(jnp.mean(field * field, axis=-1, keepdims=True) + EPSILON)
    normed = field * factor
    return factor, normed, (normed * gain).astype(BF16)


def input_back(slope, hidden_slope, field, gain):
    factor = lax.rsqrt(jnp.mean(field * field, axis=-1, keepdims=True) + EPSILON)
    normed = field * factor
    scaled = hidden_slope * gain
    return slope + factor * (scaled - normed * jnp.mean(scaled * normed, axis=-1, keepdims=True))


class Reducer:
    def __init__(self, lay, place, wires, pending, refs):
        self.lay, self.place, self.wires, self.pending = lay, place, wires, pending
        (
            self.given, self.in_1a, self.in_1b, self.sum_2a, self.sum_2b,
            self.in_2a, self.in_2b, self.sum_3, self.in_3, self.full,
        ) = refs
        self.copies = []

    def device(self, core=None, y=None, x=None, z=None):
        here = self.place
        core = here["core"] if core is None else core
        y = here["y"] if y is None else y
        x = here["x"] if x is None else x
        z = here["z"] if z is None else z
        return (y % self.lay.sec, y // self.lay.sec * 2 + core, x * self.lay.z + z)

    def send(self, source, target, device):
        copy = self.wires(source, target, device)
        copy.start()
        self.copies.append(copy)
        self.pending.append((copy, None))

    def arrive(self):
        for copy in self.copies:
            copy.wait_recv()
        self.copies = []

    def first_start(self):
        lay, here = self.lay, self.place
        low = pl.ds(0, lay.z_low)
        high = pl.ds(lay.z_low, lay.z - lay.z_low)
        for step in range(1, lay.x):
            x = (here["x"] + step) % lay.x
            self.send(self.given.at[:, x, low], self.in_1a.at[step - 1], self.device(x=x))
        for step in range(1, lay.y):
            y = (here["y"] + step) % lay.y
            self.send(self.given.at[y, :, high], self.in_1b.at[step - 1], self.device(y=y))

    def first_finish(self):
        self.arrive()
        lay, here = self.lay, self.place
        low = pl.ds(0, lay.z_low)
        high = pl.ds(lay.z_low, lay.z - lay.z_low)

        @pl.loop(0, lay.y)
        def _(y):
            total = self.given[y, here["x"], low].astype(F32)
            for k in range(lay.x - 1):
                total += self.in_1a[k, y].astype(F32)
            self.sum_2a[y] = total.astype(BF16)

        @pl.loop(0, lay.x)
        def _(x):
            total = self.given[here["y"], x, high].astype(F32)
            for k in range(lay.y - 1):
                total += self.in_1b[k, x].astype(F32)
            self.sum_2b[x] = total.astype(BF16)

    def second_start(self):
        lay, here = self.lay, self.place
        for step in range(1, lay.y):
            y = (here["y"] + step) % lay.y
            self.send(self.sum_2a.at[y], self.in_2a.at[step - 1], self.device(y=y))
        for step in range(1, lay.x):
            x = (here["x"] + step) % lay.x
            self.send(self.sum_2b.at[x], self.in_2b.at[step - 1], self.device(x=x))

    def second_finish(self):
        self.arrive()
        lay, here = self.lay, self.place
        total = self.sum_2a[here["y"]].astype(F32)
        for k in range(lay.y - 1):
            total += self.in_2a[k].astype(F32)
        self.sum_3[pl.ds(0, lay.z_low)] = total.astype(BF16)
        total = self.sum_2b[here["x"]].astype(F32)
        for k in range(lay.x - 1):
            total += self.in_2b[k].astype(F32)
        self.sum_3[pl.ds(lay.z_low, lay.z - lay.z_low)] = total.astype(BF16)

    def third_start(self):
        lay, here = self.lay, self.place
        for step in range(1, lay.z):
            z = (here["z"] + step) % lay.z
            self.send(self.sum_3.at[z], self.in_3.at[step - 1], self.device(z=z))

    def third_finish(self):
        self.arrive()
        lay, here = self.lay, self.place
        total = self.sum_3[here["z"]].astype(F32)
        for k in range(lay.z - 1):
            total += self.in_3[k].astype(F32)
        self.full[here["core"], here["y"]] = total.astype(BF16)

    def last_start(self):
        self.spread(self.full)

    def spread(self, ref):
        lay, here = self.lay, self.place
        own = ref.at[here["core"], here["y"]]
        for across in range(2):
            for step in range(lay.y):
                if across or step:
                    core = (here["core"] + across) % 2
                    y = (here["y"] + step) % lay.y
                    self.send(own, own, self.device(core=core, y=y))

    def last_finish(self):
        self.arrive()

    def column(self, start, width):
        size = self.full.shape[-1]
        parts = []
        while width > 0:
            group, offset = divmod(start, size)
            take = min(width, size - offset)
            parts.append(self.full[group // self.lay.y, group % self.lay.y, :, offset : offset + take])
            start, width = start + take, width - take
        return (parts[0] if len(parts) == 1 else jnp.concatenate(parts, 1)).astype(F32)

    def put(self, start, product):
        lay = self.lay
        size = self.given.shape[-1]
        done, width = 0, product.shape[1]
        while done < width:
            group, offset = divmod(start + done, size)
            take = min(width - done, size - offset)
            piece = product[:, done : done + take].astype(BF16)
            self.given[group, :, :, :, offset : offset + take] = piece.reshape(lay.x, lay.z, lay.depth, take)
            done += take

    def put_merged(self, part, product):
        lay = self.lay
        size = self.given.shape[-1]
        count = lay.blocks // 4
        shaped = product.astype(BF16).reshape(count, 4, lay.depth, D)
        for run in range(4):
            group, offset = divmod(run * D, size)
            for block in range(count):
                x, z = divmod(part * count + block, lay.z)
                self.given[group, x, z, :, offset : offset + D] = shaped[block, run]


class DeepReducer(Reducer):
    def __init__(self, lay, place, wires, pending, refs):
        self.lay, self.place, self.wires, self.pending = lay, place, wires, pending
        self.given, self.in_1, self.sum_2, self.in_2, self.parts, self.full = refs
        self.copies = []

    def first_start(self):
        lay, here = self.lay, self.place
        for step in range(1, lay.z):
            z = (here["z"] + step) % lay.z
            self.send(self.given.at[:, :, z], self.in_1.at[step - 1], self.device(z=z))

    def first_finish(self):
        self.arrive()
        lay, here = self.lay, self.place

        @pl.loop(0, lay.y)
        def _(y):
            total = self.given[y, :, here["z"]].astype(F32)
            for k in range(lay.z - 1):
                total += self.in_1[k, y].astype(F32)
            self.sum_2[y] = total.astype(BF16)

    def second_start(self):
        lay, here = self.lay, self.place
        for step in range(1, lay.x):
            x = (here["x"] + step) % lay.x
            self.send(self.sum_2.at[:, x], self.in_2.at[step - 1], self.device(x=x))

    def second_finish(self):
        self.arrive()
        here = self.place
        total = self.sum_2[:, here["x"]].astype(F32)
        for k in range(self.lay.x - 1):
            total += self.in_2[k].astype(F32)
        self.parts[here["core"], here["y"]] = total.astype(BF16)

    def last_start(self):
        self.spread(self.parts)

    def last_finish(self):
        self.arrive()

        @pl.loop(0, 2)
        def _(core):
            total = self.parts[core, 0].astype(F32)
            for y in range(1, self.lay.y):
                total += self.parts[core, y].astype(F32)
            self.full[core] = total.astype(BF16)


GROUPS = ((0, 1, 2, 3),)


def lanes_of(pair, start=0):
    return slice(start + pair * 128, start + pair * 128 + 128)


def with_columns(part, columns):
    return jnp.concatenate([stack_heads(part), columns], 1)


def gain_column(lay, lon, total, weight, start):
    rows = pl.ds(pl.multiple_of(lon * lay.depth, lay.depth), lay.depth)
    own = weight[rows, start : start + total.shape[1]].astype(F32)
    return jnp.sum(total * own, axis=1, keepdims=True)


def gain_back(lay, lon, column, gain):
    row = lax.broadcasted_iota(jnp.int32, (lay.depth, D), 0) + lon * lay.depth
    at = lax.broadcasted_iota(jnp.int32, (lay.depth, D), 1) == row
    column = column / jnp.sum(jnp.where(at, gain, 0.0), axis=1, keepdims=True)
    square = (lay.depth, lay.depth)
    same = lax.broadcasted_iota(jnp.int32, square, 0) == lax.broadcasted_iota(jnp.int32, square, 1)
    return jnp.sum(jnp.where(same, column, 0.0), axis=0, keepdims=True)


def kernel(
    lay,
    tokens_hbm, cotangent_hbm, fine_gain, coarse_gain,
    fine_attend_hbm, fine_output_hbm, merge_hbm, coarse_attend_hbm, coarse_output_hbm,
    bias_hbm, bias_back_hbm, heads_hbm, columns_hbm, merge_ref_hbm, split_hbm,
    coarse_field_hbm, token_gradient_hbm, fine_gain_out, coarse_gain_out, coarse_full, early_full, late_full,
    tokens, cotangent, coarse_field, token_gradient,
    fine_attend, fine_output, merge_weight, coarse_attend, coarse_output,
    bias_ref, bias_back_ref, heads_ref, columns_ref, merge_ref, split_ref,
    strip, field_f, wide_f, projected_f, attention_f, exact_f, lse_f, slope_wide_f, left_f, right_f, merged,
    field_c, wide_c, slope_wide_c, projected_c, mixed_slope_c, attention_c, exact_c, lse_c, statistics_c, factors_c,
    *rest,
):
    load_sem, send_sem, recv_sem = rest[26:]
    sec, lat, lon = (lax.axis_index(k) for k in ("sec", "lat", "lon"))
    core = lat % 2
    place = {"core": core, "y": lat // 2 * lay.sec + sec, "x": lon // lay.z, "z": lon % lay.z}
    used = [0]
    pending = []

    def wires(source, target, device):
        index = used[0]
        used[0] += 1
        return pltpu.make_async_remote_copy(
            src_ref=source,
            dst_ref=target,
            send_sem=send_sem.at[index],
            recv_sem=recv_sem.at[index],
            device_id=device,
            device_id_type=MESH,
        )

    def neighbour(step):
        return (sec, (lat + step[0] + lay.lat) % lay.lat, (lon + step[1] + lay.lon) % lay.lon)

    def start_rims(source, target):
        copies = []
        for step in AROUND:
            copy = wires(source(step), target(step), neighbour(step))
            if step[0]:
                last = lay.lat - 1
                sends = lat != (last if step[0] > 0 else 0)
                takes = lat != (0 if step[0] > 0 else last)
                pl.when(sends)(copy.start)
                copies.append((copy, takes))
                pending.append((copy, sends))
            else:
                copy.start()
                copies.append((copy, None))
                pending.append((copy, None))
        return copies

    def wait_rims(copies):
        for copy, takes in copies:
            if takes is None:
                copy.wait_recv()
            else:
                pl.when(takes)(copy.wait_recv)

    def start_twin(source, target):
        copy = wires(source, target, coarse_sum.device(core=1 - core))
        copy.start()
        pending.append((copy, None))
        return copy

    coarse_sum = Reducer(lay, place, wires, pending, rest[:10])
    early_sum = DeepReducer(lay, place, wires, pending, rest[10:16])
    late_sum = Reducer(lay, place, wires, pending, rest[16:26])

    barrier = pltpu.get_barrier_semaphore()
    peers = [neighbour(step) for step in AROUND]
    peers += [coarse_sum.device(x=(place["x"] + s) % lay.x) for s in range(1, lay.x)]
    peers += [coarse_sum.device(z=(place["z"] + s) % lay.z) for s in range(1, lay.z)]
    peers += [
        coarse_sum.device(core=(core + c) % 2, y=(place["y"] + s) % lay.y)
        for c in range(2)
        for s in range(lay.y)
        if c or s
    ]
    for peer in peers:
        pl.semaphore_signal(barrier, inc=1, device_id=peer, device_id_type=MESH)

    loads = {
        name: pltpu.make_async_copy(source, target, load_sem.at[i])
        for i, (name, source, target) in enumerate(
            (
                ("tokens", tokens_hbm, tokens),
                ("cotangent", cotangent_hbm, cotangent),
                ("fine_attend", fine_attend_hbm, fine_attend),
                ("bias_ref", bias_hbm, bias_ref),
                ("fine_output", fine_output_hbm, fine_output),
                ("merge_ref", merge_ref_hbm, merge_ref),
                ("merge_weight", merge_hbm, merge_weight),
                ("coarse_output", coarse_output_hbm, coarse_output),
                ("coarse_attend", coarse_attend_hbm, coarse_attend),
                ("heads_ref", heads_hbm, heads_ref),
                ("columns_ref", columns_hbm, columns_ref),
                ("bias_back_ref", bias_back_hbm, bias_back_ref),
                ("split_ref", split_hbm, split_ref),
            )
        )
    }
    for load in loads.values():
        load.start()

    field_f[...] = jnp.zeros_like(field_f)
    field_c[...] = jnp.zeros_like(field_c)
    loads["tokens"].wait()
    for row in range(12):
        strip[row, :12] = tokens[0, row].astype(F32)
    for row in range(12):
        for half in range(2):
            start = (row // 6 * 2 + half) * UNIT + row % 6 * 8
            field_f[start : start + 6] = strip[row, 6 * half : 6 * half + 6]
    for unit in range(4):
        wide_f[1 + unit // 2, 1 + unit % 2] = field_f[unit * UNIT : (unit + 1) * UNIT].astype(BF16)
    loads["cotangent"].wait()
    for row in range(6):
        field_c[row * 8 : row * 8 + 6] = cotangent[0, row].astype(F32)
    slope_wide_c[1, 1] = field_c[...].astype(BF16)
    factors_c[5, 0] = field_c[...].astype(BF16)

    pl.semaphore_wait(barrier, len(peers))

    def part(step, mine):
        index = []
        for way in step:
            if way == 0:
                index.append(pl.ds(1, 2))
            elif way > 0:
                index.append(2 if mine else 3)
            else:
                index.append(1 if mine else 0)
        return tuple(index)

    def opposite(step):
        return (-step[0], -step[1])

    def fine_rims(ref):
        return start_rims(lambda step: ref.at[part(step, True)], lambda step: ref.at[part(opposite(step), False)])

    def coarse_rims(ref):
        return start_rims(lambda step: ref.at[1, 1], lambda step: ref.at[1 - step[0], 1 - step[1]])

    rims = fine_rims(wide_f)

    def clear(row):
        for ref in (wide_f, slope_wide_f, wide_c, slope_wide_c, statistics_c):
            ref[row if row == 0 else ref.shape[0] - 1] = jnp.zeros(ref.shape[1:], ref.dtype)

    pl.when(lat == 0)(lambda: clear(0))
    pl.when(lat == lay.lat - 1)(lambda: clear(-1))

    top = jnp.where(lat == 0, NEGATIVE, 0.0)
    bottom = jnp.where(lat == lay.lat - 1, NEGATIVE, 0.0)
    lanes = lax.broadcasted_iota(jnp.int32, (1, 9 * UNIT), 1)

    def bias_at(is_first, is_last):
        above = jnp.where(is_first, top, 0.0)
        below = jnp.where(is_last, bottom, 0.0)
        rim = jnp.where(lanes < 3 * UNIT, above, 0.0) + jnp.where(lanes >= 6 * UNIT, below, 0.0)
        return bias_ref[...] + rim

    gain_f = fine_gain[...]
    gain_c = coarse_gain[...]
    loads["fine_attend"].wait()
    for run in range(2):
        hidden = norm(field_f[run * 96 : run * 96 + 96], gain_f)[2]
        left_f[0, 0, run * 96 : run * 96 + 96] = hidden
        projected_f[240 + run * 192 : 336 + run * 192, :] = dot(hidden, fine_attend[...]).astype(BF16)
    twin_hidden = start_twin(left_f.at[0, 0], left_f.at[0, 1])
    wait_rims(rims)
    slope_rims = coarse_rims(slope_wide_c)
    for start, units in (
        (0, (wide_f[0].reshape(4 * UNIT, D), wide_f[1, 0])),
        (336, (wide_f[1, 3], wide_f[2, 0])),
        (528, (wide_f[2, 3], wide_f[3].reshape(4 * UNIT, D))),
    ):
        field = jnp.concatenate([unit.astype(F32) for unit in units], 0)
        hidden = norm(field, gain_f)[2]
        projected_f[start : start + field.shape[0], :] = dot(hidden, fine_attend[...]).astype(BF16)

    loads["bias_ref"].wait()

    def starts_of(quad):
        first, second = quad // 2, quad % 2
        return [pl.multiple_of(((first + i) * 4 + second) * UNIT, UNIT) for i in range(3)]

    def middle_of(quad):
        return pl.ds(pl.multiple_of(((1 + quad // 2) * 4 + 1 + quad % 2) * UNIT, UNIT), UNIT)

    def own_of(quad):
        return pl.ds(pl.multiple_of(quad * UNIT, UNIT), UNIT)

    @pl.loop(0, 4, unroll=4)
    def _(quad):
        first = quad // 2
        own, middle, starts = own_of(quad), middle_of(quad), starts_of(quad)
        bias = bias_at(first == 0, first == 1)
        lse = jnp.zeros((UNIT, 128), F32)
        for pairs in GROUPS:
            results = attend(
                [stack_heads(projected_f[middle, lanes_of(pair)]) for pair in pairs],
                [unit_window(3 * UNIT, starts, projected_f, D + pair * 128) for pair in pairs],
                [unit_window(3 * UNIT, starts, projected_f, 2 * D + pair * 128) for pair in pairs],
                bias,
            )
            for pair, attention, mixed, column in zip(pairs, *results):
                attention_f[quad, pair] = attention
                exact_f[own, lanes_of(pair)] = mixed
                left_f[1, 0, own, lanes_of(pair)] = mixed.astype(BF16)
                lse = put_head_columns(lse, pair, column)
        lse_f[own, :] = lse

    twin_mixed = start_twin(left_f.at[1, 0], left_f.at[1, 1])
    loads["fine_output"].wait()
    loads["merge_ref"].wait()
    fine_field = (field_f[...] + dot(left_f[1, 0], fine_output[...])).astype(BF16)
    merged[0] = dot(merge_ref[...], fine_field).astype(BF16)
    loads["merge_weight"].wait()
    coarse_in = jnp.zeros((UNIT, D), F32)
    for quarter in range(4):
        rows = slice(quarter * UNIT, (quarter + 1) * UNIT)
        coarse_in += dot(merged[0, rows], merge_weight[quarter * D : (quarter + 1) * D])
    wide_c[1, 1] = coarse_in.astype(BF16)
    rims = coarse_rims(wide_c)
    twin_merged = start_twin(merged.at[0], merged.at[1])

    for name in ("coarse_output", "coarse_attend", "heads_ref", "columns_ref", "bias_back_ref", "split_ref"):
        loads[name].wait()
    field_c[...] = wide_c[1, 1].astype(F32)
    factors_c[0, 0] = norm(field_c[...], gain_c)[2]
    wait_rims(slope_rims)
    mixed_slope_c[...] = dot_t(slope_wide_c[...].reshape(9 * UNIT, D), coarse_output[...]).astype(BF16)
    wait_rims(rims)
    hidden = norm(wide_c[...].reshape(9 * UNIT, D).astype(F32), gain_c)[2]
    projected_c[...] = dot(hidden, coarse_attend[...]).astype(BF16)
    bias = bias_at(True, True)
    middle = slice(4 * UNIT, 5 * UNIT)
    lse = jnp.zeros((UNIT, 128), F32)
    for pairs in GROUPS:
        results = attend(
            [stack_heads(projected_c[middle, lanes_of(pair)]) for pair in pairs],
            [projected_c[:, lanes_of(pair, D)] for pair in pairs],
            [projected_c[:, lanes_of(pair, 2 * D)] for pair in pairs],
            bias,
        )
        for pair, attention, mixed, column in zip(pairs, *results):
            attention_c[pair] = attention
            exact_c[:, lanes_of(pair)] = mixed
            lse = put_head_columns(lse, pair, column)
    statistics_c[1, 1] = statistics_of(lse, mixed_slope_c[middle, :], exact_c[...], heads_ref[...])
    rims = coarse_rims(statistics_c)
    factors_c[4, 0] = exact_c[...].astype(BF16)
    moved = field_c[...] + dot(factors_c[4, 0], coarse_output[...])
    for row in range(6):
        coarse_field[0, row] = moved[row * 8 : row * 8 + 6].astype(BF16)
    field_store = pltpu.make_async_copy(coarse_field, coarse_field_hbm, load_sem.at[13])
    field_store.start()
    for pairs in GROUPS:
        results = query_back(
            [projected_c[:, lanes_of(pair, D)] for pair in pairs],
            [projected_c[:, lanes_of(pair, 2 * D)] for pair in pairs],
            [attention_c[pair] for pair in pairs],
            [stack_heads(mixed_slope_c[middle, lanes_of(pair)]) for pair in pairs],
        )
        for pair, query_slope in zip(pairs, results):
            factors_c[1, 0, :, lanes_of(pair)] = query_slope.astype(BF16)
    wait_rims(rims)
    statistics = statistics_c[...].reshape(9 * UNIT, 128)
    for pairs in GROUPS:
        results = pair_back(
            [projected_c[:, lanes_of(pair)] for pair in pairs],
            [mixed_slope_c[:, lanes_of(pair)] for pair in pairs],
            statistics,
            [with_columns(projected_c[middle, lanes_of(pair, D)], columns_ref[0, pair]) for pair in pairs],
            [with_columns(projected_c[middle, lanes_of(pair, 2 * D)], columns_ref[1, pair]) for pair in pairs],
            bias_back_ref[...],
        )
        for pair, key_slope, value_slope in zip(pairs, *results):
            factors_c[2, 0, :, lanes_of(pair)] = key_slope.astype(BF16)
            factors_c[3, 0, :, lanes_of(pair)] = value_slope.astype(BF16)
    hidden_slope = sum(
        dot_t(factors_c[1 + k, 0], coarse_attend[:, k * D : (k + 1) * D]) for k in range(3)
    )
    slope = factors_c[5, 0].astype(F32)
    coarse_slope = input_back(slope, hidden_slope, field_c[...], gain_c).astype(BF16)
    factors_c[6, 0] = coarse_slope
    twin_factors = start_twin(factors_c.at[:, 0], factors_c.at[:, 1])

    merged_slope = jnp.concatenate(
        [dot_t(coarse_slope, merge_weight[k * D : (k + 1) * D]).astype(BF16) for k in range(4)], 0
    )
    slope_f = dot(split_ref[...], merged_slope).astype(BF16)
    right_f[1, 0] = slope_f
    mixed_slope = dot_t(slope_f, fine_output[...]).astype(BF16)
    statistics = statistics_of(lse_f[...], mixed_slope, exact_f[...], heads_ref[...])
    for unit in range(4):
        rows = slice(unit * UNIT, (unit + 1) * UNIT)
        slope_wide_f[1 + unit // 2, 1 + unit % 2, :, :D] = mixed_slope[rows]
        slope_wide_f[1 + unit // 2, 1 + unit % 2, :, D:] = statistics[rows]
    rims = fine_rims(slope_wide_f)
    twin_slope = start_twin(right_f.at[1, 0], right_f.at[1, 1])

    @pl.loop(0, 4, unroll=4)
    def _(quad):
        own, starts = own_of(quad), starts_of(quad)
        for pairs in GROUPS:
            results = query_back(
                [unit_window(3 * UNIT, starts, projected_f, D + pair * 128) for pair in pairs],
                [unit_window(3 * UNIT, starts, projected_f, 2 * D + pair * 128) for pair in pairs],
                [attention_f[quad, pair] for pair in pairs],
                [stack_heads(slope_wide_f[1 + quad // 2, 1 + quad % 2, :, lanes_of(pair)]) for pair in pairs],
            )
            for pair, query_slope in zip(pairs, results):
                right_f[0, 0, own, lanes_of(pair)] = query_slope.astype(BF16)

    twin_query = start_twin(right_f.at[0, 0], right_f.at[0, 1])
    twin_factors.wait_recv()
    twin_merged.wait_recv()

    def both(index):
        return factors_c[index].reshape(2 * UNIT, D)

    @pl.when(core == 0)
    def _():
        for k in range(3):
            coarse_sum.put(k * D, t_dot(both(0), both(1 + k)))
        coarse_sum.put(3 * D, t_dot(both(4), both(5)))

    @pl.when(core == 1)
    def _():
        for k in range(4):
            rows = slice(k * UNIT, (k + 1) * UNIT)
            coarse_sum.put_merged(k, t_dot(merged[:, rows].reshape(2 * UNIT, D), both(6)))

    coarse_sum.first_start()
    twin_hidden.wait_recv()
    twin_mixed.wait_recv()
    twin_slope.wait_recv()
    twin_query.wait_recv()
    early_sum.put(0, t_dot(left_f[core].reshape(8 * UNIT, D), right_f[core].reshape(8 * UNIT, D)))
    wait_rims(rims)
    early_sum.first_start()

    @pl.loop(0, 4, unroll=4)
    def _(quad):
        own, middle, starts = own_of(quad), middle_of(quad), starts_of(quad)
        first, second = quad // 2, quad % 2

        def around(lanes):
            rows = [slope_wide_f[first + i, pl.ds(second, 3), :, lanes] for i in range(3)]
            return jnp.concatenate([r.reshape(3 * UNIT, 128) for r in rows], 0)

        statistics = around(slice(D, D + 128))
        for pairs in GROUPS:
            results = pair_back(
                [unit_window(3 * UNIT, starts, projected_f, pair * 128) for pair in pairs],
                [around(lanes_of(pair)) for pair in pairs],
                statistics,
                [with_columns(projected_f[middle, lanes_of(pair, D)], columns_ref[0, pair]) for pair in pairs],
                [with_columns(projected_f[middle, lanes_of(pair, 2 * D)], columns_ref[1, pair]) for pair in pairs],
                bias_back_ref[...],
            )
            for pair, key_slope, value_slope in zip(pairs, *results):
                right_f[2, 0, own, lanes_of(pair)] = key_slope.astype(BF16)
                right_f[3, 0, own, lanes_of(pair)] = value_slope.astype(BF16)

    other = 3 - core
    twin_pair = start_twin(right_f.at[other, 0], right_f.at[other, 1])
    hidden_slope = dot_t(right_f[0, 0], fine_attend[:, :D])
    hidden_slope += dot_t(right_f[2, 0], fine_attend[:, D : 2 * D])
    hidden_slope += dot_t(right_f[3, 0], fine_attend[:, 2 * D :])
    twin_pair.wait_recv()
    late_sum.put(0, t_dot(left_f[0].reshape(8 * UNIT, D), right_f[2 + core].reshape(8 * UNIT, D)))
    late_sum.first_start()
    coarse_sum.first_finish()
    coarse_sum.second_start()
    slope = input_back(right_f[1, 0].astype(F32), hidden_slope, field_f[...], gain_f)
    for row in range(12):
        for half in range(2):
            start = (row // 6 * 2 + half) * UNIT + row % 6 * 8
            strip[row, 6 * half : 6 * half + 6] = slope[start : start + 6]
    for row in range(12):
        token_gradient[0, row] = strip[row, :12].astype(BF16)
    gradient_store = pltpu.make_async_copy(token_gradient, token_gradient_hbm, load_sem.at[14])
    gradient_store.start()
    late_sum.first_finish()
    late_sum.second_start()
    coarse_sum.second_finish()
    coarse_sum.third_start()
    early_sum.first_finish()
    early_sum.second_start()
    late_sum.second_finish()
    late_sum.third_start()
    coarse_sum.third_finish()
    coarse_sum.last_start()
    early_sum.second_finish()
    early_sum.last_start()
    late_sum.third_finish()
    late_sum.last_start()
    coarse_sum.last_finish()
    coarse_full[...] = coarse_sum.full[...]
    column = gain_column(lay, lon, coarse_sum.column(0, 3 * D), coarse_attend, 0)
    coarse_gain_out[...] = gain_back(lay, lon, column, gain_c)
    early_sum.last_finish()
    early_full[...] = early_sum.full[...]
    column = gain_column(lay, lon, early_sum.column(0, D), fine_attend, 0)
    field_store.wait()
    gradient_store.wait()
    for copy, sends in pending:
        if sends is None:
            copy.wait_send()
        else:
            pl.when(sends)(copy.wait_send)
    late_sum.last_finish()
    late_full[...] = late_sum.full[...]
    column += gain_column(lay, lon, late_sum.column(0, 2 * D), fine_attend, D)
    fine_gain_out[...] = gain_back(lay, lon, column, gain_f)


def finish(lay, *refs):
    field, gradient, fine_gain, coarse_gain, coarse_full, early_full, late_full = refs[:7]
    (
        field_out, gradient_out, fine_gain_out, fine_attend, fine_output, merge,
        coarse_gain_out, coarse_attend, coarse_output,
    ) = refs[7:]
    field_out[...] = field[...]
    gradient_out[...] = gradient[...]
    fine_gain_out[...] = fine_gain[...]
    coarse_gain_out[...] = coarse_gain[...]

    def column(full, start, width):
        return Reducer(lay, None, None, None, (None,) * 9 + (full,)).column(start, width)

    for k in range(3):
        fine_attend[:, k * D : (k + 1) * D] = column(late_full, (k - 1) * D, D) if k else column(early_full, 0, D)
        coarse_attend[:, k * D : (k + 1) * D] = column(coarse_full, k * D, D)
    fine_output[...] = column(early_full, D, D)
    coarse_output[...] = column(coarse_full, 3 * D, D)
    for run in range(4):
        merge[run * lay.depth : (run + 1) * lay.depth, :] = column(coarse_full, (4 + run) * D, D)


def reducer_scratch(lay, width):
    y, x, z, low = lay.y, lay.x, lay.z, lay.z_low
    high = z - low
    end = (lay.depth, width)
    shapes = (
        (y, x, z), (x - 1, y, low), (y - 1, x, high), (y, low), (x, high),
        (y - 1, low), (x - 1, high), (z,), (z - 1,), (2, y),
    )
    return [pltpu.VMEM(shape + end, BF16) for shape in shapes]


def deep_scratch(lay, width):
    y, x, z = lay.y, lay.x, lay.z
    end = (lay.depth, width)
    shapes = ((y, x, z), (z - 1, y, x), (y, x), (x - 1, y), (2, y, y), (2, y))
    return [pltpu.VMEM(shape + end, BF16) for shape in shapes]


def per_device(
    lay,
    tokens,
    cotangent,
    fine_gain,
    fine_attend,
    fine_output,
    merge_weight,
    coarse_gain,
    coarse_attend,
    coarse_output,
):
    vmem = pl.BlockSpec(memory_space=pltpu.VMEM)
    hbm = pl.BlockSpec(memory_space=pl.ANY)
    select = merge_matrix()
    constants = (
        jnp.asarray(window_bias()),
        jnp.asarray(window_bias_back()),
        jnp.asarray(head_columns(), BF16),
        jnp.asarray(statistic_columns(), BF16),
        jnp.asarray(select, BF16),
        jnp.asarray(select.T, BF16),
    )
    per_batch = 2 * (lay.x - 1 + lay.y - 1) + lay.z - 1 + 2 * lay.y - 1
    deep_batch = lay.z - 1 + lay.x - 1 + 2 * lay.y - 1
    copies = 5 * 8 + 7 + 2 * per_batch + deep_batch
    depth = lay.depth
    fine_shape = jax.ShapeDtypeStruct((2, lay.y, depth, lay.fine_width), BF16)
    between = pl.pallas_call(
        functools.partial(kernel, lay),
        out_shape=(
            jax.ShapeDtypeStruct(cotangent.shape, BF16),
            jax.ShapeDtypeStruct(tokens.shape, BF16),
            jax.ShapeDtypeStruct((1, depth), F32),
            jax.ShapeDtypeStruct((1, depth), F32),
            jax.ShapeDtypeStruct((2, lay.y, depth, lay.coarse_width), BF16),
            fine_shape,
            fine_shape,
        ),
        in_specs=[hbm] * 2 + [vmem] * 2 + [hbm] * 11,
        out_specs=[hbm] * 2 + [vmem] * 5,
        scratch_shapes=[
            pltpu.VMEM(tokens.shape, BF16),
            pltpu.VMEM(cotangent.shape, BF16),
            pltpu.VMEM(cotangent.shape, BF16),
            pltpu.VMEM(tokens.shape, BF16),
            pltpu.VMEM((D, 3 * D), BF16),
            pltpu.VMEM((D, D), BF16),
            pltpu.VMEM((4 * D, D), BF16),
            pltpu.VMEM((D, 3 * D), BF16),
            pltpu.VMEM((D, D), BF16),
            *(pltpu.VMEM(c.shape, c.dtype) for c in constants),
            pltpu.VMEM((12, 16, D), F32),
            pltpu.VMEM((4 * UNIT, D), F32),
            pltpu.VMEM((4, 4, UNIT, D), BF16),
            pltpu.VMEM((16 * UNIT, 3 * D), BF16),
            pltpu.VMEM((4, PAIRS, 2 * UNIT, 9 * UNIT), F32),
            pltpu.VMEM((4 * UNIT, D), F32),
            pltpu.VMEM((4 * UNIT, 128), F32),
            pltpu.VMEM((4, 4, UNIT, D + 128), BF16),
            pltpu.VMEM((2, 2, 4 * UNIT, D), BF16),
            pltpu.VMEM((4, 2, 4 * UNIT, D), BF16),
            pltpu.VMEM((2, 4 * UNIT, D), BF16),
            pltpu.VMEM((UNIT, D), F32),
            pltpu.VMEM((3, 3, UNIT, D), BF16),
            pltpu.VMEM((3, 3, UNIT, D), BF16),
            pltpu.VMEM((9 * UNIT, 3 * D), BF16),
            pltpu.VMEM((9 * UNIT, D), BF16),
            pltpu.VMEM((PAIRS, 2 * UNIT, 9 * UNIT), F32),
            pltpu.VMEM((UNIT, D), F32),
            pltpu.VMEM((UNIT, 128), F32),
            pltpu.VMEM((3, 3, UNIT, 128), BF16),
            pltpu.VMEM((7, 2, UNIT, D), BF16),
            *reducer_scratch(lay, lay.coarse_width),
            *deep_scratch(lay, lay.fine_width),
            *reducer_scratch(lay, lay.fine_width),
            pltpu.SemaphoreType.DMA((15,)),
            pltpu.SemaphoreType.DMA((copies,)),
            pltpu.SemaphoreType.DMA((copies,)),
        ],
        compiler_params=pltpu.CompilerParams(
            collective_id=0, has_side_effects=True, vmem_limit_bytes=56 * 1024 * 1024
        ),
    )(
        tokens,
        cotangent,
        fine_gain.reshape(1, D),
        coarse_gain.reshape(1, D),
        fine_attend,
        fine_output,
        merge_weight,
        coarse_attend,
        coarse_output,
        *constants,
    )
    outs = pl.pallas_call(
        functools.partial(finish, lay),
        out_shape=(
            jax.ShapeDtypeStruct(cotangent.shape, BF16),
            jax.ShapeDtypeStruct(tokens.shape, BF16),
            jax.ShapeDtypeStruct((1, depth), F32),
            jax.ShapeDtypeStruct((depth, 3 * D), F32),
            jax.ShapeDtypeStruct((depth, D), F32),
            jax.ShapeDtypeStruct((4 * depth, D), F32),
            jax.ShapeDtypeStruct((1, depth), F32),
            jax.ShapeDtypeStruct((depth, 3 * D), F32),
            jax.ShapeDtypeStruct((depth, D), F32),
        ),
        in_specs=[vmem] * 7,
        out_specs=[vmem] * 9,
    )(*between)
    outs = list(outs)
    outs[2] = outs[2].reshape(depth)
    outs[6] = outs[6].reshape(depth)
    return tuple(outs)


def solution(mesh):
    return jax.shard_map(
        functools.partial(per_device, Layout(mesh)),
        mesh=mesh,
        in_specs=(
            P("sec", "lat", "lon", None),
            P("sec", "lat", "lon", None),
            P(),
            P(),
            P(),
            P(),
            P(),
            P(),
            P(),
        ),
        out_specs=(
            P("sec", "lat", "lon", None),
            P("sec", "lat", "lon", None),
            P("lon"),
            P("lon", None),
            P("lon", None),
            P("lon", None),
            P("lon"),
            P("lon", None),
            P("lon", None),
        ),
        check_vma=False,
    )
```

```python
import functools

import jax
import jax.numpy as jnp
import numpy as np
from jax import lax
from jax.experimental import pallas as pl
from jax.experimental.pallas import tpu as pltpu
from jax.sharding import PartitionSpec as P

HEADS = 8
RADIUS = 6
EPSILON = 1e-06
NEGATIVE = -1e30
UNIT = 48
D = 512
PAIRS = 4
MESH = pl.DeviceIdType.MESH
F32 = jnp.float32
BF16 = jnp.bfloat16
AROUND = ((1, 1), (1, -1), (-1, 1), (-1, -1), (0, 1), (0, -1), (1, 0), (-1, 0))


def dot(left, right):
    return jnp.dot(left, right, preferred_element_type=F32)


def dot_t(left, right):
    return lax.dot_general(left, right, (((1,), (1,)), ((), ())), preferred_element_type=F32)


def t_dot(left, right):
    return lax.dot_general(left, right, (((0,), (0,)), ((), ())), preferred_element_type=F32)


def near_window():
    query = np.arange(UNIT)
    row, col = query // 8, query % 8
    key = np.arange(9 * UNIT)
    unit, cell = key // UNIT, key % UNIT
    key_row = unit // 3 * RADIUS + cell // 8
    key_col = unit % 3 * RADIUS + cell % 8
    return (
        (key_row[None] >= row[:, None])
        & (key_row[None] <= row[:, None] + 2 * RADIUS)
        & (key_col[None] >= col[:, None])
        & (key_col[None] <= col[:, None] + 2 * RADIUS)
        & (cell % 8 < RADIUS)[None]
    )


def window_bias():
    bias = np.where(near_window(), 0.0, NEGATIVE).astype(np.float32)
    return np.concatenate([bias, bias], 0)


def window_bias_back():
    used = (np.arange(UNIT) % 8 < RADIUS)[:, None]
    bias = np.where(near_window() & used, 0.0, NEGATIVE).astype(np.float32).T
    return np.concatenate([bias, bias], 1)


def head_columns():
    matrix = np.zeros((D, 128), np.float32)
    for head in range(HEADS):
        matrix[head * 64 : head * 64 + 64, head * 8 : head * 8 + 6] = 1.0
    return matrix


def statistic_columns():
    matrix = np.zeros((2, PAIRS, 2 * UNIT, 128), np.float32)
    for which in range(2):
        for head in range(HEADS):
            pair, side = divmod(head, 2)
            start = head * 8 + 3 * which
            matrix[which, pair, side * UNIT : (side + 1) * UNIT, start : start + 3] = 0.125
    return matrix


def merge_matrix():
    matrix = np.zeros((4 * UNIT, 4 * UNIT), np.float32)
    for a in range(2):
        for b in range(2):
            for i in range(RADIUS):
                for j in range(RADIUS):
                    r, c = 2 * i + a, 2 * j + b
                    place = (r // 6 * 2 + c // 6) * UNIT + r % 6 * 8 + c % 6
                    matrix[(a * 2 + b) * UNIT + i * 8 + j, place] = 1.0
    return matrix


class Layout:
    def __init__(self, mesh):
        self.sec, self.lat, self.lon = (mesh.shape[k] for k in ("sec", "lat", "lon"))
        self.x = 4 if self.lon == 32 else 2
        self.z = self.lon // self.x
        self.y_hi = self.lat // 2
        self.y = self.y_hi * self.sec
        self.blocks = self.lon
        self.depth = D // self.blocks
        self.z_low = self.z // 2
        self.fine_width = 1024 // (2 * self.y)
        self.coarse_width = 4096 // (2 * self.y)


def unit_window(width, starts, ref, column):
    return jnp.concatenate([ref[pl.ds(s, width), pl.ds(column, 128)] for s in starts], 0)


def low_lanes(rows):
    return lax.broadcasted_iota(jnp.int32, (rows, 128), 1) < 64


def stack_heads(part):
    part = part.astype(F32) * 0.125
    low = low_lanes(UNIT)
    return jnp.concatenate([jnp.where(low, part, 0.0), jnp.where(low, 0.0, part)], 0).astype(BF16)


def merge_heads(both):
    return jnp.where(low_lanes(UNIT), both[:UNIT], both[UNIT:])


def attend(queries, keys, values, bias):
    scores = [dot_t(q, k) + bias for q, k in zip(queries, keys)]
    peaks = [jnp.max(s, axis=-1, keepdims=True) for s in scores]
    expos = [jnp.exp(s - m) for s, m in zip(scores, peaks)]
    totals = [jnp.sum(e, axis=-1, keepdims=True) for e in expos]
    attentions = [e * (1.0 / t) for e, t in zip(expos, totals)]
    mixed = [merge_heads(dot(a.astype(BF16), v)) for a, v in zip(attentions, values)]
    return attentions, mixed, [m + jnp.log(t) for m, t in zip(peaks, totals)]


def query_back(keys, values, attentions, slopes):
    probs = [dot_t(s, v) for s, v in zip(slopes, values)]
    means = [jnp.sum(a * p, axis=-1, keepdims=True) for a, p in zip(attentions, probs)]
    scores = [(a * (p - m)).astype(BF16) for a, p, m in zip(attentions, probs, means)]
    return [merge_heads(dot(s, k)) for s, k in zip(scores, keys)]


def pair_back(queries, slopes, statistics, keys, values, bias):
    scores = [dot_t(jnp.concatenate([q, statistics], 1), k) + bias for q, k in zip(queries, keys)]
    probs = [dot_t(jnp.concatenate([s, statistics], 1), v) for s, v in zip(slopes, values)]
    attentions = [jnp.exp(s) for s in scores]
    scores = [(a * p).astype(BF16) for a, p in zip(attentions, probs)]
    return (
        [merge_heads(t_dot(s, q)) for s, q in zip(scores, queries)],
        [merge_heads(t_dot(a.astype(BF16), s)) for a, s in zip(attentions, slopes)],
    )


def put_head_columns(total, pair, column):
    head = lax.broadcasted_iota(jnp.int32, total.shape, 1) // 8
    total = jnp.where(head == 2 * pair, column[:UNIT], total)
    return jnp.where(head == 2 * pair + 1, column[UNIT:], total)


def statistics_of(lse, slope, mixed, heads):
    product = slope.astype(F32) * mixed
    high = product.astype(BF16)
    low = (product - high.astype(F32)).astype(BF16)
    mean = dot(high, heads) + dot(low, heads)
    lane = lax.broadcasted_iota(jnp.int32, lse.shape, 1)
    part = lane % 8
    value = jnp.where(part < 3, lse * -8.0, -mean)
    first = value.astype(BF16)
    rest = value - first.astype(F32)
    second = rest.astype(BF16)
    third = rest - second.astype(F32)
    value = jnp.where(part % 3 == 0, first.astype(F32), jnp.where(part % 3 == 1, second.astype(F32), third))
    return jnp.where((part < 6) & (lane < 64), value, 0.0).astype(BF16)


def norm(field, gain):
    factor = lax.rsqrt(jnp.mean(field * field, axis=-1, keepdims=True) + EPSILON)
    normed = field * factor
    return factor, normed, (normed * gain).astype(BF16)


def input_back(slope, hidden_slope, field, gain):
    factor = lax.rsqrt(jnp.mean(field * field, axis=-1, keepdims=True) + EPSILON)
    normed = field * factor
    scaled = hidden_slope * gain
    return slope + factor * (scaled - normed * jnp.mean(scaled * normed, axis=-1, keepdims=True))


def far_first(size):
    return sorted(range(1, size), key=lambda step: -min(step, size - step))


class Reducer:
    def __init__(self, lay, place, wires, pending, refs):
        self.lay, self.place, self.wires, self.pending = lay, place, wires, pending
        (
            self.given, self.in_1a, self.in_1b, self.sum_2a, self.sum_2b,
            self.in_2a, self.in_2b, self.sum_3, self.in_3, self.full,
        ) = refs
        self.copies = []

    def device(self, core=None, y=None, x=None, z=None):
        here = self.place
        core = here["core"] if core is None else core
        y = here["y"] if y is None else y
        x = here["x"] if x is None else x
        z = here["z"] if z is None else z
        return (y % self.lay.sec, y // self.lay.sec * 2 + core, x * self.lay.z + z)

    def send(self, source, target, device):
        copy = self.wires(source, target, device)
        copy.start()
        self.copies.append(copy)
        self.pending.append((copy, None))

    def arrive(self):
        for copy in self.copies:
            copy.wait_recv()
        self.copies = []

    def first_start(self):
        lay, here = self.lay, self.place
        low = pl.ds(0, lay.z_low)
        high = pl.ds(lay.z_low, lay.z - lay.z_low)
        for step in far_first(lay.x):
            x = (here["x"] + step) % lay.x
            self.send(self.given.at[:, x, low], self.in_1a.at[step - 1], self.device(x=x))
        for step in far_first(lay.y):
            y = (here["y"] + step) % lay.y
            self.send(self.given.at[y, :, high], self.in_1b.at[step - 1], self.device(y=y))

    def first_finish(self):
        self.arrive()
        lay, here = self.lay, self.place
        low = pl.ds(0, lay.z_low)
        high = pl.ds(lay.z_low, lay.z - lay.z_low)

        @pl.loop(0, lay.y)
        def _(y):
            total = self.given[y, here["x"], low].astype(F32)
            for k in range(lay.x - 1):
                total += self.in_1a[k, y].astype(F32)
            self.sum_2a[y] = total.astype(BF16)

        @pl.loop(0, lay.x)
        def _(x):
            total = self.given[here["y"], x, high].astype(F32)
            for k in range(lay.y - 1):
                total += self.in_1b[k, x].astype(F32)
            self.sum_2b[x] = total.astype(BF16)

    def second_start(self):
        lay, here = self.lay, self.place
        for step in far_first(lay.y):
            y = (here["y"] + step) % lay.y
            self.send(self.sum_2a.at[y], self.in_2a.at[step - 1], self.device(y=y))
        for step in far_first(lay.x):
            x = (here["x"] + step) % lay.x
            self.send(self.sum_2b.at[x], self.in_2b.at[step - 1], self.device(x=x))

    def second_finish(self):
        self.arrive()
        lay, here = self.lay, self.place
        total = self.sum_2a[here["y"]].astype(F32)
        for k in range(lay.y - 1):
            total += self.in_2a[k].astype(F32)
        self.sum_3[pl.ds(0, lay.z_low)] = total.astype(BF16)
        total = self.sum_2b[here["x"]].astype(F32)
        for k in range(lay.x - 1):
            total += self.in_2b[k].astype(F32)
        self.sum_3[pl.ds(lay.z_low, lay.z - lay.z_low)] = total.astype(BF16)

    def third_start(self):
        lay, here = self.lay, self.place
        for step in far_first(lay.z):
            z = (here["z"] + step) % lay.z
            self.send(self.sum_3.at[z], self.in_3.at[step - 1], self.device(z=z))

    def third_finish(self):
        self.arrive()
        lay, here = self.lay, self.place
        total = self.sum_3[here["z"]].astype(F32)
        for k in range(lay.z - 1):
            total += self.in_3[k].astype(F32)
        self.full[here["core"], here["y"]] = total.astype(BF16)

    def last_start(self):
        here = self.place
        self.spread(self.full.at[here["core"], here["y"]])

    def spread(self, own):
        for step in far_first(self.lay.y):
            self.send(own, own, self.device(y=(self.place["y"] + step) % self.lay.y))

    def last_finish(self):
        self.arrive()

    def share_start(self):
        core = self.place["core"]
        half = self.full.at[core]
        self.send(half, half, self.device(core=1 - core))

    def share_finish(self):
        self.arrive()

    def column(self, start, width):
        size = self.full.shape[-1]
        parts = []
        while width > 0:
            group, offset = divmod(start, size)
            take = min(width, size - offset)
            parts.append(self.full[group // self.lay.y, group % self.lay.y, :, offset : offset + take])
            start, width = start + take, width - take
        return (parts[0] if len(parts) == 1 else jnp.concatenate(parts, 1)).astype(F32)

    def put(self, start, product):
        lay = self.lay
        size = self.given.shape[-1]
        done, width = 0, product.shape[1]
        while done < width:
            group, offset = divmod(start + done, size)
            take = min(width - done, size - offset)
            piece = product[:, done : done + take].astype(BF16)
            self.given[group, :, :, :, offset : offset + take] = piece.reshape(lay.x, lay.z, lay.depth, take)
            done += take

    def put_merged(self, part, product):
        lay = self.lay
        size = self.given.shape[-1]
        count = lay.blocks // 4
        shaped = product.astype(BF16).reshape(count, 4, lay.depth, D)
        for run in range(4):
            group, offset = divmod(run * D, size)
            for block in range(count):
                x, z = divmod(part * count + block, lay.z)
                self.given[group, x, z, :, offset : offset + D] = shaped[block, run]


class DeepReducer(Reducer):
    def __init__(self, lay, place, wires, pending, refs):
        self.lay, self.place, self.wires, self.pending = lay, place, wires, pending
        self.given, self.in_1, self.sum_2, self.in_2, self.parts, self.full = refs
        self.copies = []

    def first_start(self):
        lay, here = self.lay, self.place
        for step in far_first(lay.z):
            z = (here["z"] + step) % lay.z
            self.send(self.given.at[:, :, z], self.in_1.at[step - 1], self.device(z=z))

    def first_finish(self):
        self.arrive()
        lay, here = self.lay, self.place

        @pl.loop(0, lay.y)
        def _(y):
            total = self.given[y, :, here["z"]].astype(F32)
            for k in range(lay.z - 1):
                total += self.in_1[k, y].astype(F32)
            self.sum_2[y] = total.astype(BF16)

    def second_start(self):
        lay, here = self.lay, self.place
        for step in far_first(lay.x):
            x = (here["x"] + step) % lay.x
            self.send(self.sum_2.at[:, x], self.in_2.at[step - 1], self.device(x=x))

    def second_finish(self):
        self.arrive()
        here = self.place
        total = self.sum_2[:, here["x"]].astype(F32)
        for k in range(self.lay.x - 1):
            total += self.in_2[k].astype(F32)
        self.parts[here["y"]] = total.astype(BF16)

    def last_start(self):
        self.spread(self.parts.at[self.place["y"]])

    def last_finish(self):
        self.arrive()
        total = self.parts[0].astype(F32)
        for y in range(1, self.lay.y):
            total += self.parts[y].astype(F32)
        self.full[self.place["core"]] = total.astype(BF16)


GROUPS = ((0, 1, 2, 3),)


def lanes_of(pair, start=0):
    return slice(start + pair * 128, start + pair * 128 + 128)


def with_columns(part, columns):
    return jnp.concatenate([stack_heads(part), columns], 1)


def gain_column(lay, lon, total, weight, start):
    rows = pl.ds(pl.multiple_of(lon * lay.depth, lay.depth), lay.depth)
    own = weight[rows, start : start + total.shape[1]].astype(F32)
    return jnp.sum(total * own, axis=1, keepdims=True)


def gain_back(lay, lon, column, gain):
    row = lax.broadcasted_iota(jnp.int32, (lay.depth, D), 0) + lon * lay.depth
    at = lax.broadcasted_iota(jnp.int32, (lay.depth, D), 1) == row
    column = column / jnp.sum(jnp.where(at, gain, 0.0), axis=1, keepdims=True)
    square = (lay.depth, lay.depth)
    same = lax.broadcasted_iota(jnp.int32, square, 0) == lax.broadcasted_iota(jnp.int32, square, 1)
    return jnp.sum(jnp.where(same, column, 0.0), axis=0, keepdims=True)


def kernel(
    lay,
    tokens_hbm, cotangent_hbm, fine_gain, coarse_gain,
    fine_attend_hbm, fine_output_hbm, merge_hbm, coarse_attend_hbm, coarse_output_hbm,
    bias_hbm, bias_back_hbm, heads_hbm, columns_hbm, merge_ref_hbm, split_hbm,
    coarse_field_hbm, token_gradient_hbm, fine_gain_out, coarse_gain_out, coarse_full, early_full, late_full,
    tokens, cotangent, coarse_field, token_gradient,
    fine_attend, fine_output, merge_weight, coarse_attend, coarse_output,
    bias_ref, bias_back_ref, heads_ref, columns_ref, merge_ref, split_ref,
    strip, field_f, wide_f, projected_f, attention_f, exact_f, lse_f, slope_wide_f, left_f, right_f, merged,
    field_c, wide_c, slope_wide_c, projected_c, mixed_slope_c, attention_c, exact_c, lse_c, statistics_c, factors_c,
    *rest,
):
    load_sem, send_sem, recv_sem = rest[26:]
    sec, lat, lon = (lax.axis_index(k) for k in ("sec", "lat", "lon"))
    core = lat % 2
    place = {"core": core, "y": lat // 2 * lay.sec + sec, "x": lon // lay.z, "z": lon % lay.z}
    used = [0]
    pending = []

    def wires(source, target, device):
        index = used[0]
        used[0] += 1
        return pltpu.make_async_remote_copy(
            src_ref=source,
            dst_ref=target,
            send_sem=send_sem.at[index],
            recv_sem=recv_sem.at[index],
            device_id=device,
            device_id_type=MESH,
        )

    def neighbour(step):
        return (sec, (lat + step[0] + lay.lat) % lay.lat, (lon + step[1] + lay.lon) % lay.lon)

    def start_rims(source, target):
        copies = []
        for step in AROUND:
            copy = wires(source(step), target(step), neighbour(step))
            if step[0]:
                last = lay.lat - 1
                sends = lat != (last if step[0] > 0 else 0)
                takes = lat != (0 if step[0] > 0 else last)
                pl.when(sends)(copy.start)
                copies.append((copy, takes))
                pending.append((copy, sends))
            else:
                copy.start()
                copies.append((copy, None))
                pending.append((copy, None))
        return copies

    def wait_rims(copies):
        for copy, takes in copies:
            if takes is None:
                copy.wait_recv()
            else:
                pl.when(takes)(copy.wait_recv)

    def start_twin(source, target):
        copy = wires(source, target, coarse_sum.device(core=1 - core))
        copy.start()
        pending.append((copy, None))
        return copy

    coarse_sum = Reducer(lay, place, wires, pending, rest[:10])
    early_sum = DeepReducer(lay, place, wires, pending, rest[10:16])
    late_sum = Reducer(lay, place, wires, pending, rest[16:26])

    barrier = pltpu.get_barrier_semaphore()
    peers = [neighbour(step) for step in AROUND]
    peers += [coarse_sum.device(x=(place["x"] + s) % lay.x) for s in range(1, lay.x)]
    peers += [coarse_sum.device(z=(place["z"] + s) % lay.z) for s in range(1, lay.z)]
    peers += [coarse_sum.device(y=(place["y"] + s) % lay.y) for s in range(1, lay.y)]
    peers += [coarse_sum.device(core=1 - core)]
    for peer in peers:
        pl.semaphore_signal(barrier, inc=1, device_id=peer, device_id_type=MESH)

    loads = {
        name: pltpu.make_async_copy(source, target, load_sem.at[i])
        for i, (name, source, target) in enumerate(
            (
                ("tokens", tokens_hbm, tokens),
                ("cotangent", cotangent_hbm, cotangent),
                ("fine_attend", fine_attend_hbm, fine_attend),
                ("bias_ref", bias_hbm, bias_ref),
                ("fine_output", fine_output_hbm, fine_output),
                ("merge_ref", merge_ref_hbm, merge_ref),
                ("merge_weight", merge_hbm, merge_weight),
                ("coarse_output", coarse_output_hbm, coarse_output),
                ("coarse_attend", coarse_attend_hbm, coarse_attend),
                ("heads_ref", heads_hbm, heads_ref),
                ("columns_ref", columns_hbm, columns_ref),
                ("bias_back_ref", bias_back_hbm, bias_back_ref),
                ("split_ref", split_hbm, split_ref),
            )
        )
    }
    for load in loads.values():
        load.start()

    field_f[...] = jnp.zeros_like(field_f)
    field_c[...] = jnp.zeros_like(field_c)
    loads["tokens"].wait()
    for row in range(12):
        strip[row, :12] = tokens[0, row].astype(F32)
    for row in range(12):
        for half in range(2):
            start = (row // 6 * 2 + half) * UNIT + row % 6 * 8
            field_f[start : start + 6] = strip[row, 6 * half : 6 * half + 6]
    for unit in range(4):
        wide_f[1 + unit // 2, 1 + unit % 2] = field_f[unit * UNIT : (unit + 1) * UNIT].astype(BF16)
    loads["cotangent"].wait()
    for row in range(6):
        field_c[row * 8 : row * 8 + 6] = cotangent[0, row].astype(F32)
    slope_wide_c[1, 1] = field_c[...].astype(BF16)
    factors_c[5, 0] = field_c[...].astype(BF16)

    pl.semaphore_wait(barrier, len(peers))

    def part(step, mine):
        index = []
        for way in step:
            if way == 0:
                index.append(pl.ds(1, 2))
            elif way > 0:
                index.append(2 if mine else 3)
            else:
                index.append(1 if mine else 0)
        return tuple(index)

    def opposite(step):
        return (-step[0], -step[1])

    def fine_rims(ref):
        return start_rims(lambda step: ref.at[part(step, True)], lambda step: ref.at[part(opposite(step), False)])

    def coarse_rims(ref):
        return start_rims(lambda step: ref.at[1, 1], lambda step: ref.at[1 - step[0], 1 - step[1]])

    rims = fine_rims(wide_f)

    def clear(row):
        for ref in (wide_f, slope_wide_f, wide_c, slope_wide_c, statistics_c):
            ref[row if row == 0 else ref.shape[0] - 1] = jnp.zeros(ref.shape[1:], ref.dtype)

    pl.when(lat == 0)(lambda: clear(0))
    pl.when(lat == lay.lat - 1)(lambda: clear(-1))

    top = jnp.where(lat == 0, NEGATIVE, 0.0)
    bottom = jnp.where(lat == lay.lat - 1, NEGATIVE, 0.0)
    lanes = lax.broadcasted_iota(jnp.int32, (1, 9 * UNIT), 1)

    def bias_at(is_first, is_last):
        above = jnp.where(is_first, top, 0.0)
        below = jnp.where(is_last, bottom, 0.0)
        rim = jnp.where(lanes < 3 * UNIT, above, 0.0) + jnp.where(lanes >= 6 * UNIT, below, 0.0)
        return bias_ref[...] + rim

    gain_f = fine_gain[...]
    gain_c = coarse_gain[...]
    loads["fine_attend"].wait()
    for run in range(2):
        hidden = norm(field_f[run * 96 : run * 96 + 96], gain_f)[2]
        left_f[0, 0, run * 96 : run * 96 + 96] = hidden
        projected_f[240 + run * 192 : 336 + run * 192, :] = dot(hidden, fine_attend[...]).astype(BF16)
    twin_hidden = start_twin(left_f.at[0, 0], left_f.at[0, 1])
    wait_rims(rims)
    slope_rims = coarse_rims(slope_wide_c)
    for start, units in (
        (0, (wide_f[0].reshape(4 * UNIT, D), wide_f[1, 0])),
        (336, (wide_f[1, 3], wide_f[2, 0])),
        (528, (wide_f[2, 3], wide_f[3].reshape(4 * UNIT, D))),
    ):
        field = jnp.concatenate([unit.astype(F32) for unit in units], 0)
        hidden = norm(field, gain_f)[2]
        projected_f[start : start + field.shape[0], :] = dot(hidden, fine_attend[...]).astype(BF16)

    loads["bias_ref"].wait()

    def starts_of(quad):
        first, second = quad // 2, quad % 2
        return [pl.multiple_of(((first + i) * 4 + second) * UNIT, UNIT) for i in range(3)]

    def middle_of(quad):
        return pl.ds(pl.multiple_of(((1 + quad // 2) * 4 + 1 + quad % 2) * UNIT, UNIT), UNIT)

    def own_of(quad):
        return pl.ds(pl.multiple_of(quad * UNIT, UNIT), UNIT)

    @pl.loop(0, 4, unroll=4)
    def _(quad):
        first = quad // 2
        own, middle, starts = own_of(quad), middle_of(quad), starts_of(quad)
        bias = bias_at(first == 0, first == 1)
        lse = jnp.zeros((UNIT, 128), F32)
        for pairs in GROUPS:
            results = attend(
                [stack_heads(projected_f[middle, lanes_of(pair)]) for pair in pairs],
                [unit_window(3 * UNIT, starts, projected_f, D + pair * 128) for pair in pairs],
                [unit_window(3 * UNIT, starts, projected_f, 2 * D + pair * 128) for pair in pairs],
                bias,
            )
            for pair, attention, mixed, column in zip(pairs, *results):
                attention_f[quad, pair] = attention
                exact_f[own, lanes_of(pair)] = mixed
                left_f[1, 0, own, lanes_of(pair)] = mixed.astype(BF16)
                lse = put_head_columns(lse, pair, column)
        lse_f[own, :] = lse

    twin_mixed = start_twin(left_f.at[1, 0], left_f.at[1, 1])
    loads["fine_output"].wait()
    loads["merge_ref"].wait()
    fine_field = (field_f[...] + dot(left_f[1, 0], fine_output[...])).astype(BF16)
    merged[0] = dot(merge_ref[...], fine_field).astype(BF16)
    loads["merge_weight"].wait()
    coarse_in = jnp.zeros((UNIT, D), F32)
    for quarter in range(4):
        rows = slice(quarter * UNIT, (quarter + 1) * UNIT)
        coarse_in += dot(merged[0, rows], merge_weight[quarter * D : (quarter + 1) * D])
    wide_c[1, 1] = coarse_in.astype(BF16)
    rims = coarse_rims(wide_c)
    twin_merged = start_twin(merged.at[0], merged.at[1])

    for name in ("coarse_output", "coarse_attend", "heads_ref", "columns_ref", "bias_back_ref", "split_ref"):
        loads[name].wait()
    field_c[...] = wide_c[1, 1].astype(F32)
    factors_c[0, 0] = norm(field_c[...], gain_c)[2]
    wait_rims(slope_rims)
    mixed_slope_c[...] = dot_t(slope_wide_c[...].reshape(9 * UNIT, D), coarse_output[...]).astype(BF16)
    wait_rims(rims)
    hidden = norm(wide_c[...].reshape(9 * UNIT, D).astype(F32), gain_c)[2]
    projected_c[...] = dot(hidden, coarse_attend[...]).astype(BF16)
    bias = bias_at(True, True)
    middle = slice(4 * UNIT, 5 * UNIT)
    lse = jnp.zeros((UNIT, 128), F32)
    for pairs in GROUPS:
        results = attend(
            [stack_heads(projected_c[middle, lanes_of(pair)]) for pair in pairs],
            [projected_c[:, lanes_of(pair, D)] for pair in pairs],
            [projected_c[:, lanes_of(pair, 2 * D)] for pair in pairs],
            bias,
        )
        for pair, attention, mixed, column in zip(pairs, *results):
            attention_c[pair] = attention
            exact_c[:, lanes_of(pair)] = mixed
            lse = put_head_columns(lse, pair, column)
    statistics_c[1, 1] = statistics_of(lse, mixed_slope_c[middle, :], exact_c[...], heads_ref[...])
    rims = coarse_rims(statistics_c)
    factors_c[4, 0] = exact_c[...].astype(BF16)
    moved = field_c[...] + dot(factors_c[4, 0], coarse_output[...])
    for row in range(6):
        coarse_field[0, row] = moved[row * 8 : row * 8 + 6].astype(BF16)
    field_store = pltpu.make_async_copy(coarse_field, coarse_field_hbm, load_sem.at[13])
    field_store.start()
    for pairs in GROUPS:
        results = query_back(
            [projected_c[:, lanes_of(pair, D)] for pair in pairs],
            [projected_c[:, lanes_of(pair, 2 * D)] for pair in pairs],
            [attention_c[pair] for pair in pairs],
            [stack_heads(mixed_slope_c[middle, lanes_of(pair)]) for pair in pairs],
        )
        for pair, query_slope in zip(pairs, results):
            factors_c[1, 0, :, lanes_of(pair)] = query_slope.astype(BF16)
    wait_rims(rims)
    statistics = statistics_c[...].reshape(9 * UNIT, 128)
    for pairs in GROUPS:
        results = pair_back(
            [projected_c[:, lanes_of(pair)] for pair in pairs],
            [mixed_slope_c[:, lanes_of(pair)] for pair in pairs],
            statistics,
            [with_columns(projected_c[middle, lanes_of(pair, D)], columns_ref[0, pair]) for pair in pairs],
            [with_columns(projected_c[middle, lanes_of(pair, 2 * D)], columns_ref[1, pair]) for pair in pairs],
            bias_back_ref[...],
        )
        for pair, key_slope, value_slope in zip(pairs, *results):
            factors_c[2, 0, :, lanes_of(pair)] = key_slope.astype(BF16)
            factors_c[3, 0, :, lanes_of(pair)] = value_slope.astype(BF16)
    hidden_slope = sum(
        dot_t(factors_c[1 + k, 0], coarse_attend[:, k * D : (k + 1) * D]) for k in range(3)
    )
    slope = factors_c[5, 0].astype(F32)
    coarse_slope = input_back(slope, hidden_slope, field_c[...], gain_c).astype(BF16)
    factors_c[6, 0] = coarse_slope
    twin_factors = start_twin(factors_c.at[:, 0], factors_c.at[:, 1])

    merged_slope = jnp.concatenate(
        [dot_t(coarse_slope, merge_weight[k * D : (k + 1) * D]).astype(BF16) for k in range(4)], 0
    )
    slope_f = dot(split_ref[...], merged_slope).astype(BF16)
    right_f[1, 0] = slope_f
    mixed_slope = dot_t(slope_f, fine_output[...]).astype(BF16)
    statistics = statistics_of(lse_f[...], mixed_slope, exact_f[...], heads_ref[...])
    for unit in range(4):
        rows = slice(unit * UNIT, (unit + 1) * UNIT)
        slope_wide_f[1 + unit // 2, 1 + unit % 2, :, :D] = mixed_slope[rows]
        slope_wide_f[1 + unit // 2, 1 + unit % 2, :, D:] = statistics[rows]
    rims = fine_rims(slope_wide_f)
    twin_slope = start_twin(right_f.at[1, 0], right_f.at[1, 1])

    @pl.loop(0, 4, unroll=4)
    def _(quad):
        own, starts = own_of(quad), starts_of(quad)
        for pairs in GROUPS:
            results = query_back(
                [unit_window(3 * UNIT, starts, projected_f, D + pair * 128) for pair in pairs],
                [unit_window(3 * UNIT, starts, projected_f, 2 * D + pair * 128) for pair in pairs],
                [attention_f[quad, pair] for pair in pairs],
                [stack_heads(slope_wide_f[1 + quad // 2, 1 + quad % 2, :, lanes_of(pair)]) for pair in pairs],
            )
            for pair, query_slope in zip(pairs, results):
                right_f[0, 0, own, lanes_of(pair)] = query_slope.astype(BF16)

    twin_query = start_twin(right_f.at[0, 0], right_f.at[0, 1])
    twin_factors.wait_recv()
    twin_merged.wait_recv()

    def both(index):
        return factors_c[index].reshape(2 * UNIT, D)

    @pl.when(core == 0)
    def _():
        for k in range(3):
            coarse_sum.put(k * D, t_dot(both(0), both(1 + k)))
        coarse_sum.put(3 * D, t_dot(both(4), both(5)))

    @pl.when(core == 1)
    def _():
        for k in range(4):
            rows = slice(k * UNIT, (k + 1) * UNIT)
            coarse_sum.put_merged(k, t_dot(merged[:, rows].reshape(2 * UNIT, D), both(6)))

    coarse_sum.first_start()
    twin_hidden.wait_recv()
    twin_mixed.wait_recv()
    twin_slope.wait_recv()
    twin_query.wait_recv()
    early_sum.put(0, t_dot(left_f[core].reshape(8 * UNIT, D), right_f[core].reshape(8 * UNIT, D)))
    wait_rims(rims)
    early_sum.first_start()

    @pl.loop(0, 4, unroll=4)
    def _(quad):
        own, middle, starts = own_of(quad), middle_of(quad), starts_of(quad)
        first, second = quad // 2, quad % 2

        def around(lanes):
            rows = [slope_wide_f[first + i, pl.ds(second, 3), :, lanes] for i in range(3)]
            return jnp.concatenate([r.reshape(3 * UNIT, 128) for r in rows], 0)

        statistics = around(slice(D, D + 128))
        for pairs in GROUPS:
            results = pair_back(
                [unit_window(3 * UNIT, starts, projected_f, pair * 128) for pair in pairs],
                [around(lanes_of(pair)) for pair in pairs],
                statistics,
                [with_columns(projected_f[middle, lanes_of(pair, D)], columns_ref[0, pair]) for pair in pairs],
                [with_columns(projected_f[middle, lanes_of(pair, 2 * D)], columns_ref[1, pair]) for pair in pairs],
                bias_back_ref[...],
            )
            for pair, key_slope, value_slope in zip(pairs, *results):
                right_f[2, 0, own, lanes_of(pair)] = key_slope.astype(BF16)
                right_f[3, 0, own, lanes_of(pair)] = value_slope.astype(BF16)

    other = 3 - core
    twin_pair = start_twin(right_f.at[other, 0], right_f.at[other, 1])
    hidden_slope = dot_t(right_f[0, 0], fine_attend[:, :D])
    hidden_slope += dot_t(right_f[2, 0], fine_attend[:, D : 2 * D])
    hidden_slope += dot_t(right_f[3, 0], fine_attend[:, 2 * D :])
    twin_pair.wait_recv()
    late_sum.put(0, t_dot(left_f[0].reshape(8 * UNIT, D), right_f[2 + core].reshape(8 * UNIT, D)))
    late_sum.first_start()
    coarse_sum.first_finish()
    coarse_sum.second_start()
    slope = input_back(right_f[1, 0].astype(F32), hidden_slope, field_f[...], gain_f)
    for row in range(12):
        for half in range(2):
            start = (row // 6 * 2 + half) * UNIT + row % 6 * 8
            strip[row, 6 * half : 6 * half + 6] = slope[start : start + 6]
    for row in range(12):
        token_gradient[0, row] = strip[row, :12].astype(BF16)
    gradient_store = pltpu.make_async_copy(token_gradient, token_gradient_hbm, load_sem.at[14])
    gradient_store.start()
    late_sum.first_finish()
    late_sum.second_start()
    coarse_sum.second_finish()
    coarse_sum.third_start()
    early_sum.first_finish()
    early_sum.second_start()
    late_sum.second_finish()
    late_sum.third_start()
    coarse_sum.third_finish()
    coarse_sum.last_start()
    early_sum.second_finish()
    early_sum.last_start()
    late_sum.third_finish()
    late_sum.last_start()
    coarse_sum.last_finish()
    coarse_sum.share_start()
    early_sum.last_finish()
    early_sum.share_start()
    late_sum.last_finish()
    late_sum.share_start()
    coarse_sum.share_finish()
    coarse_full[...] = coarse_sum.full[...]
    column = gain_column(lay, lon, coarse_sum.column(0, 3 * D), coarse_attend, 0)
    coarse_gain_out[...] = gain_back(lay, lon, column, gain_c)
    early_sum.share_finish()
    early_full[...] = early_sum.full[...]
    column = gain_column(lay, lon, early_sum.column(0, D), fine_attend, 0)
    field_store.wait()
    gradient_store.wait()
    for copy, sends in pending:
        if sends is None:
            copy.wait_send()
        else:
            pl.when(sends)(copy.wait_send)
    late_sum.share_finish()
    late_full[...] = late_sum.full[...]
    column += gain_column(lay, lon, late_sum.column(0, 2 * D), fine_attend, D)
    fine_gain_out[...] = gain_back(lay, lon, column, gain_f)


def finish(lay, *refs):
    field, gradient, fine_gain, coarse_gain, coarse_full, early_full, late_full = refs[:7]
    (
        field_out, gradient_out, fine_gain_out, fine_attend, fine_output, merge,
        coarse_gain_out, coarse_attend, coarse_output,
    ) = refs[7:]
    field_out[...] = field[...]
    gradient_out[...] = gradient[...]
    fine_gain_out[...] = fine_gain[...]
    coarse_gain_out[...] = coarse_gain[...]

    def column(full, start, width):
        return Reducer(lay, None, None, None, (None,) * 9 + (full,)).column(start, width)

    for k in range(3):
        fine_attend[:, k * D : (k + 1) * D] = column(late_full, (k - 1) * D, D) if k else column(early_full, 0, D)
        coarse_attend[:, k * D : (k + 1) * D] = column(coarse_full, k * D, D)
    fine_output[...] = column(early_full, D, D)
    coarse_output[...] = column(coarse_full, 3 * D, D)
    for run in range(4):
        merge[run * lay.depth : (run + 1) * lay.depth, :] = column(coarse_full, (4 + run) * D, D)


def reducer_scratch(lay, width):
    y, x, z, low = lay.y, lay.x, lay.z, lay.z_low
    high = z - low
    end = (lay.depth, width)
    shapes = (
        (y, x, z), (x - 1, y, low), (y - 1, x, high), (y, low), (x, high),
        (y - 1, low), (x - 1, high), (z,), (z - 1,), (2, y),
    )
    return [pltpu.VMEM(shape + end, BF16) for shape in shapes]


def deep_scratch(lay, width):
    y, x, z = lay.y, lay.x, lay.z
    end = (lay.depth, width)
    shapes = ((y, x, z), (z - 1, y, x), (y, x), (x - 1, y), (y, y), (2, y))
    return [pltpu.VMEM(shape + end, BF16) for shape in shapes]


def per_device(
    lay,
    tokens,
    cotangent,
    fine_gain,
    fine_attend,
    fine_output,
    merge_weight,
    coarse_gain,
    coarse_attend,
    coarse_output,
):
    vmem = pl.BlockSpec(memory_space=pltpu.VMEM)
    hbm = pl.BlockSpec(memory_space=pl.ANY)
    select = merge_matrix()
    constants = (
        jnp.asarray(window_bias()),
        jnp.asarray(window_bias_back()),
        jnp.asarray(head_columns(), BF16),
        jnp.asarray(statistic_columns(), BF16),
        jnp.asarray(select, BF16),
        jnp.asarray(select.T, BF16),
    )
    per_batch = 2 * (lay.x - 1 + lay.y - 1) + lay.z - 1 + lay.y
    deep_batch = lay.z - 1 + lay.x - 1 + lay.y
    copies = 5 * 8 + 7 + 2 * per_batch + deep_batch
    depth = lay.depth
    fine_shape = jax.ShapeDtypeStruct((2, lay.y, depth, lay.fine_width), BF16)
    between = pl.pallas_call(
        functools.partial(kernel, lay),
        out_shape=(
            jax.ShapeDtypeStruct(cotangent.shape, BF16),
            jax.ShapeDtypeStruct(tokens.shape, BF16),
            jax.ShapeDtypeStruct((1, depth), F32),
            jax.ShapeDtypeStruct((1, depth), F32),
            jax.ShapeDtypeStruct((2, lay.y, depth, lay.coarse_width), BF16),
            fine_shape,
            fine_shape,
        ),
        in_specs=[hbm] * 2 + [vmem] * 2 + [hbm] * 11,
        out_specs=[hbm] * 2 + [vmem] * 5,
        scratch_shapes=[
            pltpu.VMEM(tokens.shape, BF16),
            pltpu.VMEM(cotangent.shape, BF16),
            pltpu.VMEM(cotangent.shape, BF16),
            pltpu.VMEM(tokens.shape, BF16),
            pltpu.VMEM((D, 3 * D), BF16),
            pltpu.VMEM((D, D), BF16),
            pltpu.VMEM((4 * D, D), BF16),
            pltpu.VMEM((D, 3 * D), BF16),
            pltpu.VMEM((D, D), BF16),
            *(pltpu.VMEM(c.shape, c.dtype) for c in constants),
            pltpu.VMEM((12, 16, D), F32),
            pltpu.VMEM((4 * UNIT, D), F32),
            pltpu.VMEM((4, 4, UNIT, D), BF16),
            pltpu.VMEM((16 * UNIT, 3 * D), BF16),
            pltpu.VMEM((4, PAIRS, 2 * UNIT, 9 * UNIT), F32),
            pltpu.VMEM((4 * UNIT, D), F32),
            pltpu.VMEM((4 * UNIT, 128), F32),
            pltpu.VMEM((4, 4, UNIT, D + 128), BF16),
            pltpu.VMEM((2, 2, 4 * UNIT, D), BF16),
            pltpu.VMEM((4, 2, 4 * UNIT, D), BF16),
            pltpu.VMEM((2, 4 * UNIT, D), BF16),
            pltpu.VMEM((UNIT, D), F32),
            pltpu.VMEM((3, 3, UNIT, D), BF16),
            pltpu.VMEM((3, 3, UNIT, D), BF16),
            pltpu.VMEM((9 * UNIT, 3 * D), BF16),
            pltpu.VMEM((9 * UNIT, D), BF16),
            pltpu.VMEM((PAIRS, 2 * UNIT, 9 * UNIT), F32),
            pltpu.VMEM((UNIT, D), F32),
            pltpu.VMEM((UNIT, 128), F32),
            pltpu.VMEM((3, 3, UNIT, 128), BF16),
            pltpu.VMEM((7, 2, UNIT, D), BF16),
            *reducer_scratch(lay, lay.coarse_width),
            *deep_scratch(lay, lay.fine_width),
            *reducer_scratch(lay, lay.fine_width),
            pltpu.SemaphoreType.DMA((15,)),
            pltpu.SemaphoreType.DMA((copies,)),
            pltpu.SemaphoreType.DMA((copies,)),
        ],
        compiler_params=pltpu.CompilerParams(
            collective_id=0, has_side_effects=True, vmem_limit_bytes=56 * 1024 * 1024
        ),
    )(
        tokens,
        cotangent,
        fine_gain.reshape(1, D),
        coarse_gain.reshape(1, D),
        fine_attend,
        fine_output,
        merge_weight,
        coarse_attend,
        coarse_output,
        *constants,
    )
    outs = pl.pallas_call(
        functools.partial(finish, lay),
        out_shape=(
            jax.ShapeDtypeStruct(cotangent.shape, BF16),
            jax.ShapeDtypeStruct(tokens.shape, BF16),
            jax.ShapeDtypeStruct((1, depth), F32),
            jax.ShapeDtypeStruct((depth, 3 * D), F32),
            jax.ShapeDtypeStruct((depth, D), F32),
            jax.ShapeDtypeStruct((4 * depth, D), F32),
            jax.ShapeDtypeStruct((1, depth), F32),
            jax.ShapeDtypeStruct((depth, 3 * D), F32),
            jax.ShapeDtypeStruct((depth, D), F32),
        ),
        in_specs=[vmem] * 7,
        out_specs=[vmem] * 9,
    )(*between)
    outs = list(outs)
    outs[2] = outs[2].reshape(depth)
    outs[6] = outs[6].reshape(depth)
    return tuple(outs)


def solution(mesh):
    return jax.shard_map(
        functools.partial(per_device, Layout(mesh)),
        mesh=mesh,
        in_specs=(
            P("sec", "lat", "lon", None),
            P("sec", "lat", "lon", None),
            P(),
            P(),
            P(),
            P(),
            P(),
            P(),
            P(),
        ),
        out_specs=(
            P("sec", "lat", "lon", None),
            P("sec", "lat", "lon", None),
            P("lon"),
            P("lon", None),
            P("lon", None),
            P("lon", None),
            P("lon"),
            P("lon", None),
            P("lon", None),
        ),
        check_vma=False,
    )
```
